32 devices in a mesh: groups: 2 (over x), utt: 16 (over z, y, core).
Axes of the slice: x: 2, y: 2, z: 4, core: 2. Of those that a mesh axis runs over, the one named last changes fastest.
Arguments:
- cache_kv: bfloat16 [512, 8, 3072], P(('groups', 'utt')), parts along dimension 0, may hold values from -160 to 160
- new_rows: bfloat16 [512, 4608], P(('groups', 'utt')), parts along dimension 0, may hold values from -6 to 6
- cross_queries: bfloat16 [512, 1536], P(('groups', 'utt')), parts along dimension 0, may hold values from -6 to 6
- enc_kv: bfloat16 [32, 256, 3072], P(('groups', 'utt')), parts along dimension 0, may hold values from -160 to 160
- lengths: int32 [32], P(('groups', 'utt')), parts along dimension 0, may hold values from 64 to 256, as said below
- parents: int32 [32, 16], P(('groups', 'utt')), parts along dimension 0, may hold values from 0 to 15
Outputs:
- mixed: bfloat16 [512, 1536], P(('groups', 'utt')), parts along dimension 0
The draws below stay inside these ranges and needn't reach their ends.
There are 2 independent parts, one for each index of `groups`. The reference program is written for one: setup_inputs(seed, part) draws one part's arguments, and reference() takes and returns one part's arrays. A program takes and returns all parts, laid end to end along the dimension named above; each array names one. Nothing has to cross between parts.
Inputs may be any that keep to these rules, and one draw needn't show every extreme that they name: `lengths`: some utterance of each part has all 256 frames.
All inputs are finite; a program needn't handle non-finite values.
Results may differ from the reference program's by a relative error of at most 0.009.
Values may be sent and summed in bfloat16 or wider, within the bound.
No kernel may reach another device: no remote copies, remote signals or barrier semaphores. Data moves between devices by JAX's collectives and lax.ppermute only.
A program may use at most 64 MiB of HBM per device.

```python
import jax
import jax.numpy as jnp
from jax import lax

BEAM = 16
HEADS = 12
HD = 128
PREV = 8
FRAMES = 256
FEAT = 1536
ULOC = 1
UTT = 16
HYP = 256
N_UTT = 16


def draw_cache_kv(key, part):
    shape = (HYP, PREV, 2 * FEAT)
    drawn = jax.random.truncated_normal(key, -8.0, 8.0, shape, jnp.float32)
    return drawn.astype(jnp.bfloat16)


def draw_enc_kv(key, part):
    shape = (UTT, FRAMES, 2 * FEAT)
    drawn = jax.random.truncated_normal(key, -8.0, 8.0, shape, jnp.float32)
    return drawn.astype(jnp.bfloat16)


def draw_lengths(key, part):
    spans = jax.random.randint(key, (UTT,), FRAMES // 4, FRAMES + 1)
    longest = jax.random.randint(jax.random.fold_in(key, 17), (), 0, UTT)
    places = lax.broadcasted_iota(jnp.int32, (UTT,), 0)
    return jnp.where(places == longest, FRAMES, spans).astype(jnp.int32)


def set_ends(values, rng, smallest, high):
    shape = values.shape
    spot = [jax.random.randint(jax.random.fold_in(rng, axis), (), 0, shape[axis]) for axis in range(len(shape))]
    values = values.at[tuple(spot)].set(smallest)
    longest = shape.index(max(shape))
    spot[longest] = (spot[longest] + 1) % shape[longest]
    return values.at[tuple(spot)].set(high)


def shard_levels(stream_key, shape, shards, low, high):
    gain = 1.0
    for axis_at, parts in shards:
        draws = jax.random.uniform(jax.random.fold_in(jax.random.fold_in(stream_key, 6), axis_at), (parts,), jnp.float32, low / len(shards), high / len(shards))
        gain = gain * jnp.repeat(jnp.exp(draws), shape[axis_at] // parts).reshape((-1,) + (1,) * (len(shape) - 1 - axis_at))
    return gain


def bell_draw(rng, shape, spread, bound, shards=(), held_as=jnp.bfloat16):
    entries = jax.random.normal(rng, shape, jnp.float32) * spread
    if len(shards) > 0:
        entries = shard_levels(rng, shape, shards, -0.22, 0.18) * entries
    return jnp.clip(entries, min=-bound, max=bound).astype(held_as)


def setup_inputs(seed: int = 0, part: int = 0) -> dict:
    splits = jax.random.split(jax.random.key(seed), 7)
    own_keys = jax.random.split(jax.random.fold_in(splits[6], part), 7)
    cache_kv = draw_cache_kv(jax.random.fold_in(jax.random.fold_in(splits[6], part), 71), part)
    new_rows = bell_draw(own_keys[1], (HYP, 3 * FEAT), 1.0, 6.0, ((0, 16),))
    cross_queries = bell_draw(own_keys[2], (HYP, FEAT), 1.0, 6.0, ((0, 16),))
    enc_kv = draw_enc_kv(jax.random.fold_in(jax.random.fold_in(splits[6], part), 71), part)
    lengths = draw_lengths(jax.random.fold_in(jax.random.fold_in(splits[6], part), 71), part)
    parents = set_ends(jax.random.randint(own_keys[5], (UTT, BEAM), 0, BEAM), jax.random.fold_in(own_keys[5], 1), 0, BEAM - 1).astype(jnp.int32)
    return {"cache_kv": cache_kv, "new_rows": new_rows, "cross_queries": cross_queries, "enc_kv": enc_kv, "lengths": lengths, "parents": parents}


def to_utterance(lm_rows):
    rest = lm_rows.shape[1:]
    grouped = lm_rows.reshape((ULOC, BEAM, N_UTT) + rest)
    order = (2, 0, 1) + tuple(range(3, 3 + len(rest)))
    return jnp.transpose(grouped, order).reshape((ULOC * BEAM * N_UTT,) + rest)


def to_grouped(utt_rows):
    width = utt_rows.shape[1]
    grouped = utt_rows.reshape(N_UTT, ULOC, BEAM, width)
    return jnp.transpose(grouped, (1, 2, 0, 3)).reshape(HYP, width)


def attend_self(query, old_keys, old_values, new_key, new_value):
    row_count = query.shape[0]
    history = old_keys.shape[1]
    scale = HD ** -0.5
    query_heads = query.astype(jnp.float32).reshape(row_count, HEADS, HD)
    key_heads = old_keys.astype(jnp.float32).reshape(row_count, history, HEADS, HD)
    value_heads = old_values.astype(jnp.float32).reshape(row_count, history, HEADS, HD)
    old_scores = jnp.einsum("rhd,rthd->rht", query_heads, key_heads) * scale
    own_score = jnp.einsum("rhd,rhd->rh", query_heads, new_key.astype(jnp.float32).reshape(row_count, HEADS, HD)) * scale
    peak = jnp.maximum(jnp.max(old_scores, axis=2), own_score)
    old_exp = jnp.exp(old_scores - peak[:, :, None])
    own_exp = jnp.exp(own_score - peak)
    total = jnp.sum(old_exp, axis=2) + own_exp
    old_weight = (old_exp / total[:, :, None]).astype(jnp.bfloat16).astype(jnp.float32)
    own_weight = (own_exp / total).astype(jnp.bfloat16).astype(jnp.float32)
    context = jnp.einsum("rht,rthd->rhd", old_weight, value_heads)
    context = context + own_weight[:, :, None] * new_value.astype(jnp.float32).reshape(row_count, HEADS, HD)
    return context.reshape(row_count, HEADS * HD).astype(jnp.bfloat16)


def attend_frames(queries, frames_kv, frame_counts):
    utterances = frame_counts.shape[0]
    frame_total = frames_kv.shape[1]
    scale = HD ** -0.5
    query_heads = queries.astype(jnp.float32).reshape(utterances, BEAM, HEADS, HD)
    key_heads = frames_kv[:, :, :FEAT].astype(jnp.float32).reshape(utterances, frame_total, HEADS, HD)
    value_heads = frames_kv[:, :, FEAT:].astype(jnp.float32).reshape(utterances, frame_total, HEADS, HD)
    scores = jnp.einsum("ubhd,ufhd->uhbf", query_heads, key_heads) * scale
    live = lax.broadcasted_iota(jnp.int32, (utterances, 1, 1, frame_total), 3) < frame_counts[:, None, None, None]
    scores = jnp.where(live, scores, -1e30)
    peak = jnp.max(scores, axis=3, keepdims=True)
    raised = jnp.where(live, jnp.exp(scores - peak), 0.0)
    weights = (raised / jnp.sum(raised, axis=3, keepdims=True)).astype(jnp.bfloat16).astype(jnp.float32)
    context = jnp.einsum("uhbf,ufhd->ubhd", weights, value_heads)
    return context.reshape(utterances * BEAM, HEADS * HD)


def reference(cache_kv, new_rows, cross_queries, enc_kv, lengths, parents):
    cache_u = to_utterance(cache_kv)
    new_u = to_utterance(new_rows)
    grouped = cache_u.reshape(UTT, BEAM, PREV, 2 * FEAT)
    reordered = jax.vmap(lambda block, picks: block[picks])(grouped, parents).reshape(HYP, PREV, 2 * FEAT)
    self_context = attend_self(new_u[:, :FEAT], reordered[:, :, :FEAT], reordered[:, :, FEAT:], new_u[:, FEAT:2 * FEAT], new_u[:, 2 * FEAT:])
    cross_context = attend_frames(cross_queries, enc_kv, lengths)
    mixed_u = (self_context.astype(jnp.float32) + cross_context).astype(jnp.bfloat16)
    return to_grouped(mixed_u)
```

```python
import functools

import jax
import jax.numpy as jnp
from jax import lax
from jax.experimental import pallas as pl
from jax.experimental.pallas import tpu as pltpu
from jax.sharding import PartitionSpec as P

HD = 128
LANES = 128
PARENT_LANE = 64
MASKED = -1e30


def reorder(cache_rows, parents):
    utterances, beam_width = parents.shape
    grouped = cache_rows.reshape(utterances, beam_width, cache_rows.shape[1], cache_rows.shape[2])
    picked = jax.vmap(lambda block, picks: block[picks])(grouped, parents)
    return picked.reshape(cache_rows.shape)


def attend_self(query, old_keys, old_values, new_key, new_value):
    row_count = query.shape[0]
    history = old_keys.shape[1]
    head_count = query.shape[1] // HD
    scale = HD ** (-0.5)
    query_heads = query.reshape(row_count, head_count, HD)
    key_heads = old_keys.reshape(row_count, history, head_count, HD)
    value_heads = old_values.reshape(row_count, history, head_count, HD)
    old_scores = (
        jnp.einsum("rhd,rthd->rht", query_heads, key_heads, preferred_element_type=jnp.float32)
        * scale
    )
    own_score = (
        jnp.einsum(
            "rhd,rhd->rh",
            query_heads,
            new_key.reshape(row_count, head_count, HD),
            preferred_element_type=jnp.float32,
        )
        * scale
    )
    peak = jnp.maximum(jnp.max(old_scores, axis=2), own_score)
    old_exp = jnp.exp(old_scores - peak[:, :, None])
    own_exp = jnp.exp(own_score - peak)
    total = jnp.sum(old_exp, axis=2) + own_exp
    old_weight = (old_exp / total[:, :, None]).astype(jnp.bfloat16)
    own_weight = (own_exp / total).astype(jnp.bfloat16)
    context = jnp.einsum(
        "rht,rthd->rhd", old_weight, value_heads, preferred_element_type=jnp.float32
    )
    context = context + own_weight.astype(jnp.float32)[:, :, None] * new_value.reshape(
        row_count, head_count, HD
    ).astype(jnp.float32)
    return context.reshape(row_count, head_count * HD).astype(jnp.bfloat16)


def attend_frames(queries, frames_kv, frame_counts):
    utterances = frame_counts.shape[0]
    beam_width = queries.shape[0] // utterances
    feature = queries.shape[1]
    head_count = feature // HD
    frame_total = frames_kv.shape[1]
    scale = HD ** (-0.5)
    query_heads = queries.reshape(utterances, beam_width, head_count, HD)
    key_heads = frames_kv[:, :, :feature].reshape(utterances, frame_total, head_count, HD)
    value_heads = frames_kv[:, :, feature:].reshape(utterances, frame_total, head_count, HD)
    scores = (
        jnp.einsum("ubhd,ufhd->uhbf", query_heads, key_heads, preferred_element_type=jnp.float32)
        * scale
    )
    live = (
        lax.broadcasted_iota(jnp.int32, (utterances, 1, 1, frame_total), 3)
        < frame_counts[:, None, None, None]
    )
    scores = jnp.where(live, scores, -1e30)
    peak = jnp.max(scores, axis=3, keepdims=True)
    raised = jnp.where(live, jnp.exp(scores - peak), 0.0)
    weights = (raised / jnp.sum(raised, axis=3, keepdims=True)).astype(jnp.bfloat16)
    context = jnp.einsum(
        "uhbf,ufhd->ubhd", weights, value_heads, preferred_element_type=jnp.float32
    )
    return context.reshape(utterances * beam_width, feature)


def body_by_utterance(cache_kv, new_rows, cross_queries, enc_kv, lengths, parents):
    feature = cross_queries.shape[1]
    cross_context = attend_frames(cross_queries, enc_kv, lengths)
    arrived, new_here = (
        lax.all_to_all(cache_kv, "utt", split_axis=0, concat_axis=0, tiled=True),
        lax.all_to_all(new_rows, "utt", split_axis=0, concat_axis=0, tiled=True),
    )
    reordered = reorder(arrived, parents)
    self_context = attend_self(
        new_here[:, :feature],
        reordered[:, :, :feature],
        reordered[:, :, feature:],
        new_here[:, feature : 2 * feature],
        new_here[:, 2 * feature :],
    )
    mixed_here = (self_context.astype(jnp.float32) + cross_context).astype(jnp.bfloat16)
    mixed = lax.all_to_all(mixed_here, "utt", split_axis=0, concat_axis=0, tiled=True)
    return mixed


def column(tile, lane_index, at):
    return jnp.sum(jnp.where(lane_index == at, tile, 0.0), axis=1, keepdims=True)


def pack_kernel(query_ref, key_ref, parents_ref, out_ref):
    rows, feature = query_ref.shape
    query = query_ref[...]
    product = query.astype(jnp.float32) * key_ref[...].astype(jnp.float32)
    lane = lax.broadcasted_iota(jnp.int32, (rows, LANES), 1)
    heads = feature // HD
    extra = jnp.zeros((rows, LANES), jnp.float32)
    for head in range(heads):
        own = jnp.sum(product[:, head * HD : (head + 1) * HD], axis=1, keepdims=True) * HD ** (-0.5)
        for part in range(3):
            term = own.astype(jnp.bfloat16).astype(jnp.float32)
            extra = jnp.where(lane == part * heads + head, term, extra)
            own = own - term
    extra = extra + parents_ref[...].astype(jnp.float32)
    out_ref[:, :feature] = query
    out_ref[:, feature:] = extra.astype(jnp.bfloat16)


def cross_kernel(lengths_ref, query_ref, frames_ref, out_ref):
    rows, feature = query_ref.shape
    frames = frames_ref.shape[0]
    live = lax.broadcasted_iota(jnp.int32, (rows, frames), 1) < lengths_ref[0]
    for head in range(feature // HD):
        at = slice(head * HD, (head + 1) * HD)
        value_at = slice(feature + head * HD, feature + (head + 1) * HD)
        scores = lax.dot_general(
            query_ref[:, at],
            frames_ref[:, at],
            (((1,), (1,)), ((), ())),
            preferred_element_type=jnp.float32,
        ) * HD ** (-0.5)
        scores = jnp.where(live, scores, MASKED)
        raised = jnp.where(live, jnp.exp(scores - jnp.max(scores, axis=1, keepdims=True)), 0.0)
        weights = (raised / jnp.sum(raised, axis=1, keepdims=True)).astype(jnp.bfloat16)
        context = jnp.dot(weights, frames_ref[:, value_at], preferred_element_type=jnp.float32)
        out_ref[:, at] = context.astype(jnp.bfloat16)


def self_kernel(masks, counts, me_ref, *refs):
    query_refs, refs = refs[:counts], refs[counts:]
    near_ref, far_ref, cross_near_ref, cross_far_ref, send_ref, keep_ref = refs
    me = me_ref[0]
    blocks = len(masks)
    keys, feature = near_ref.shape[0], near_ref.shape[1] // 2
    heads = feature // HD
    queries = jnp.concatenate([ref[...] for ref in query_refs], axis=0)
    rows = queries.shape[0]
    beams = rows // blocks
    history = keys // beams
    extra = queries[:, feature:].astype(jnp.float32)

    utt = lax.broadcasted_iota(jnp.int32, (beams, LANES), 0)
    lane = lax.broadcasted_iota(jnp.int32, (beams, LANES), 1)
    table = jnp.zeros((beams, LANES), jnp.float32)
    for at, mask in enumerate(masks):
        lists = extra[at * beams : (at + 1) * beams]
        owner = me ^ mask
        table = jnp.where(utt == owner, lists, table)
        table = jnp.where(utt == (owner ^ 1), pltpu.roll(lists, LANES - beams, 1), table)
    chosen = jnp.concatenate(
        [column(table, lane, PARENT_LANE + (me ^ mask)) for mask in masks], axis=0
    ).astype(jnp.int32)

    row_utt = lax.broadcasted_iota(jnp.int32, (rows, 1), 0) % beams
    row_mark = chosen * beams + row_utt
    key_utt = lax.broadcasted_iota(jnp.int32, (rows, keys), 1) // history
    near_live = row_mark == me * beams + key_utt
    far_live = row_mark == (me ^ 1) * beams + key_utt
    near_bias = jnp.where(near_live, 0.0, MASKED)
    far_bias = jnp.where(far_live, 0.0, MASKED)
    row_live = (chosen >> 1) == (me >> 1)

    place = lax.broadcasted_iota(jnp.int32, (rows, beams), 1)
    row_beam = me ^ jnp.concatenate(
        [jnp.full((beams, beams), mask, jnp.int32) for mask in masks], axis=0
    )
    near_pick = ((place == row_beam) & (row_utt == me)).astype(jnp.bfloat16)
    far_pick = ((place == row_beam) & (row_utt == (me ^ 1))).astype(jnp.bfloat16)

    own_all = extra + pltpu.roll(extra, LANES - heads, 1) + pltpu.roll(extra, LANES - 2 * heads, 1)
    row_lane = lax.broadcasted_iota(jnp.int32, (rows, LANES), 1)
    shares = jnp.zeros((rows, LANES), jnp.float32)
    half = rows // 2
    scale = HD ** (-0.5)
    over_last = (((1,), (1,)), ((), ()))
    for head in range(heads):
        at = slice(head * HD, (head + 1) * HD)
        value_at = slice(feature + head * HD, feature + (head + 1) * HD)
        query = queries[:, at]
        near = lax.dot_general(query, near_ref[:, at], over_last, preferred_element_type=jnp.float32)
        far = lax.dot_general(query, far_ref[:, at], over_last, preferred_element_type=jnp.float32)
        near = near * scale + near_bias
        far = far * scale + far_bias
        own = own_all[:, head : head + 1]
        peak = jnp.maximum(jnp.max(jnp.maximum(near, far), axis=1, keepdims=True), own)
        near = jnp.exp(near - peak)
        far = jnp.exp(far - peak)
        own = jnp.exp(own - peak)
        share = 1.0 / (jnp.sum(near + far, axis=1, keepdims=True) + own)
        context = jnp.dot(
            near.astype(jnp.bfloat16), near_ref[:, value_at], preferred_element_type=jnp.float32
        ) + jnp.dot(far.astype(jnp.bfloat16), far_ref[:, value_at], preferred_element_type=jnp.float32)
        cross = jnp.dot(
            near_pick, cross_near_ref[:, at], preferred_element_type=jnp.float32
        ) + jnp.dot(far_pick, cross_far_ref[:, at], preferred_element_type=jnp.float32)
        out = (context * share + cross).astype(jnp.bfloat16)
        keep_ref[:, at] = out[:half]
        send_ref[:, at] = out[half:]
        shares = jnp.where(row_lane == head, own * share, shares)
    shares = jnp.where(row_live, shares, 0.0).astype(jnp.bfloat16)
    keep_ref[:, feature:] = shares[:half]
    send_ref[:, feature:] = shares[half:]


def finish_kernel(kept_ref, came_ref, value_ref, out_ref):
    feature = out_ref.shape[1]
    shares = kept_ref[:, feature:].astype(jnp.float32) + came_ref[:, feature:].astype(jnp.float32)
    for head in range(feature // HD):
        at = slice(head * HD, (head + 1) * HD)
        context = kept_ref[:, at].astype(jnp.float32) + came_ref[:, at].astype(jnp.float32)
        out = context + shares[:, head : head + 1] * value_ref[:, at].astype(jnp.float32)
        out_ref[:, at] = out.astype(jnp.bfloat16)


def whole(shape):
    return pl.BlockSpec(shape, lambda: (0,) * len(shape))


def body_by_parent(devices, cache_kv, new_rows, cross_queries, enc_kv, lengths, parents):
    beams = parents.shape[1]
    rows, feature = cross_queries.shape
    history = cache_kv.shape[1]
    width = feature + LANES
    keys = beams * history
    me = lax.axis_index("utt").astype(jnp.int32).reshape(1)
    smem = pl.BlockSpec(memory_space=pltpu.SMEM)
    params = pltpu.CompilerParams(vmem_limit_bytes=32 * 1024 * 1024)

    def swap(array, bit):
        return lax.ppermute(array, "utt", [(i, i ^ bit) for i in range(devices)])

    hops = [1 << k for k in range(devices.bit_length() - 2, 0, -1)]

    lists = jnp.pad(parents, ((0, 0), (PARENT_LANE, LANES - PARENT_LANE - beams)))
    lists = lists + jnp.pad(
        swap(parents, 1), ((0, 0), (PARENT_LANE + beams, LANES - PARENT_LANE - 2 * beams))
    )
    near = cache_kv.reshape(keys, 2 * feature)
    far = swap(near, 1)
    own = pl.pallas_call(
        pack_kernel,
        out_shape=jax.ShapeDtypeStruct((rows, width), jnp.bfloat16),
        grid=(1,),
        in_specs=[
            pl.BlockSpec((rows, feature), lambda i: (0, 0)),
            pl.BlockSpec((rows, feature), lambda i: (0, 1)),
            pl.BlockSpec((1, LANES), lambda i: (0, 0)),
        ],
        out_specs=pl.BlockSpec((rows, width), lambda i: (0, 0)),
        compiler_params=params,
    )(new_rows, new_rows, lists)

    cross_near = pl.pallas_call(
        cross_kernel,
        out_shape=jax.ShapeDtypeStruct((rows, feature), jnp.bfloat16),
        in_specs=[smem, whole((rows, feature)), whole((enc_kv.shape[1], 2 * feature))],
        out_specs=whole((rows, feature)),
        compiler_params=params,
        cost_estimate=pl.CostEstimate(
            flops=4 * rows * enc_kv.shape[1] * feature,
            bytes_accessed=2 * enc_kv.size,
            transcendentals=rows * enc_kv.shape[1] * feature // HD,
        ),
    )(lengths, cross_queries, enc_kv.reshape(enc_kv.shape[1], 2 * feature))
    cross_far = swap(cross_near, 1)

    gathered, masks, held, held_masks = [own], [0], own, [0]
    for bit in hops:
        came = swap(held, bit)
        gathered.append(came)
        masks = masks + [mask ^ bit for mask in held_masks]
        held_masks = masks
        if bit != hops[-1]:
            held = jnp.concatenate([held, came], axis=0)

    half = rows * len(masks) // 2
    part = jax.ShapeDtypeStruct((half, width), jnp.bfloat16)
    send, keep = pl.pallas_call(
        functools.partial(self_kernel, tuple(masks), len(gathered)),
        out_shape=(part, part),
        in_specs=[smem]
        + [whole(block.shape) for block in gathered]
        + [whole((keys, 2 * feature))] * 2
        + [whole((rows, feature))] * 2,
        out_specs=(whole(part.shape), whole(part.shape)),
        compiler_params=params,
    )(me, *gathered, near, far, cross_near, cross_far)

    for bit in hops[::-1]:
        came = swap(send, bit)
        if bit != hops[0]:
            half = half // 2
            send = keep[half:] + came[half:]
            keep = keep[:half] + came[:half]

    return pl.pallas_call(
        finish_kernel,
        out_shape=jax.ShapeDtypeStruct((rows, feature), jnp.bfloat16),
        grid=(1,),
        in_specs=[
            pl.BlockSpec((rows, width), lambda i: (0, 0)),
            pl.BlockSpec((rows, width), lambda i: (0, 0)),
            pl.BlockSpec((rows, feature), lambda i: (0, 2)),
        ],
        out_specs=pl.BlockSpec((rows, feature), lambda i: (0, 0)),
        compiler_params=params,
    )(keep, came, new_rows)


def solution(mesh):
    placed = (
        P(("groups", "utt"), None, None),
        P(("groups", "utt"), None),
        P(("groups", "utt"), None),
        P(("groups", "utt"), None, None),
        P(("groups", "utt")),
        P(("groups", "utt"), None),
    )
    devices = mesh.shape["utt"]

    def body(cache_kv, new_rows, cross_queries, enc_kv, lengths, parents):
        beams = parents.shape[1]
        heads = cross_queries.shape[1] // HD
        fits = (
            parents.shape[0] == 1
            and devices == beams
            and devices >= 4
            and devices & (devices - 1) == 0
            and beams % 16 == 0
            and 3 * heads <= PARENT_LANE
            and PARENT_LANE + 2 * beams <= LANES
        )
        plan = functools.partial(body_by_parent, devices) if fits else body_by_utterance
        return plan(cache_kv, new_rows, cross_queries, enc_kv, lengths, parents)

    return jax.shard_map(
        body, mesh=mesh, in_specs=placed, out_specs=P(("groups", "utt"), None), check_vma=False
    )
```

```python
import functools

import jax
import jax.numpy as jnp
from jax import lax
from jax.experimental import pallas as pl
from jax.experimental.pallas import tpu as pltpu
from jax.sharding import PartitionSpec as P

HD = 128
LANES = 128
PARENT_LANE = 64
MASKED = -1e30


def reorder(cache_rows, parents):
    utterances, beam_width = parents.shape
    grouped = cache_rows.reshape(utterances, beam_width, cache_rows.shape[1], cache_rows.shape[2])
    picked = jax.vmap(lambda block, picks: block[picks])(grouped, parents)
    return picked.reshape(cache_rows.shape)


def attend_self(query, old_keys, old_values, new_key, new_value):
    row_count = query.shape[0]
    history = old_keys.shape[1]
    head_count = query.shape[1] // HD
    scale = HD ** (-0.5)
    query_heads = query.reshape(row_count, head_count, HD)
    key_heads = old_keys.reshape(row_count, history, head_count, HD)
    value_heads = old_values.reshape(row_count, history, head_count, HD)
    old_scores = (
        jnp.einsum("rhd,rthd->rht", query_heads, key_heads, preferred_element_type=jnp.float32)
        * scale
    )
    own_score = (
        jnp.einsum(
            "rhd,rhd->rh",
            query_heads,
            new_key.reshape(row_count, head_count, HD),
            preferred_element_type=jnp.float32,
        )
        * scale
    )
    peak = jnp.maximum(jnp.max(old_scores, axis=2), own_score)
    old_exp = jnp.exp(old_scores - peak[:, :, None])
    own_exp = jnp.exp(own_score - peak)
    total = jnp.sum(old_exp, axis=2) + own_exp
    old_weight = (old_exp / total[:, :, None]).astype(jnp.bfloat16)
    own_weight = (own_exp / total).astype(jnp.bfloat16)
    context = jnp.einsum(
        "rht,rthd->rhd", old_weight, value_heads, preferred_element_type=jnp.float32
    )
    context = context + own_weight.astype(jnp.float32)[:, :, None] * new_value.reshape(
        row_count, head_count, HD
    ).astype(jnp.float32)
    return context.reshape(row_count, head_count * HD).astype(jnp.bfloat16)


def attend_frames(queries, frames_kv, frame_counts):
    utterances = frame_counts.shape[0]
    beam_width = queries.shape[0] // utterances
    feature = queries.shape[1]
    head_count = feature // HD
    frame_total = frames_kv.shape[1]
    scale = HD ** (-0.5)
    query_heads = queries.reshape(utterances, beam_width, head_count, HD)
    key_heads = frames_kv[:, :, :feature].reshape(utterances, frame_total, head_count, HD)
    value_heads = frames_kv[:, :, feature:].reshape(utterances, frame_total, head_count, HD)
    scores = (
        jnp.einsum("ubhd,ufhd->uhbf", query_heads, key_heads, preferred_element_type=jnp.float32)
        * scale
    )
    live = (
        lax.broadcasted_iota(jnp.int32, (utterances, 1, 1, frame_total), 3)
        < frame_counts[:, None, None, None]
    )
    scores = jnp.where(live, scores, -1e30)
    peak = jnp.max(scores, axis=3, keepdims=True)
    raised = jnp.where(live, jnp.exp(scores - peak), 0.0)
    weights = (raised / jnp.sum(raised, axis=3, keepdims=True)).astype(jnp.bfloat16)
    context = jnp.einsum(
        "uhbf,ufhd->ubhd", weights, value_heads, preferred_element_type=jnp.float32
    )
    return context.reshape(utterances * beam_width, feature)


def body_by_utterance(cache_kv, new_rows, cross_queries, enc_kv, lengths, parents):
    feature = cross_queries.shape[1]
    cross_context = attend_frames(cross_queries, enc_kv, lengths)
    arrived, new_here = (
        lax.all_to_all(cache_kv, "utt", split_axis=0, concat_axis=0, tiled=True),
        lax.all_to_all(new_rows, "utt", split_axis=0, concat_axis=0, tiled=True),
    )
    reordered = reorder(arrived, parents)
    self_context = attend_self(
        new_here[:, :feature],
        reordered[:, :, :feature],
        reordered[:, :, feature:],
        new_here[:, feature : 2 * feature],
        new_here[:, 2 * feature :],
    )
    mixed_here = (self_context.astype(jnp.float32) + cross_context).astype(jnp.bfloat16)
    mixed = lax.all_to_all(mixed_here, "utt", split_axis=0, concat_axis=0, tiled=True)
    return mixed


CORE = 1
CLASS = 2
PAIR = CLASS | CORE
OVER_LAST = (((1,), (1,)), ((), ()))


def class_of(index):
    return (index // CLASS) % 2


def rank_in_class(utt):
    return utt // (2 * CLASS) * CLASS + utt % CLASS


def utt_of_rank(rank, device):
    return rank // CLASS * (2 * CLASS) + class_of(device) * CLASS + rank % CLASS


def class_order(beams, device):
    row = lax.broadcasted_iota(jnp.int32, (beams, beams), 0)
    col = lax.broadcasted_iota(jnp.int32, (beams, beams), 1)
    half = beams // 2
    place = rank_in_class(col) + jnp.where(class_of(col) == class_of(device), 0, half)
    return (row == place).astype(jnp.bfloat16)


def pack_kernel(query_ref, key_ref, parents_ref, keep_ref, send_ref):
    rows, feature = query_ref.shape
    half = rows // 2
    beams = parents_ref.shape[1]
    order = class_order(rows, lax.axis_index("utt"))
    query = query_ref[...]
    product = query.astype(jnp.float32) * key_ref[...].astype(jnp.float32)
    lane = lax.broadcasted_iota(jnp.int32, (rows, LANES), 1)
    heads = feature // HD
    at_parent_lane = lax.broadcasted_iota(jnp.int32, (beams, LANES), 0) + PARENT_LANE
    at_parent_lane = at_parent_lane == lax.broadcasted_iota(jnp.int32, (beams, LANES), 1)
    extra = jnp.dot(
        jnp.broadcast_to(parents_ref[...], (rows, beams)).astype(jnp.bfloat16),
        at_parent_lane.astype(jnp.bfloat16),
        preferred_element_type=jnp.float32,
    )
    for head in range(heads):
        own = jnp.sum(product[:, head * HD : (head + 1) * HD], axis=1, keepdims=True) * HD ** (-0.5)
        for part in range(3):
            term = own.astype(jnp.bfloat16).astype(jnp.float32)
            extra = jnp.where(lane == part * heads + head, term, extra)
            own = own - term
    extra = extra.astype(jnp.bfloat16)
    for at in range(0, feature + LANES, LANES):
        tile = query[:, at : at + LANES] if at < feature else extra
        tile = jnp.dot(order, tile, preferred_element_type=jnp.float32)
        keep_ref[:, at : at + LANES] = tile[:half].astype(jnp.bfloat16)
        send_ref[:, at : at + LANES] = tile[half:].astype(jnp.bfloat16)


def cross_weights_kernel(lengths_ref, query_ref, keys_ref, out_ref):
    rows, feature = query_ref.shape
    frames = keys_ref.shape[0]
    heads = feature // HD
    live = lax.broadcasted_iota(jnp.int32, (rows, frames), 1) < lengths_ref[...]
    scores = []
    for head in range(heads):
        at = slice(head * HD, (head + 1) * HD)
        scores.append(
            lax.dot_general(
                query_ref[:, at], keys_ref[:, at], OVER_LAST, preferred_element_type=jnp.float32
            )
        )
    for head in range(heads):
        masked = jnp.where(live, scores[head] * HD ** (-0.5), MASKED)
        raised = jnp.where(live, jnp.exp(masked - jnp.max(masked, axis=1, keepdims=True)), 0.0)
        weights = raised / jnp.sum(raised, axis=1, keepdims=True)
        out_ref[head] = weights.astype(jnp.bfloat16)


def cross_values_kernel(weights_ref, values_ref, out_ref):
    for head in range(weights_ref.shape[0]):
        at = slice(head * HD, (head + 1) * HD)
        out_ref[:, at] = jnp.dot(
            weights_ref[head], values_ref[:, at], preferred_element_type=jnp.float32
        ).astype(jnp.bfloat16)


def cached(near_ref, far_ref, pair_near_ref, pair_far_ref, mine, at):
    pieces = [ref[part, mine, :, at] for ref in (near_ref, far_ref) for part in range(near_ref.shape[0])]
    return jnp.concatenate(pieces + [pair_near_ref[:, at], pair_far_ref[:, at]], axis=0)


def rows_of(masks, beams):
    return [mask ^ pair for mask in masks for pair in (0, PAIR)]


def self_weights_kernel(masks, counts, *refs):
    query_refs, refs = refs[:counts], refs[counts:]
    *cache_refs, weight_ref, share_ref = refs
    me = lax.axis_index("utt").astype(jnp.int32)
    mine = class_of(me)
    pair_keys, feature = cache_refs[-1].shape
    heads, rows, keys = weight_ref.shape
    beams = query_refs[0].shape[0]
    half_beams = beams // 2
    history = pair_keys // half_beams
    queries = jnp.concatenate([ref[...] for ref in query_refs], axis=0)
    extra = queries[:, feature:].astype(jnp.float32)

    scores = []
    for head in range(heads):
        at = slice(head * HD, (head + 1) * HD)
        scores.append(
            lax.dot_general(
                queries[:, at],
                cached(*cache_refs, mine, at),
                OVER_LAST,
                preferred_element_type=jnp.float32,
            )
        )

    utt = utt_of_rank(lax.broadcasted_iota(jnp.int32, (half_beams, LANES), 0), me)
    lane = lax.broadcasted_iota(jnp.int32, (half_beams, LANES), 1)
    table = jnp.zeros((half_beams, LANES), jnp.float32)
    for at, mask in enumerate(masks):
        lists = extra[at * beams : at * beams + half_beams]
        owner = me ^ mask
        table = jnp.where(utt == owner, lists, table)
        table = jnp.where(utt == (owner ^ CORE), pltpu.roll(lists, LANES - beams, 1), table)
    chosen = jnp.concatenate(
        [
            jnp.sum(
                jnp.where(lane == PARENT_LANE + (me ^ mask), table, 0.0), axis=1, keepdims=True
            )
            for mask in rows_of(masks, beams)
        ],
        axis=0,
    ).astype(jnp.int32)

    row_rank = lax.broadcasted_iota(jnp.int32, (rows, keys), 0) % half_beams
    key = lax.broadcasted_iota(jnp.int32, (rows, keys), 1)
    key_rank = key % pair_keys // history
    run = key // pair_keys
    owner = me ^ jnp.where(
        run == 0, 0, jnp.where(run == 1, CORE, jnp.where(run == 2, PAIR, PAIR ^ CORE))
    )
    bias = jnp.where((key_rank == row_rank) & (chosen == owner), 0.0, MASKED)
    group = CORE | PAIR
    row_live = (chosen // (group + 1)) == (me // (group + 1))

    own_all = extra + pltpu.roll(extra, LANES - heads, 1) + pltpu.roll(extra, LANES - 2 * heads, 1)
    row_lane = lax.broadcasted_iota(jnp.int32, (rows, LANES), 1)
    shares = jnp.zeros((rows, LANES), jnp.float32)
    for head in range(heads):
        masked = scores[head] * HD ** (-0.5) + bias
        own = own_all[:, head : head + 1]
        peak = jnp.maximum(jnp.max(masked, axis=1, keepdims=True), own)
        raised = jnp.exp(masked - peak)
        own = jnp.exp(own - peak)
        share = 1.0 / (jnp.sum(raised, axis=1, keepdims=True) + own)
        weight_ref[head] = (raised * share).astype(jnp.bfloat16)
        shares = jnp.where(row_lane == head, own * share, shares)
    share_ref[...] = jnp.where(row_live, shares, 0.0).astype(jnp.bfloat16)


def self_values_kernel(masks, *refs):
    weight_ref, share_ref, *cache_refs, cross_near_ref, cross_far_ref, send_ref, keep_ref = refs
    me = lax.axis_index("utt").astype(jnp.int32)
    mine = class_of(me)
    heads, rows, _ = weight_ref.shape
    feature = heads * HD
    half = rows // 2
    beams = cross_near_ref.shape[0]
    half_beams = beams // 2
    keep_ref[:, feature:] = share_ref[:half]
    send_ref[:, feature:] = share_ref[half:]

    place = lax.broadcasted_iota(jnp.int32, (rows, beams), 1)
    pick_utt = utt_of_rank(lax.broadcasted_iota(jnp.int32, (rows, beams), 0) % half_beams, me)
    row_beam = me ^ jnp.concatenate(
        [jnp.full((half_beams, beams), mask, jnp.int32) for mask in rows_of(masks, beams)], axis=0
    )
    near_pick = ((place == row_beam) & (pick_utt == me)).astype(jnp.bfloat16)
    far_pick = ((place == row_beam) & (pick_utt == (me ^ CORE))).astype(jnp.bfloat16)
    pick = jnp.concatenate([near_pick, far_pick], axis=1)
    for head in range(heads):
        at = slice(head * HD, (head + 1) * HD)
        out = jnp.dot(
            weight_ref[head], cached(*cache_refs, mine, at), preferred_element_type=jnp.float32
        )
        cross = jnp.concatenate([cross_near_ref[:, at], cross_far_ref[:, at]], axis=0)
        out = out + jnp.dot(pick, cross, preferred_element_type=jnp.float32)
        out = out.astype(jnp.bfloat16)
        keep_ref[:, at] = out[:half]
        send_ref[:, at] = out[half:]


def finish_kernel(mine_ref, came_ref, value_ref, out_ref):
    rows, feature = out_ref.shape
    order = class_order(rows, lax.axis_index("utt"))

    def ordered(at):
        tile = jnp.concatenate(
            [mine_ref[:, at].astype(jnp.float32), came_ref[:, at].astype(jnp.float32)], axis=0
        ).astype(jnp.bfloat16)
        return lax.dot_general(
            order, tile, (((0,), (0,)), ((), ())), preferred_element_type=jnp.float32
        )

    shares = ordered(slice(feature, feature + LANES))
    for head in range(feature // HD):
        at = slice(head * HD, (head + 1) * HD)
        out = ordered(at) + shares[:, head : head + 1] * value_ref[:, at].astype(jnp.float32)
        out_ref[:, at] = out.astype(jnp.bfloat16)


def whole(shape):
    return pl.BlockSpec(shape, lambda *_: (0,) * len(shape))


def body_by_parent(devices, cache_kv, new_rows, cross_queries, enc_kv, lengths, parents):
    beams = parents.shape[1]
    rows, feature = cross_queries.shape
    frames = enc_kv.shape[1]
    history = cache_kv.shape[1]
    heads = feature // HD
    width = feature + LANES
    keys = beams * history
    me = lax.axis_index("utt").astype(jnp.int32)
    params = pltpu.CompilerParams(vmem_limit_bytes=16 * 1024 * 1024)

    def swap(array, bits):
        return lax.ppermute(array, "utt", [(i, i ^ bits) for i in range(devices)])

    def after(array, *others):
        return lax.optimization_barrier((array,) + others)[0]

    hops = [(1 << k) | CORE for k in range(devices.bit_length() - 2, 1, -1)]

    half_rows = jax.ShapeDtypeStruct((rows // 2, width), jnp.bfloat16)
    own, other = pl.pallas_call(
        pack_kernel,
        out_shape=(half_rows, half_rows),
        grid=(1,),
        in_specs=[
            pl.BlockSpec((rows, feature), lambda i: (0, 0)),
            pl.BlockSpec((rows, feature), lambda i: (0, 1)),
            whole(parents.shape),
        ],
        out_specs=(whole(half_rows.shape), whole(half_rows.shape)),
        compiler_params=params,
    )(new_rows, new_rows, parents)
    pair_rows = swap(other, PAIR)

    near = cache_kv.reshape(beams // (2 * CLASS), 2, CLASS * history, 2 * feature)
    far = swap(near, CORE)
    other_class = lax.dynamic_index_in_dim(near, 1 - class_of(me), 1, keepdims=False)
    pair_keys = swap(other_class[..., :feature], PAIR).reshape(keys // 2, feature)
    pair_values = swap(after(other_class[..., feature:], pair_rows), PAIR)
    pair_values = pair_values.reshape(keys // 2, feature)

    lists = jnp.pad(
        swap(parents, CORE).astype(jnp.bfloat16),
        ((0, 0), (feature + PARENT_LANE + beams, LANES - PARENT_LANE - 2 * beams)),
    )
    held = jnp.concatenate([own + lists, pair_rows], axis=0)
    gathered, masks, held_masks = [held], [0], [0]
    for bits in hops:
        came = swap(held, bits)
        gathered.append(came)
        masks = masks + [mask ^ bits for mask in held_masks]
        held_masks = masks
        if bits != hops[-1]:
            held = jnp.concatenate([held, came], axis=0)

    weights = pl.pallas_call(
        cross_weights_kernel,
        out_shape=jax.ShapeDtypeStruct((heads, rows, frames), jnp.bfloat16),
        grid=(1,),
        in_specs=[
            whole((1, 1)),
            whole((rows, feature)),
            pl.BlockSpec((frames, feature), lambda i: (0, 0)),
        ],
        out_specs=whole((heads, rows, frames)),
        compiler_params=params,
    )(lengths.reshape(1, 1), cross_queries, enc_kv.reshape(frames, 2 * feature))
    cross_near = pl.pallas_call(
        cross_values_kernel,
        out_shape=jax.ShapeDtypeStruct((rows, feature), jnp.bfloat16),
        grid=(1,),
        in_specs=[
            whole((heads, rows, frames)),
            pl.BlockSpec((frames, feature), lambda i: (0, 1)),
        ],
        out_specs=whole((rows, feature)),
        compiler_params=params,
    )(weights, enc_kv.reshape(frames, 2 * feature))
    cross_far = swap(cross_near, CORE)

    pair_far_keys = swap(after(pair_keys, held), CORE)
    pair_far_values = swap(after(pair_values, gathered[-1]), CORE)

    all_rows = rows * len(masks)
    half = all_rows // 2
    weight_shape = jax.ShapeDtypeStruct((heads, all_rows, 2 * keys), jnp.bfloat16)
    share_shape = jax.ShapeDtypeStruct((all_rows, LANES), jnp.bfloat16)
    part = jax.ShapeDtypeStruct((half, width), jnp.bfloat16)
    near_shape = near.shape[:3] + (feature,)
    in_keys = pl.BlockSpec(near_shape, lambda i: (0, 0, 0, 0))
    in_values = pl.BlockSpec(near_shape, lambda i: (0, 0, 0, 1))
    pair_spec = whole(pair_keys.shape)
    weights, shares = pl.pallas_call(
        functools.partial(self_weights_kernel, tuple(masks), len(gathered)),
        out_shape=(weight_shape, share_shape),
        grid=(1,),
        in_specs=[whole(block.shape) for block in gathered]
        + [in_keys, in_keys, pair_spec, pair_spec],
        out_specs=(whole(weight_shape.shape), whole(share_shape.shape)),
        compiler_params=params,
    )(*gathered, near, far, pair_keys, pair_far_keys)
    send, keep = pl.pallas_call(
        functools.partial(self_values_kernel, tuple(masks)),
        out_shape=(part, part),
        grid=(1,),
        in_specs=[whole(weights.shape), whole(shares.shape)]
        + [in_values, in_values, pair_spec, pair_spec]
        + [whole((rows, feature))] * 2,
        out_specs=(whole(part.shape), whole(part.shape)),
        compiler_params=params,
    )(weights, shares, near, far, pair_values, pair_far_values, cross_near, cross_far)

    for bits in hops[::-1]:
        came = swap(send, bits)
        half = half // 2
        send = keep[half:] + came[half:]
        keep = keep[:half] + came[:half]
    came = swap(send, PAIR)

    return pl.pallas_call(
        finish_kernel,
        out_shape=jax.ShapeDtypeStruct((rows, feature), jnp.bfloat16),
        grid=(1,),
        in_specs=[
            whole(half_rows.shape),
            whole(half_rows.shape),
            pl.BlockSpec((rows, feature), lambda i: (0, 2)),
        ],
        out_specs=whole((rows, feature)),
        compiler_params=params,
    )(keep, came, new_rows)


def solution(mesh):
    placed = (
        P(("groups", "utt"), None, None),
        P(("groups", "utt"), None),
        P(("groups", "utt"), None),
        P(("groups", "utt"), None, None),
        P(("groups", "utt")),
        P(("groups", "utt"), None),
    )
    devices = mesh.shape["utt"]

    def body(cache_kv, new_rows, cross_queries, enc_kv, lengths, parents):
        beams = parents.shape[1]
        heads = cross_queries.shape[1] // HD
        fits = (
            parents.shape[0] == 1
            and devices == beams
            and devices >= 8
            and devices & (devices - 1) == 0
            and beams % 16 == 0
            and 3 * heads <= PARENT_LANE
            and PARENT_LANE + 2 * beams <= LANES
        )
        plan = functools.partial(body_by_parent, devices) if fits else body_by_utterance
        return plan(cache_kv, new_rows, cross_queries, enc_kv, lengths, parents)

    return jax.shard_map(
        body, mesh=mesh, in_specs=placed, out_specs=P(("groups", "utt"), None), check_vma=False
    )
```

```python
import functools

import jax
import jax.numpy as jnp
from jax import lax
from jax.experimental import pallas as pl
from jax.experimental.pallas import tpu as pltpu
from jax.sharding import PartitionSpec as P

HD = 128
LANES = 128
PARENT_LANE = 64
MASKED = -1e30


def reorder(cache_rows, parents):
    utterances, beam_width = parents.shape
    grouped = cache_rows.reshape(utterances, beam_width, cache_rows.shape[1], cache_rows.shape[2])
    picked = jax.vmap(lambda block, picks: block[picks])(grouped, parents)
    return picked.reshape(cache_rows.shape)


def attend_self(query, old_keys, old_values, new_key, new_value):
    row_count = query.shape[0]
    history = old_keys.shape[1]
    head_count = query.shape[1] // HD
    scale = HD ** (-0.5)
    query_heads = query.reshape(row_count, head_count, HD)
    key_heads = old_keys.reshape(row_count, history, head_count, HD)
    value_heads = old_values.reshape(row_count, history, head_count, HD)
    old_scores = (
        jnp.einsum("rhd,rthd->rht", query_heads, key_heads, preferred_element_type=jnp.float32)
        * scale
    )
    own_score = (
        jnp.einsum(
            "rhd,rhd->rh",
            query_heads,
            new_key.reshape(row_count, head_count, HD),
            preferred_element_type=jnp.float32,
        )
        * scale
    )
    peak = jnp.maximum(jnp.max(old_scores, axis=2), own_score)
    old_exp = jnp.exp(old_scores - peak[:, :, None])
    own_exp = jnp.exp(own_score - peak)
    total = jnp.sum(old_exp, axis=2) + own_exp
    old_weight = (old_exp / total[:, :, None]).astype(jnp.bfloat16)
    own_weight = (own_exp / total).astype(jnp.bfloat16)
    context = jnp.einsum(
        "rht,rthd->rhd", old_weight, value_heads, preferred_element_type=jnp.float32
    )
    context = context + own_weight.astype(jnp.float32)[:, :, None] * new_value.reshape(
        row_count, head_count, HD
    ).astype(jnp.float32)
    return context.reshape(row_count, head_count * HD).astype(jnp.bfloat16)


def attend_frames(queries, frames_kv, frame_counts):
    utterances = frame_counts.shape[0]
    beam_width = queries.shape[0] // utterances
    feature = queries.shape[1]
    head_count = feature // HD
    frame_total = frames_kv.shape[1]
    scale = HD ** (-0.5)
    query_heads = queries.reshape(utterances, beam_width, head_count, HD)
    key_heads = frames_kv[:, :, :feature].reshape(utterances, frame_total, head_count, HD)
    value_heads = frames_kv[:, :, feature:].reshape(utterances, frame_total, head_count, HD)
    scores = (
        jnp.einsum("ubhd,ufhd->uhbf", query_heads, key_heads, preferred_element_type=jnp.float32)
        * scale
    )
    live = (
        lax.broadcasted_iota(jnp.int32, (utterances, 1, 1, frame_total), 3)
        < frame_counts[:, None, None, None]
    )
    scores = jnp.where(live, scores, -1e30)
    peak = jnp.max(scores, axis=3, keepdims=True)
    raised = jnp.where(live, jnp.exp(scores - peak), 0.0)
    weights = (raised / jnp.sum(raised, axis=3, keepdims=True)).astype(jnp.bfloat16)
    context = jnp.einsum(
        "uhbf,ufhd->ubhd", weights, value_heads, preferred_element_type=jnp.float32
    )
    return context.reshape(utterances * beam_width, feature)


def body_by_utterance(cache_kv, new_rows, cross_queries, enc_kv, lengths, parents):
    feature = cross_queries.shape[1]
    cross_context = attend_frames(cross_queries, enc_kv, lengths)
    arrived, new_here = (
        lax.all_to_all(cache_kv, "utt", split_axis=0, concat_axis=0, tiled=True),
        lax.all_to_all(new_rows, "utt", split_axis=0, concat_axis=0, tiled=True),
    )
    reordered = reorder(arrived, parents)
    self_context = attend_self(
        new_here[:, :feature],
        reordered[:, :, :feature],
        reordered[:, :, feature:],
        new_here[:, feature : 2 * feature],
        new_here[:, 2 * feature :],
    )
    mixed_here = (self_context.astype(jnp.float32) + cross_context).astype(jnp.bfloat16)
    mixed = lax.all_to_all(mixed_here, "utt", split_axis=0, concat_axis=0, tiled=True)
    return mixed


CORE = 1
CLASS = 2
PAIR = CLASS | CORE
OVER_LAST = (((1,), (1,)), ((), ()))


def class_of(index):
    return (index // CLASS) % 2


def rank_in_class(utt):
    return utt // (2 * CLASS) * CLASS + utt % CLASS


def utt_of_rank(rank, device):
    return rank // CLASS * (2 * CLASS) + class_of(device) * CLASS + rank % CLASS


def class_order(beams, device):
    row = lax.broadcasted_iota(jnp.int32, (beams, beams), 0)
    col = lax.broadcasted_iota(jnp.int32, (beams, beams), 1)
    half = beams // 2
    place = rank_in_class(col) + jnp.where(class_of(col) == class_of(device), 0, half)
    return (row == place).astype(jnp.bfloat16)


def pack_kernel(
    new_ref, parents_hbm_ref, cache_ref, keep_ref, send_ref, other_ref, query_ref, key_ref, parents_ref, sems
):
    rows, feature = query_ref.shape
    other = 1 - class_of(lax.axis_index("utt").astype(jnp.int32))
    slicing = pltpu.make_async_copy(cache_ref.at[:, other], other_ref, sems.at[3])
    copies = [
        pltpu.make_async_copy(new_ref.at[:, :feature], query_ref, sems.at[0]),
        pltpu.make_async_copy(new_ref.at[:, feature : 2 * feature], key_ref, sems.at[1]),
        pltpu.make_async_copy(parents_hbm_ref, parents_ref, sems.at[2]),
    ]
    for copy in copies:
        copy.start()
    slicing.start()
    half = rows // 2
    beams = parents_ref.shape[1]
    order = class_order(rows, lax.axis_index("utt"))
    for copy in copies:
        copy.wait()
    query = query_ref[...]
    product = query.astype(jnp.float32) * key_ref[...].astype(jnp.float32)
    lane = lax.broadcasted_iota(jnp.int32, (rows, LANES), 1)
    heads = feature // HD
    at_parent_lane = lax.broadcasted_iota(jnp.int32, (beams, LANES), 0) + PARENT_LANE
    at_parent_lane = at_parent_lane == lax.broadcasted_iota(jnp.int32, (beams, LANES), 1)
    extra = jnp.dot(
        jnp.broadcast_to(parents_ref[...], (rows, beams)).astype(jnp.bfloat16),
        at_parent_lane.astype(jnp.bfloat16),
        preferred_element_type=jnp.float32,
    )
    for head in range(heads):
        own = jnp.sum(product[:, head * HD : (head + 1) * HD], axis=1, keepdims=True) * HD ** (-0.5)
        for part in range(3):
            term = own.astype(jnp.bfloat16).astype(jnp.float32)
            extra = jnp.where(lane == part * heads + head, term, extra)
            own = own - term
    extra = extra.astype(jnp.bfloat16)
    for at in range(0, feature + LANES, LANES):
        tile = query[:, at : at + LANES] if at < feature else extra
        tile = jnp.dot(order, tile, preferred_element_type=jnp.float32)
        keep_ref[:, at : at + LANES] = tile[:half].astype(jnp.bfloat16)
        send_ref[:, at : at + LANES] = tile[half:].astype(jnp.bfloat16)
    slicing.wait()


def cross_weights_kernel(lengths_ref, query_ref, frames_ref, out_ref, keys_ref, sem):
    rows, feature = query_ref.shape
    copy = pltpu.make_async_copy(frames_ref.at[:, :feature], keys_ref, sem)
    copy.start()
    copy.wait()
    frames = keys_ref.shape[0]
    heads = feature // HD
    live = lax.broadcasted_iota(jnp.int32, (rows, frames), 1) < lengths_ref[...]
    scores = []
    for head in range(heads):
        at = slice(head * HD, (head + 1) * HD)
        scores.append(
            lax.dot_general(
                query_ref[:, at], keys_ref[:, at], OVER_LAST, preferred_element_type=jnp.float32
            )
        )
    for head in range(heads):
        masked = jnp.where(live, scores[head] * HD ** (-0.5), MASKED)
        raised = jnp.where(live, jnp.exp(masked - jnp.max(masked, axis=1, keepdims=True)), 0.0)
        weights = raised / jnp.sum(raised, axis=1, keepdims=True)
        out_ref[head] = weights.astype(jnp.bfloat16)


def cross_values_kernel(weights_ref, frames_ref, out_ref, values_ref, sem):
    feature = values_ref.shape[1]
    copy = pltpu.make_async_copy(frames_ref.at[:, feature:], values_ref, sem)
    copy.start()
    copy.wait()
    for head in range(weights_ref.shape[0]):
        at = slice(head * HD, (head + 1) * HD)
        out_ref[:, at] = jnp.dot(
            weights_ref[head], values_ref[:, at], preferred_element_type=jnp.float32
        ).astype(jnp.bfloat16)


def cached(near_ref, far_ref, pair_near_ref, pair_far_ref, mine, at):
    pieces = [ref[part, mine, :, at] for ref in (near_ref, far_ref) for part in range(near_ref.shape[0])]
    return jnp.concatenate(pieces + [pair_near_ref[:, at], pair_far_ref[:, at]], axis=0)


def rows_of(masks, beams):
    return [mask ^ pair for mask in masks for pair in (0, PAIR)]


def self_weights_kernel(masks, counts, *refs):
    query_refs, refs = refs[:counts], refs[counts:]
    *cache_refs, weight_ref, share_ref, terms_ref, spread_ref = refs
    me = lax.axis_index("utt").astype(jnp.int32)
    mine = class_of(me)
    pair_keys, feature = cache_refs[-1].shape
    heads, rows, keys = weight_ref.shape
    beams = query_refs[0].shape[0]
    half_beams = beams // 2
    history = pair_keys // half_beams
    queries = jnp.concatenate([ref[...] for ref in query_refs], axis=0)
    extra = queries[:, feature:].astype(jnp.float32)

    utt = utt_of_rank(lax.broadcasted_iota(jnp.int32, (half_beams, LANES), 0), me)
    lane = lax.broadcasted_iota(jnp.int32, (half_beams, LANES), 1)
    table = jnp.zeros((half_beams, LANES), jnp.float32)
    for at, mask in enumerate(masks):
        lists = extra[at * beams : at * beams + half_beams]
        owner = me ^ mask
        table = jnp.where(utt == owner, lists, table)
        table = jnp.where(utt == (owner ^ CORE), pltpu.roll(lists, LANES - beams, 1), table)
    chosen = jnp.concatenate(
        [
            jnp.sum(
                jnp.where(lane == PARENT_LANE + (me ^ mask), table, 0.0), axis=1, keepdims=True
            )
            for mask in rows_of(masks, beams)
        ],
        axis=0,
    ).astype(jnp.int32)

    row_rank = lax.broadcasted_iota(jnp.int32, (rows, keys), 0) % half_beams
    key = lax.broadcasted_iota(jnp.int32, (rows, keys), 1)
    key_rank = key % pair_keys // history
    run = key // pair_keys
    owner = me ^ jnp.where(
        run == 0, 0, jnp.where(run == 1, CORE, jnp.where(run == 2, PAIR, PAIR ^ CORE))
    )
    live = (key_rank == row_rank) & (chosen == owner)
    group = CORE | PAIR
    row_live = (chosen // (group + 1)) == (me // (group + 1))

    tiles = [slice(at, at + LANES) for at in range(0, keys, LANES)]
    for head in range(heads):
        at = slice(head * HD, (head + 1) * HD)
        scores = lax.dot_general(
            queries[:, at], cached(*cache_refs, mine, at), OVER_LAST, preferred_element_type=jnp.float32
        )
        scores = jnp.where(live, scores, 0.0)
        rest = sum(scores[:, tile] for tile in tiles)
        for term_at in range(3):
            term = rest.astype(jnp.bfloat16)
            rest = rest - term.astype(jnp.float32)
            terms_ref[head * rows : (head + 1) * rows, term_at * LANES : (term_at + 1) * LANES] = term
    row_lane = lax.broadcasted_iota(jnp.int32, (rows, LANES), 1)
    fold = lax.broadcasted_iota(jnp.int32, (3 * LANES, LANES), 0) % history
    fold = fold == lax.broadcasted_iota(jnp.int32, (3 * LANES, LANES), 1) % history
    fold = fold.astype(jnp.bfloat16)
    folded = jnp.dot(terms_ref[...], fold, preferred_element_type=jnp.float32)
    packed = jnp.zeros((rows, LANES), jnp.float32)
    for head in range(heads):
        packed = jnp.where(
            row_lane // history == head, folded[head * rows : (head + 1) * rows], packed
        )
    packed = packed * HD ** (-0.5)
    part = lax.broadcasted_iota(jnp.int32, (LANES, LANES), 0)
    spread = lax.broadcasted_iota(jnp.int32, (LANES, LANES), 1) // history
    spread = (part < 3 * heads) & (part % heads == spread)
    own = jnp.dot(
        queries[:, feature:], spread.astype(jnp.bfloat16), preferred_element_type=jnp.float32
    )

    def over_tokens(tile, combine):
        step = 1
        while step < history:
            left = pltpu.roll(tile, step, 1)
            right = pltpu.roll(tile, LANES - step, 1)
            tile = combine(tile, jnp.where(row_lane // step % 2 == 0, right, left))
            step = 2 * step
        return tile

    peak = jnp.maximum(over_tokens(packed, jnp.maximum), own)
    raised = jnp.exp(packed - peak)
    own = jnp.exp(own - peak)
    share = 1.0 / (over_tokens(raised, jnp.add) + own)
    share_ref[...] = jnp.where(row_live, own * share, 0.0).astype(jnp.bfloat16)
    packed = (raised * share).astype(jnp.bfloat16)
    for head in range(heads):
        spread_ref[head * rows : (head + 1) * rows] = jnp.where(
            row_lane // history == head, packed, jnp.zeros_like(packed)
        )
    weights = jnp.dot(spread_ref[...], fold[:LANES], preferred_element_type=jnp.float32)
    for head in range(heads):
        for tile in tiles:
            weight_ref[head, :, tile] = jnp.where(
                live[:, tile], weights[head * rows : (head + 1) * rows], 0.0
            ).astype(jnp.bfloat16)


def self_values_kernel(masks, *refs):
    weight_ref, share_ref, *cache_refs, cross_near_ref, cross_far_ref, send_ref, keep_ref = refs
    me = lax.axis_index("utt").astype(jnp.int32)
    mine = class_of(me)
    heads, rows, _ = weight_ref.shape
    feature = heads * HD
    half = rows // 2
    beams = cross_near_ref.shape[0]
    half_beams = beams // 2
    keep_ref[:, feature:] = share_ref[:half]
    send_ref[:, feature:] = share_ref[half:]

    place = lax.broadcasted_iota(jnp.int32, (rows, beams), 1)
    pick_utt = utt_of_rank(lax.broadcasted_iota(jnp.int32, (rows, beams), 0) % half_beams, me)
    row_beam = me ^ jnp.concatenate(
        [jnp.full((half_beams, beams), mask, jnp.int32) for mask in rows_of(masks, beams)], axis=0
    )
    near_pick = ((place == row_beam) & (pick_utt == me)).astype(jnp.bfloat16)
    far_pick = ((place == row_beam) & (pick_utt == (me ^ CORE))).astype(jnp.bfloat16)
    pick = jnp.concatenate([near_pick, far_pick], axis=1)
    for head in range(heads):
        at = slice(head * HD, (head + 1) * HD)
        out = jnp.dot(
            weight_ref[head], cached(*cache_refs, mine, at), preferred_element_type=jnp.float32
        )
        cross = jnp.concatenate([cross_near_ref[:, at], cross_far_ref[:, at]], axis=0)
        out = out + jnp.dot(pick, cross, preferred_element_type=jnp.float32)
        out = out.astype(jnp.bfloat16)
        keep_ref[:, at] = out[:half]
        send_ref[:, at] = out[half:]


def finish_kernel(history, mine_ref, came_ref, value_ref, out_ref):
    rows, feature = out_ref.shape
    order = class_order(rows, lax.axis_index("utt"))

    def ordered(at):
        tile = jnp.concatenate(
            [mine_ref[:, at].astype(jnp.float32), came_ref[:, at].astype(jnp.float32)], axis=0
        ).astype(jnp.bfloat16)
        return lax.dot_general(
            order, tile, (((0,), (0,)), ((), ())), preferred_element_type=jnp.float32
        )

    shares = ordered(slice(feature, feature + LANES))
    for head in range(feature // HD):
        at = slice(head * HD, (head + 1) * HD)
        out = ordered(at) + shares[:, head * history : head * history + 1] * value_ref[:, at].astype(jnp.float32)
        out_ref[:, at] = out.astype(jnp.bfloat16)


def whole(shape):
    return pl.BlockSpec(shape, lambda *_: (0,) * len(shape))


def body_by_parent(devices, cache_kv, new_rows, cross_queries, enc_kv, lengths, parents):
    beams = parents.shape[1]
    rows, feature = cross_queries.shape
    frames = enc_kv.shape[1]
    history = cache_kv.shape[1]
    heads = feature // HD
    width = feature + LANES
    keys = beams * history
    me = lax.axis_index("utt").astype(jnp.int32)
    params = pltpu.CompilerParams(vmem_limit_bytes=16 * 1024 * 1024)

    def swap(array, bits):
        return lax.ppermute(array, "utt", [(i, i ^ bits) for i in range(devices)])

    def after(array, *others):
        return lax.optimization_barrier((array,) + others)[0]

    hops = [(1 << k) | CORE for k in range(devices.bit_length() - 2, 1, -1)]

    near = cache_kv.reshape(beams // (2 * CLASS), 2, CLASS * history, 2 * feature)
    half_rows = jax.ShapeDtypeStruct((rows // 2, width), jnp.bfloat16)
    half_cache = jax.ShapeDtypeStruct(near.shape[:1] + near.shape[2:], jnp.bfloat16)
    own, other, other_cache = pl.pallas_call(
        pack_kernel,
        out_shape=(half_rows, half_rows, half_cache),
        in_specs=[pl.BlockSpec(memory_space=pltpu.HBM)] * 3,
        out_specs=(whole(half_rows.shape), whole(half_rows.shape), whole(half_cache.shape)),
        scratch_shapes=[
            pltpu.VMEM((rows, feature), jnp.bfloat16),
            pltpu.VMEM((rows, feature), jnp.bfloat16),
            pltpu.VMEM(parents.shape, jnp.int32),
            pltpu.SemaphoreType.DMA((4,)),
        ],
        compiler_params=params,
    )(
        pltpu.with_memory_space_constraint(new_rows, pltpu.HBM),
        pltpu.with_memory_space_constraint(parents, pltpu.HBM),
        pltpu.with_memory_space_constraint(near, pltpu.HBM),
    )
    pair_rows = swap(other, PAIR)
    far = swap(near, CORE)
    pair_near = swap(other_cache, PAIR).reshape(keys // 2, 2 * feature)

    lists = jnp.pad(
        swap(after(parents, other), CORE).astype(jnp.bfloat16),
        ((0, 0), (feature + PARENT_LANE + beams, LANES - PARENT_LANE - 2 * beams)),
    )
    held = jnp.concatenate([own + lists, pair_rows], axis=0)
    gathered, masks, held_masks = [held], [0], [0]

    frames_kv = pltpu.with_memory_space_constraint(enc_kv.reshape(frames, 2 * feature), pltpu.HBM)
    frames_scratch = [pltpu.VMEM((frames, feature), jnp.bfloat16), pltpu.SemaphoreType.DMA(())]
    cross_weights = pl.pallas_call(
        cross_weights_kernel,
        out_shape=jax.ShapeDtypeStruct((heads, rows, frames), jnp.bfloat16),
        grid=(1,),
        in_specs=[
            whole((1, 1)),
            whole((rows, feature)),
            pl.BlockSpec(memory_space=pltpu.HBM),
        ],
        out_specs=whole((heads, rows, frames)),
        scratch_shapes=frames_scratch,
        compiler_params=params,
    )(lengths.reshape(1, 1), after(cross_queries, held), frames_kv)
    for bits in hops:
        came = swap(held, bits)
        gathered.append(came)
        masks = masks + [mask ^ bits for mask in held_masks]
        held_masks = masks
        if bits != hops[-1]:
            held = after(jnp.concatenate([held, came], axis=0), cross_weights)

    cross_near = pl.pallas_call(
        cross_values_kernel,
        out_shape=jax.ShapeDtypeStruct((rows, feature), jnp.bfloat16),
        grid=(1,),
        in_specs=[whole((heads, rows, frames)), pl.BlockSpec(memory_space=pltpu.HBM)],
        out_specs=whole((rows, feature)),
        scratch_shapes=frames_scratch,
        compiler_params=params,
    )(after(cross_weights, held), frames_kv)
    cross_far = swap(cross_near, CORE)

    pair_keys, pair_values = pair_near[:, :feature], pair_near[:, feature:]
    pair_far_keys = swap(after(pair_keys, held), CORE)
    pair_far_values = swap(after(pair_values, gathered[-1], cross_near), CORE)

    all_rows = rows * len(masks)
    half = all_rows // 2
    weight_shape = jax.ShapeDtypeStruct((heads, all_rows, 2 * keys), jnp.bfloat16)
    share_shape = jax.ShapeDtypeStruct((all_rows, LANES), jnp.bfloat16)
    part = jax.ShapeDtypeStruct((half, width), jnp.bfloat16)
    near_shape = near.shape[:3] + (feature,)
    in_keys = pl.BlockSpec(near_shape, lambda i: (0, 0, 0, 0))
    in_values = pl.BlockSpec(near_shape, lambda i: (0, 0, 0, 1))
    pair_spec = whole(pair_keys.shape)
    weights, shares = pl.pallas_call(
        functools.partial(self_weights_kernel, tuple(masks), len(gathered)),
        out_shape=(weight_shape, share_shape),
        grid=(1,),
        in_specs=[whole(block.shape) for block in gathered]
        + [in_keys, in_keys, pair_spec, pair_spec],
        out_specs=(whole(weight_shape.shape), whole(share_shape.shape)),
        scratch_shapes=[
            pltpu.VMEM((heads * all_rows, 3 * LANES), jnp.bfloat16),
            pltpu.VMEM((heads * all_rows, LANES), jnp.bfloat16),
        ],
        compiler_params=params,
    )(*gathered, near, far, pair_keys, pair_far_keys)
    send, keep = pl.pallas_call(
        functools.partial(self_values_kernel, tuple(masks)),
        out_shape=(part, part),
        grid=(1,),
        in_specs=[whole(weights.shape), whole(shares.shape)]
        + [in_values, in_values, pair_spec, pair_spec]
        + [whole((rows, feature))] * 2,
        out_specs=(whole(part.shape), whole(part.shape)),
        compiler_params=params,
    )(weights, shares, near, far, pair_values, pair_far_values, cross_near, cross_far)

    for bits in hops[::-1]:
        came = swap(send, bits)
        half = half // 2
        send = keep[half:] + came[half:]
        keep = keep[:half] + came[:half]
    came = swap(send, PAIR)

    return pl.pallas_call(
        functools.partial(finish_kernel, history),
        out_shape=jax.ShapeDtypeStruct((rows, feature), jnp.bfloat16),
        grid=(1,),
        in_specs=[
            whole(half_rows.shape),
            whole(half_rows.shape),
            pl.BlockSpec((rows, feature), lambda i: (0, 2)),
        ],
        out_specs=whole((rows, feature)),
        compiler_params=params,
    )(keep, came, new_rows)


def solution(mesh):
    placed = (
        P(("groups", "utt"), None, None),
        P(("groups", "utt"), None),
        P(("groups", "utt"), None),
        P(("groups", "utt"), None, None),
        P(("groups", "utt")),
        P(("groups", "utt"), None),
    )
    devices = mesh.shape["utt"]

    def body(cache_kv, new_rows, cross_queries, enc_kv, lengths, parents):
        beams = parents.shape[1]
        heads = cross_queries.shape[1] // HD
        history = cache_kv.shape[1]
        fits = (
            parents.shape[0] == 1
            and devices == beams
            and devices >= 8
            and devices & (devices - 1) == 0
            and beams % 16 == 0
            and history & (history - 1) == 0
            and heads * history <= LANES
            and 3 * heads <= PARENT_LANE
            and PARENT_LANE + 2 * beams <= LANES
        )
        plan = functools.partial(body_by_parent, devices) if fits else body_by_utterance
        return plan(cache_kv, new_rows, cross_queries, enc_kv, lengths, parents)

    return jax.shard_map(
        body, mesh=mesh, in_specs=placed, out_specs=P(("groups", "utt"), None), check_vma=False
    )
```

```python
import functools

import jax
import jax.numpy as jnp
from jax import lax
from jax.experimental import pallas as pl
from jax.experimental.pallas import tpu as pltpu
from jax.sharding import PartitionSpec as P

HD = 128
LANES = 128
PARENT_LANE = 64
MASKED = -1e30


def reorder(cache_rows, parents):
    utterances, beam_width = parents.shape
    grouped = cache_rows.reshape(utterances, beam_width, cache_rows.shape[1], cache_rows.shape[2])
    picked = jax.vmap(lambda block, picks: block[picks])(grouped, parents)
    return picked.reshape(cache_rows.shape)


def attend_self(query, old_keys, old_values, new_key, new_value):
    row_count = query.shape[0]
    history = old_keys.shape[1]
    head_count = query.shape[1] // HD
    scale = HD ** (-0.5)
    query_heads = query.reshape(row_count, head_count, HD)
    key_heads = old_keys.reshape(row_count, history, head_count, HD)
    value_heads = old_values.reshape(row_count, history, head_count, HD)
    old_scores = (
        jnp.einsum("rhd,rthd->rht", query_heads, key_heads, preferred_element_type=jnp.float32)
        * scale
    )
    own_score = (
        jnp.einsum(
            "rhd,rhd->rh",
            query_heads,
            new_key.reshape(row_count, head_count, HD),
            preferred_element_type=jnp.float32,
        )
        * scale
    )
    peak = jnp.maximum(jnp.max(old_scores, axis=2), own_score)
    old_exp = jnp.exp(old_scores - peak[:, :, None])
    own_exp = jnp.exp(own_score - peak)
    total = jnp.sum(old_exp, axis=2) + own_exp
    old_weight = (old_exp / total[:, :, None]).astype(jnp.bfloat16)
    own_weight = (own_exp / total).astype(jnp.bfloat16)
    context = jnp.einsum(
        "rht,rthd->rhd", old_weight, value_heads, preferred_element_type=jnp.float32
    )
    context = context + own_weight.astype(jnp.float32)[:, :, None] * new_value.reshape(
        row_count, head_count, HD
    ).astype(jnp.float32)
    return context.reshape(row_count, head_count * HD).astype(jnp.bfloat16)


def attend_frames(queries, frames_kv, frame_counts):
    utterances = frame_counts.shape[0]
    beam_width = queries.shape[0] // utterances
    feature = queries.shape[1]
    head_count = feature // HD
    frame_total = frames_kv.shape[1]
    scale = HD ** (-0.5)
    query_heads = queries.reshape(utterances, beam_width, head_count, HD)
    key_heads = frames_kv[:, :, :feature].reshape(utterances, frame_total, head_count, HD)
    value_heads = frames_kv[:, :, feature:].reshape(utterances, frame_total, head_count, HD)
    scores = (
        jnp.einsum("ubhd,ufhd->uhbf", query_heads, key_heads, preferred_element_type=jnp.float32)
        * scale
    )
    live = (
        lax.broadcasted_iota(jnp.int32, (utterances, 1, 1, frame_total), 3)
        < frame_counts[:, None, None, None]
    )
    scores = jnp.where(live, scores, -1e30)
    peak = jnp.max(scores, axis=3, keepdims=True)
    raised = jnp.where(live, jnp.exp(scores - peak), 0.0)
    weights = (raised / jnp.sum(raised, axis=3, keepdims=True)).astype(jnp.bfloat16)
    context = jnp.einsum(
        "uhbf,ufhd->ubhd", weights, value_heads, preferred_element_type=jnp.float32
    )
    return context.reshape(utterances * beam_width, feature)


def body_by_utterance(cache_kv, new_rows, cross_queries, enc_kv, lengths, parents):
    feature = cross_queries.shape[1]
    cross_context = attend_frames(cross_queries, enc_kv, lengths)
    arrived, new_here = (
        lax.all_to_all(cache_kv, "utt", split_axis=0, concat_axis=0, tiled=True),
        lax.all_to_all(new_rows, "utt", split_axis=0, concat_axis=0, tiled=True),
    )
    reordered = reorder(arrived, parents)
    self_context = attend_self(
        new_here[:, :feature],
        reordered[:, :, :feature],
        reordered[:, :, feature:],
        new_here[:, feature : 2 * feature],
        new_here[:, 2 * feature :],
    )
    mixed_here = (self_context.astype(jnp.float32) + cross_context).astype(jnp.bfloat16)
    mixed = lax.all_to_all(mixed_here, "utt", split_axis=0, concat_axis=0, tiled=True)
    return mixed


CORE = 1
CLASS = 2
PAIR = CLASS | CORE
OVER_LAST = (((1,), (1,)), ((), ()))


def class_of(index):
    return (index // CLASS) % 2


def rank_in_class(utt):
    return utt // (2 * CLASS) * CLASS + utt % CLASS


def utt_of_rank(rank, device):
    return rank // CLASS * (2 * CLASS) + class_of(device) * CLASS + rank % CLASS


def class_order(beams, device):
    row = lax.broadcasted_iota(jnp.int32, (beams, beams), 0)
    col = lax.broadcasted_iota(jnp.int32, (beams, beams), 1)
    half = beams // 2
    place = rank_in_class(col) + jnp.where(class_of(col) == class_of(device), 0, half)
    return (row == place).astype(jnp.bfloat16)


def pack_kernel(
    new_ref, parents_hbm_ref, cache_ref, keep_ref, send_ref, other_ref, query_ref, key_ref, parents_ref, sems
):
    rows, feature = query_ref.shape
    other = 1 - class_of(lax.axis_index("utt").astype(jnp.int32))
    slicing = pltpu.make_async_copy(cache_ref.at[:, other], other_ref, sems.at[3])
    copies = [
        pltpu.make_async_copy(new_ref.at[:, :feature], query_ref, sems.at[0]),
        pltpu.make_async_copy(new_ref.at[:, feature : 2 * feature], key_ref, sems.at[1]),
        pltpu.make_async_copy(parents_hbm_ref, parents_ref, sems.at[2]),
    ]
    for copy in copies:
        copy.start()
    slicing.start()
    half = rows // 2
    beams = parents_ref.shape[1]
    order = class_order(rows, lax.axis_index("utt"))
    for copy in copies:
        copy.wait()
    query = query_ref[...]
    product = query.astype(jnp.float32) * key_ref[...].astype(jnp.float32)
    lane = lax.broadcasted_iota(jnp.int32, (rows, LANES), 1)
    heads = feature // HD
    at_parent_lane = lax.broadcasted_iota(jnp.int32, (beams, LANES), 0) + PARENT_LANE
    at_parent_lane = at_parent_lane == lax.broadcasted_iota(jnp.int32, (beams, LANES), 1)
    extra = jnp.dot(
        jnp.broadcast_to(parents_ref[...], (rows, beams)).astype(jnp.bfloat16),
        at_parent_lane.astype(jnp.bfloat16),
        preferred_element_type=jnp.float32,
    )
    for head in range(heads):
        own = jnp.sum(product[:, head * HD : (head + 1) * HD], axis=1, keepdims=True) * HD ** (-0.5)
        for part in range(3):
            term = own.astype(jnp.bfloat16).astype(jnp.float32)
            extra = jnp.where(lane == part * heads + head, term, extra)
            own = own - term
    extra = extra.astype(jnp.bfloat16)
    for at in range(0, feature + LANES, LANES):
        tile = query[:, at : at + LANES] if at < feature else extra
        tile = jnp.dot(order, tile, preferred_element_type=jnp.float32)
        keep_ref[:, at : at + LANES] = tile[:half].astype(jnp.bfloat16)
        send_ref[:, at : at + LANES] = tile[half:].astype(jnp.bfloat16)
    slicing.wait()


def cross_weights_kernel(
    lengths_ref, query_hbm_ref, frames_ref, out_ref, query_ref, keys_ref, sems
):
    rows, feature = query_ref.shape
    copies = [
        pltpu.make_async_copy(frames_ref.at[:, :feature], keys_ref, sems.at[0]),
        pltpu.make_async_copy(query_hbm_ref, query_ref, sems.at[1]),
    ]
    for copy in copies:
        copy.start()
    for copy in copies:
        copy.wait()
    frames = keys_ref.shape[0]
    heads = feature // HD
    live = lax.broadcasted_iota(jnp.int32, (rows, frames), 1) < lengths_ref[:, :1]
    scores = []
    for head in range(heads):
        at = slice(head * HD, (head + 1) * HD)
        scores.append(
            lax.dot_general(
                query_ref[:, at], keys_ref[:, at], OVER_LAST, preferred_element_type=jnp.float32
            )
        )
    for head in range(heads):
        masked = jnp.where(live, scores[head] * HD ** (-0.5), MASKED)
        raised = jnp.where(live, jnp.exp(masked - jnp.max(masked, axis=1, keepdims=True)), 0.0)
        weights = raised / jnp.sum(raised, axis=1, keepdims=True)
        out_ref[head] = weights.astype(jnp.bfloat16)


def cross_values_kernel(weights_ref, frames_ref, out_ref, values_ref, sem):
    feature = values_ref.shape[1]
    copy = pltpu.make_async_copy(frames_ref.at[:, feature:], values_ref, sem)
    copy.start()
    copy.wait()
    for head in range(weights_ref.shape[0]):
        at = slice(head * HD, (head + 1) * HD)
        out_ref[:, at] = jnp.dot(
            weights_ref[head], values_ref[:, at], preferred_element_type=jnp.float32
        ).astype(jnp.bfloat16)


def cached(near_ref, far_ref, pair_near_ref, pair_far_ref, mine, at):
    pieces = [ref[part, mine, :, at] for ref in (near_ref, far_ref) for part in range(near_ref.shape[0])]
    return jnp.concatenate(pieces + [pair_near_ref[:, at], pair_far_ref[:, at]], axis=0)


def rows_of(masks, beams):
    return [mask ^ pair for mask in masks for pair in (0, PAIR)]


def self_weights_kernel(masks, counts, *refs):
    query_refs, refs = refs[:counts], refs[counts:]
    *cache_refs, weight_ref, share_ref, terms_ref, spread_ref = refs
    me = lax.axis_index("utt").astype(jnp.int32)
    mine = class_of(me)
    pair_keys, feature = cache_refs[-1].shape
    heads, rows, keys = weight_ref.shape
    beams = query_refs[0].shape[0]
    half_beams = beams // 2
    history = pair_keys // half_beams
    queries = jnp.concatenate([ref[...] for ref in query_refs], axis=0)
    extra = queries[:, feature:].astype(jnp.float32)

    utt = utt_of_rank(lax.broadcasted_iota(jnp.int32, (half_beams, LANES), 0), me)
    lane = lax.broadcasted_iota(jnp.int32, (half_beams, LANES), 1)
    table = jnp.zeros((half_beams, LANES), jnp.float32)
    for at, mask in enumerate(masks):
        lists = extra[at * beams : at * beams + half_beams]
        owner = me ^ mask
        table = jnp.where(utt == owner, lists, table)
        table = jnp.where(utt == (owner ^ CORE), pltpu.roll(lists, LANES - beams, 1), table)
    chosen = jnp.concatenate(
        [
            jnp.sum(
                jnp.where(lane == PARENT_LANE + (me ^ mask), table, 0.0), axis=1, keepdims=True
            )
            for mask in rows_of(masks, beams)
        ],
        axis=0,
    ).astype(jnp.int32)

    row_rank = lax.broadcasted_iota(jnp.int32, (rows, keys), 0) % half_beams
    key = lax.broadcasted_iota(jnp.int32, (rows, keys), 1)
    key_rank = key % pair_keys // history
    run = key // pair_keys
    owner = me ^ jnp.where(
        run == 0, 0, jnp.where(run == 1, CORE, jnp.where(run == 2, PAIR, PAIR ^ CORE))
    )
    live = (key_rank == row_rank) & (chosen == owner)
    group = CORE | PAIR
    row_live = (chosen // (group + 1)) == (me // (group + 1))

    tiles = [slice(at, at + LANES) for at in range(0, keys, LANES)]
    for head in range(heads):
        at = slice(head * HD, (head + 1) * HD)
        scores = lax.dot_general(
            queries[:, at], cached(*cache_refs, mine, at), OVER_LAST, preferred_element_type=jnp.float32
        )
        scores = jnp.where(live, scores, 0.0)
        rest = sum(scores[:, tile] for tile in tiles)
        for term_at in range(3):
            term = rest.astype(jnp.bfloat16)
            rest = rest - term.astype(jnp.float32)
            terms_ref[head * rows : (head + 1) * rows, term_at * LANES : (term_at + 1) * LANES] = term
    row_lane = lax.broadcasted_iota(jnp.int32, (rows, LANES), 1)
    fold = lax.broadcasted_iota(jnp.int32, (3 * LANES, LANES), 0) % history
    fold = fold == lax.broadcasted_iota(jnp.int32, (3 * LANES, LANES), 1) % history
    fold = fold.astype(jnp.bfloat16)
    folded = jnp.dot(terms_ref[...], fold, preferred_element_type=jnp.float32)
    packed = jnp.zeros((rows, LANES), jnp.float32)
    for head in range(heads):
        packed = jnp.where(
            row_lane // history == head, folded[head * rows : (head + 1) * rows], packed
        )
    packed = packed * HD ** (-0.5)
    part = lax.broadcasted_iota(jnp.int32, (LANES, LANES), 0)
    spread = lax.broadcasted_iota(jnp.int32, (LANES, LANES), 1) // history
    spread = (part < 3 * heads) & (part % heads == spread)
    own = jnp.dot(
        queries[:, feature:], spread.astype(jnp.bfloat16), preferred_element_type=jnp.float32
    )

    def over_tokens(tile, combine):
        step = 1
        while step < history:
            left = pltpu.roll(tile, step, 1)
            right = pltpu.roll(tile, LANES - step, 1)
            tile = combine(tile, jnp.where(row_lane // step % 2 == 0, right, left))
            step = 2 * step
        return tile

    peak = jnp.maximum(over_tokens(packed, jnp.maximum), own)
    raised = jnp.exp(packed - peak)
    own = jnp.exp(own - peak)
    share = 1.0 / (over_tokens(raised, jnp.add) + own)
    share_ref[...] = jnp.where(row_live, own * share, 0.0).astype(jnp.bfloat16)
    packed = (raised * share).astype(jnp.bfloat16)
    for head in range(heads):
        spread_ref[head * rows : (head + 1) * rows] = jnp.where(
            row_lane // history == head, packed, jnp.zeros_like(packed)
        )
    weights = jnp.dot(spread_ref[...], fold[:LANES], preferred_element_type=jnp.float32)
    for head in range(heads):
        for tile in tiles:
            weight_ref[head, :, tile] = jnp.where(
                live[:, tile], weights[head * rows : (head + 1) * rows], 0.0
            ).astype(jnp.bfloat16)


def self_values_kernel(masks, *refs):
    weight_ref, share_ref, *cache_refs, cross_near_ref, cross_far_ref, send_ref, keep_ref = refs
    me = lax.axis_index("utt").astype(jnp.int32)
    mine = class_of(me)
    heads, rows, _ = weight_ref.shape
    feature = heads * HD
    half = rows // 2
    beams = cross_near_ref.shape[0]
    half_beams = beams // 2
    keep_ref[:, feature:] = share_ref[:half]
    send_ref[:, feature:] = share_ref[half:]

    place = lax.broadcasted_iota(jnp.int32, (rows, beams), 1)
    pick_utt = utt_of_rank(lax.broadcasted_iota(jnp.int32, (rows, beams), 0) % half_beams, me)
    row_beam = me ^ jnp.concatenate(
        [jnp.full((half_beams, beams), mask, jnp.int32) for mask in rows_of(masks, beams)], axis=0
    )
    near_pick = ((place == row_beam) & (pick_utt == me)).astype(jnp.bfloat16)
    far_pick = ((place == row_beam) & (pick_utt == (me ^ CORE))).astype(jnp.bfloat16)
    pick = jnp.concatenate([near_pick, far_pick], axis=1)
    for head in range(heads):
        at = slice(head * HD, (head + 1) * HD)
        out = jnp.dot(
            weight_ref[head], cached(*cache_refs, mine, at), preferred_element_type=jnp.float32
        )
        cross = jnp.concatenate([cross_near_ref[:, at], cross_far_ref[:, at]], axis=0)
        out = out + jnp.dot(pick, cross, preferred_element_type=jnp.float32)
        out = out.astype(jnp.bfloat16)
        keep_ref[:, at] = out[:half]
        send_ref[:, at] = out[half:]


def finish_kernel(history, mine_ref, came_ref, value_ref, out_ref):
    rows, feature = out_ref.shape
    order = class_order(rows, lax.axis_index("utt"))

    def ordered(at):
        tile = jnp.concatenate(
            [mine_ref[:, at].astype(jnp.float32), came_ref[:, at].astype(jnp.float32)], axis=0
        ).astype(jnp.bfloat16)
        return lax.dot_general(
            order, tile, (((0,), (0,)), ((), ())), preferred_element_type=jnp.float32
        )

    shares = ordered(slice(feature, feature + LANES))
    for head in range(feature // HD):
        at = slice(head * HD, (head + 1) * HD)
        out = ordered(at) + shares[:, head * history : head * history + 1] * value_ref[:, at].astype(jnp.float32)
        out_ref[:, at] = out.astype(jnp.bfloat16)


def whole(shape):
    return pl.BlockSpec(shape, lambda *_: (0,) * len(shape))


def body_by_parent(devices, cache_kv, new_rows, cross_queries, enc_kv, lengths, parents):
    beams = parents.shape[1]
    rows, feature = cross_queries.shape
    frames = enc_kv.shape[1]
    history = cache_kv.shape[1]
    heads = feature // HD
    width = feature + LANES
    keys = beams * history
    me = lax.axis_index("utt").astype(jnp.int32)
    params = pltpu.CompilerParams(vmem_limit_bytes=16 * 1024 * 1024)

    def swap(array, bits):
        return lax.ppermute(array, "utt", [(i, i ^ bits) for i in range(devices)])

    def after(array, *others):
        return lax.optimization_barrier((array,) + others)[0]

    def in_hbm(array):
        return pltpu.with_memory_space_constraint(array, pltpu.HBM)

    hops = [(1 << k) | CORE for k in range(devices.bit_length() - 2, 1, -1)]

    near = cache_kv.reshape(beams // (2 * CLASS), 2, CLASS * history, 2 * feature)
    half_rows = jax.ShapeDtypeStruct((rows // 2, width), jnp.bfloat16)
    half_cache = jax.ShapeDtypeStruct(near.shape[:1] + near.shape[2:], jnp.bfloat16)
    own, other, other_cache = pl.pallas_call(
        pack_kernel,
        out_shape=(half_rows, half_rows, half_cache),
        in_specs=[pl.BlockSpec(memory_space=pltpu.HBM)] * 3,
        out_specs=(whole(half_rows.shape), whole(half_rows.shape), whole(half_cache.shape)),
        scratch_shapes=[
            pltpu.VMEM((rows, feature), jnp.bfloat16),
            pltpu.VMEM((rows, feature), jnp.bfloat16),
            pltpu.VMEM(parents.shape, jnp.int32),
            pltpu.SemaphoreType.DMA((4,)),
        ],
        compiler_params=params,
    )(
        in_hbm(new_rows),
        in_hbm(parents),
        in_hbm(near),
    )
    pair_rows = swap(other, PAIR)
    far = swap(near, CORE)
    pair_near = swap(other_cache, PAIR).reshape(keys // 2, 2 * feature)

    lists = jnp.pad(
        swap(after(parents, other), CORE).astype(jnp.bfloat16),
        ((0, 0), (feature + PARENT_LANE + beams, LANES - PARENT_LANE - 2 * beams)),
    )
    frame_count = jnp.broadcast_to(lengths.reshape(1, 1), (1, LANES))
    held = after(jnp.concatenate([own + lists, pair_rows], axis=0), frame_count)
    gathered, masks, held_masks = [held], [0], [0]

    frames_kv = in_hbm(enc_kv.reshape(frames, 2 * feature))
    cross_weights = pl.pallas_call(
        cross_weights_kernel,
        out_shape=jax.ShapeDtypeStruct((heads, rows, frames), jnp.bfloat16),
        in_specs=[whole((1, LANES))] + [pl.BlockSpec(memory_space=pltpu.HBM)] * 2,
        out_specs=whole((heads, rows, frames)),
        scratch_shapes=[
            pltpu.VMEM((rows, feature), jnp.bfloat16),
            pltpu.VMEM((frames, feature), jnp.bfloat16),
            pltpu.SemaphoreType.DMA((2,)),
        ],
        compiler_params=params,
    )(frame_count, in_hbm(after(cross_queries, held)), frames_kv)
    for bits in hops:
        came = swap(held, bits)
        gathered.append(came)
        masks = masks + [mask ^ bits for mask in held_masks]
        held_masks = masks
        if bits != hops[-1]:
            held = after(jnp.concatenate([held, came], axis=0), cross_weights)

    cross_near = pl.pallas_call(
        cross_values_kernel,
        out_shape=jax.ShapeDtypeStruct((rows, feature), jnp.bfloat16),
        grid=(1,),
        in_specs=[whole((heads, rows, frames)), pl.BlockSpec(memory_space=pltpu.HBM)],
        out_specs=whole((rows, feature)),
        scratch_shapes=[
            pltpu.VMEM((frames, feature), jnp.bfloat16),
            pltpu.SemaphoreType.DMA(()),
        ],
        compiler_params=params,
    )(after(cross_weights, held), frames_kv)
    cross_far = swap(cross_near, CORE)

    pair_keys, pair_values = pair_near[:, :feature], pair_near[:, feature:]
    pair_far_keys = swap(after(pair_keys, held), CORE)
    pair_far_values = swap(after(pair_values, gathered[-1], cross_near), CORE)

    all_rows = rows * len(masks)
    half = all_rows // 2
    weight_shape = jax.ShapeDtypeStruct((heads, all_rows, 2 * keys), jnp.bfloat16)
    share_shape = jax.ShapeDtypeStruct((all_rows, LANES), jnp.bfloat16)
    part = jax.ShapeDtypeStruct((half, width), jnp.bfloat16)
    near_shape = near.shape[:3] + (feature,)
    in_keys = pl.BlockSpec(near_shape, lambda i: (0, 0, 0, 0))
    in_values = pl.BlockSpec(near_shape, lambda i: (0, 0, 0, 1))
    pair_spec = whole(pair_keys.shape)
    weights, shares = pl.pallas_call(
        functools.partial(self_weights_kernel, tuple(masks), len(gathered)),
        out_shape=(weight_shape, share_shape),
        grid=(1,),
        in_specs=[whole(block.shape) for block in gathered]
        + [in_keys, in_keys, pair_spec, pair_spec],
        out_specs=(whole(weight_shape.shape), whole(share_shape.shape)),
        scratch_shapes=[
            pltpu.VMEM((heads * all_rows, 3 * LANES), jnp.bfloat16),
            pltpu.VMEM((heads * all_rows, LANES), jnp.bfloat16),
        ],
        compiler_params=params,
    )(*gathered, near, far, pair_keys, pair_far_keys)
    send, keep = pl.pallas_call(
        functools.partial(self_values_kernel, tuple(masks)),
        out_shape=(part, part),
        grid=(1,),
        in_specs=[whole(weights.shape), whole(shares.shape)]
        + [in_values, in_values, pair_spec, pair_spec]
        + [whole((rows, feature))] * 2,
        out_specs=(whole(part.shape), whole(part.shape)),
        compiler_params=params,
    )(weights, shares, near, far, pair_values, pair_far_values, cross_near, cross_far)

    for bits in hops[::-1]:
        came = swap(send, bits)
        half = half // 2
        send = keep[half:] + came[half:]
        keep = keep[:half] + came[:half]
    came = swap(send, PAIR)

    return pl.pallas_call(
        functools.partial(finish_kernel, history),
        out_shape=jax.ShapeDtypeStruct((rows, feature), jnp.bfloat16),
        grid=(1,),
        in_specs=[
            whole(half_rows.shape),
            whole(half_rows.shape),
            pl.BlockSpec((rows, feature), lambda i: (0, 2)),
        ],
        out_specs=whole((rows, feature)),
        compiler_params=params,
    )(keep, came, new_rows)


def solution(mesh):
    placed = (
        P(("groups", "utt"), None, None),
        P(("groups", "utt"), None),
        P(("groups", "utt"), None),
        P(("groups", "utt"), None, None),
        P(("groups", "utt")),
        P(("groups", "utt"), None),
    )
    devices = mesh.shape["utt"]

    def body(cache_kv, new_rows, cross_queries, enc_kv, lengths, parents):
        beams = parents.shape[1]
        heads = cross_queries.shape[1] // HD
        history = cache_kv.shape[1]
        fits = (
            parents.shape[0] == 1
            and devices == beams
            and devices >= 8
            and devices & (devices - 1) == 0
            and beams % 16 == 0
            and history & (history - 1) == 0
            and heads * history <= LANES
            and 3 * heads <= PARENT_LANE
            and PARENT_LANE + 2 * beams <= LANES
        )
        plan = functools.partial(body_by_parent, devices) if fits else body_by_utterance
        return plan(cache_kv, new_rows, cross_queries, enc_kv, lengths, parents)

    return jax.shard_map(
        body, mesh=mesh, in_specs=placed, out_specs=P(("groups", "utt"), None), check_vma=False
    )
```

```python
import functools

import jax
import jax.numpy as jnp
from jax import lax
from jax.experimental import pallas as pl
from jax.experimental.pallas import tpu as pltpu
from jax.sharding import PartitionSpec as P

HD = 128
LANES = 128
PARENT_LANE = 64
MASKED = -1e30


def reorder(cache_rows, parents):
    utterances, beam_width = parents.shape
    grouped = cache_rows.reshape(utterances, beam_width, cache_rows.shape[1], cache_rows.shape[2])
    picked = jax.vmap(lambda block, picks: block[picks])(grouped, parents)
    return picked.reshape(cache_rows.shape)


def attend_self(query, old_keys, old_values, new_key, new_value):
    row_count = query.shape[0]
    history = old_keys.shape[1]
    head_count = query.shape[1] // HD
    scale = HD ** (-0.5)
    query_heads = query.reshape(row_count, head_count, HD)
    key_heads = old_keys.reshape(row_count, history, head_count, HD)
    value_heads = old_values.reshape(row_count, history, head_count, HD)
    old_scores = (
        jnp.einsum("rhd,rthd->rht", query_heads, key_heads, preferred_element_type=jnp.float32)
        * scale
    )
    own_score = (
        jnp.einsum(
            "rhd,rhd->rh",
            query_heads,
            new_key.reshape(row_count, head_count, HD),
            preferred_element_type=jnp.float32,
        )
        * scale
    )
    peak = jnp.maximum(jnp.max(old_scores, axis=2), own_score)
    old_exp = jnp.exp(old_scores - peak[:, :, None])
    own_exp = jnp.exp(own_score - peak)
    total = jnp.sum(old_exp, axis=2) + own_exp
    old_weight = (old_exp / total[:, :, None]).astype(jnp.bfloat16)
    own_weight = (own_exp / total).astype(jnp.bfloat16)
    context = jnp.einsum(
        "rht,rthd->rhd", old_weight, value_heads, preferred_element_type=jnp.float32
    )
    context = context + own_weight.astype(jnp.float32)[:, :, None] * new_value.reshape(
        row_count, head_count, HD
    ).astype(jnp.float32)
    return context.reshape(row_count, head_count * HD).astype(jnp.bfloat16)


def attend_frames(queries, frames_kv, frame_counts):
    utterances = frame_counts.shape[0]
    beam_width = queries.shape[0] // utterances
    feature = queries.shape[1]
    head_count = feature // HD
    frame_total = frames_kv.shape[1]
    scale = HD ** (-0.5)
    query_heads = queries.reshape(utterances, beam_width, head_count, HD)
    key_heads = frames_kv[:, :, :feature].reshape(utterances, frame_total, head_count, HD)
    value_heads = frames_kv[:, :, feature:].reshape(utterances, frame_total, head_count, HD)
    scores = (
        jnp.einsum("ubhd,ufhd->uhbf", query_heads, key_heads, preferred_element_type=jnp.float32)
        * scale
    )
    live = (
        lax.broadcasted_iota(jnp.int32, (utterances, 1, 1, frame_total), 3)
        < frame_counts[:, None, None, None]
    )
    scores = jnp.where(live, scores, -1e30)
    peak = jnp.max(scores, axis=3, keepdims=True)
    raised = jnp.where(live, jnp.exp(scores - peak), 0.0)
    weights = (raised / jnp.sum(raised, axis=3, keepdims=True)).astype(jnp.bfloat16)
    context = jnp.einsum(
        "uhbf,ufhd->ubhd", weights, value_heads, preferred_element_type=jnp.float32
    )
    return context.reshape(utterances * beam_width, feature)


def body_by_utterance(cache_kv, new_rows, cross_queries, enc_kv, lengths, parents):
    feature = cross_queries.shape[1]
    cross_context = attend_frames(cross_queries, enc_kv, lengths)
    arrived, new_here = (
        lax.all_to_all(cache_kv, "utt", split_axis=0, concat_axis=0, tiled=True),
        lax.all_to_all(new_rows, "utt", split_axis=0, concat_axis=0, tiled=True),
    )
    reordered = reorder(arrived, parents)
    self_context = attend_self(
        new_here[:, :feature],
        reordered[:, :, :feature],
        reordered[:, :, feature:],
        new_here[:, feature : 2 * feature],
        new_here[:, 2 * feature :],
    )
    mixed_here = (self_context.astype(jnp.float32) + cross_context).astype(jnp.bfloat16)
    mixed = lax.all_to_all(mixed_here, "utt", split_axis=0, concat_axis=0, tiled=True)
    return mixed


CORE = 1
CLASS = 2
PAIR = CLASS | CORE
OVER_LAST = (((1,), (1,)), ((), ()))


def class_of(index):
    return (index // CLASS) % 2


def rank_in_class(utt):
    return utt // (2 * CLASS) * CLASS + utt % CLASS


def utt_of_rank(rank, device):
    return rank // CLASS * (2 * CLASS) + class_of(device) * CLASS + rank % CLASS


def class_order(beams, device):
    row = lax.broadcasted_iota(jnp.int32, (beams, beams), 0)
    col = lax.broadcasted_iota(jnp.int32, (beams, beams), 1)
    half = beams // 2
    place = rank_in_class(col) + jnp.where(class_of(col) == class_of(device), 0, half)
    return (row == place).astype(jnp.bfloat16)


def pack_kernel(
    new_ref, parents_hbm_ref, cache_ref, keep_ref, send_ref, other_ref, query_ref, key_ref, parents_ref, sems
):
    rows, feature = query_ref.shape
    other = 1 - class_of(lax.axis_index("utt").astype(jnp.int32))
    slicing = pltpu.make_async_copy(cache_ref.at[:, other], other_ref, sems.at[3])
    copies = [
        pltpu.make_async_copy(new_ref.at[:, :feature], query_ref, sems.at[0]),
        pltpu.make_async_copy(new_ref.at[:, feature : 2 * feature], key_ref, sems.at[1]),
        pltpu.make_async_copy(parents_hbm_ref, parents_ref, sems.at[2]),
    ]
    for copy in copies:
        copy.start()
    slicing.start()
    half = rows // 2
    beams = parents_ref.shape[1]
    order = class_order(rows, lax.axis_index("utt"))
    for copy in copies:
        copy.wait()
    query = query_ref[...]
    product = query.astype(jnp.float32) * key_ref[...].astype(jnp.float32)
    lane = lax.broadcasted_iota(jnp.int32, (rows, LANES), 1)
    heads = feature // HD
    at_parent_lane = lax.broadcasted_iota(jnp.int32, (beams, LANES), 0) + PARENT_LANE
    at_parent_lane = at_parent_lane == lax.broadcasted_iota(jnp.int32, (beams, LANES), 1)
    extra = jnp.dot(
        jnp.broadcast_to(parents_ref[...], (rows, beams)).astype(jnp.bfloat16),
        at_parent_lane.astype(jnp.bfloat16),
        preferred_element_type=jnp.float32,
    )
    for head in range(heads):
        own = jnp.sum(product[:, head * HD : (head + 1) * HD], axis=1, keepdims=True) * HD ** (-0.5)
        for part in range(3):
            term = own.astype(jnp.bfloat16).astype(jnp.float32)
            extra = jnp.where(lane == part * heads + head, term, extra)
            own = own - term
    extra = extra.astype(jnp.bfloat16)
    for at in range(0, feature + LANES, LANES):
        tile = query[:, at : at + LANES] if at < feature else extra
        tile = jnp.dot(order, tile, preferred_element_type=jnp.float32)
        keep_ref[:, at : at + LANES] = tile[:half].astype(jnp.bfloat16)
        send_ref[:, at : at + LANES] = tile[half:].astype(jnp.bfloat16)
    slicing.wait()


def cross_weights_kernel(
    lengths_ref, query_hbm_ref, frames_ref, out_ref, query_ref, keys_ref, sems
):
    rows, feature = query_ref.shape
    copies = [
        pltpu.make_async_copy(frames_ref.at[:, :feature], keys_ref, sems.at[0]),
        pltpu.make_async_copy(query_hbm_ref, query_ref, sems.at[1]),
    ]
    for copy in copies:
        copy.start()
    for copy in copies:
        copy.wait()
    frames = keys_ref.shape[0]
    heads = feature // HD
    live = lax.broadcasted_iota(jnp.int32, (rows, frames), 1) < lengths_ref[:, :1]
    scores = []
    for head in range(heads):
        at = slice(head * HD, (head + 1) * HD)
        scores.append(
            lax.dot_general(
                query_ref[:, at], keys_ref[:, at], OVER_LAST, preferred_element_type=jnp.float32
            )
        )
    for head in range(heads):
        masked = jnp.where(live, scores[head] * HD ** (-0.5), MASKED)
        raised = jnp.where(live, jnp.exp(masked - jnp.max(masked, axis=1, keepdims=True)), 0.0)
        weights = raised / jnp.sum(raised, axis=1, keepdims=True)
        out_ref[head] = weights.astype(jnp.bfloat16)


def cross_values_kernel(weights_ref, frames_ref, out_ref, values_ref, sem):
    feature = values_ref.shape[1]
    copy = pltpu.make_async_copy(frames_ref.at[:, feature:], values_ref, sem)
    copy.start()
    copy.wait()
    for head in range(weights_ref.shape[0]):
        at = slice(head * HD, (head + 1) * HD)
        out_ref[:, at] = jnp.dot(
            weights_ref[head], values_ref[:, at], preferred_element_type=jnp.float32
        ).astype(jnp.bfloat16)


def cached(near_ref, far_ref, pair_near_ref, pair_far_ref, mine, at):
    pieces = [ref[part, mine, :, at] for ref in (near_ref, far_ref) for part in range(near_ref.shape[0])]
    return jnp.concatenate(pieces + [pair_near_ref[:, at], pair_far_ref[:, at]], axis=0)


def rows_of(masks, beams):
    return [mask ^ pair for mask in masks for pair in (0, PAIR)]


def self_weights_kernel(masks, counts, *refs):
    query_refs, refs = refs[:counts], refs[counts:]
    *cache_refs, weight_ref, share_ref, terms_ref, spread_ref = refs
    me = lax.axis_index("utt").astype(jnp.int32)
    mine = class_of(me)
    pair_keys, feature = cache_refs[-1].shape
    heads, rows, keys = weight_ref.shape
    beams = query_refs[0].shape[0]
    half_beams = beams // 2
    history = pair_keys // half_beams
    queries = jnp.concatenate([ref[...] for ref in query_refs], axis=0)
    extra = queries[:, feature:].astype(jnp.float32)

    utt = utt_of_rank(lax.broadcasted_iota(jnp.int32, (half_beams, LANES), 0), me)
    lane = lax.broadcasted_iota(jnp.int32, (half_beams, LANES), 1)
    table = jnp.zeros((half_beams, LANES), jnp.float32)
    for at, mask in enumerate(masks):
        lists = extra[at * beams : at * beams + half_beams]
        owner = me ^ mask
        table = jnp.where(utt == owner, lists, table)
        table = jnp.where(utt == (owner ^ CORE), pltpu.roll(lists, LANES - beams, 1), table)
    chosen = jnp.concatenate(
        [
            jnp.sum(
                jnp.where(lane == PARENT_LANE + (me ^ mask), table, 0.0), axis=1, keepdims=True
            )
            for mask in rows_of(masks, beams)
        ],
        axis=0,
    ).astype(jnp.int32)

    row_rank = lax.broadcasted_iota(jnp.int32, (rows, keys), 0) % half_beams
    key = lax.broadcasted_iota(jnp.int32, (rows, keys), 1)
    key_rank = key % pair_keys // history
    run = key // pair_keys
    owner = me ^ jnp.where(
        run == 0, 0, jnp.where(run == 1, CORE, jnp.where(run == 2, PAIR, PAIR ^ CORE))
    )
    live = (key_rank == row_rank) & (chosen == owner)
    group = CORE | PAIR
    row_live = (chosen // (group + 1)) == (me // (group + 1))

    tiles = [slice(at, at + LANES) for at in range(0, keys, LANES)]
    for head in range(heads):
        at = slice(head * HD, (head + 1) * HD)
        scores = lax.dot_general(
            queries[:, at], cached(*cache_refs, mine, at), OVER_LAST, preferred_element_type=jnp.float32
        )
        scores = jnp.where(live, scores, 0.0)
        rest = sum(scores[:, tile] for tile in tiles)
        for term_at in range(3):
            term = rest.astype(jnp.bfloat16)
            rest = rest - term.astype(jnp.float32)
            terms_ref[head * rows : (head + 1) * rows, term_at * LANES : (term_at + 1) * LANES] = term
    row_lane = lax.broadcasted_iota(jnp.int32, (rows, LANES), 1)
    fold = lax.broadcasted_iota(jnp.int32, (3 * LANES, LANES), 0) % history
    fold = fold == lax.broadcasted_iota(jnp.int32, (3 * LANES, LANES), 1) % history
    fold = fold.astype(jnp.bfloat16)
    folded = jnp.dot(terms_ref[...], fold, preferred_element_type=jnp.float32)
    packed = jnp.zeros((rows, LANES), jnp.float32)
    for head in range(heads):
        packed = jnp.where(
            row_lane // history == head, folded[head * rows : (head + 1) * rows], packed
        )
    packed = packed * HD ** (-0.5)
    part = lax.broadcasted_iota(jnp.int32, (LANES, LANES), 0)
    spread = lax.broadcasted_iota(jnp.int32, (LANES, LANES), 1) // history
    spread = (part < 3 * heads) & (part % heads == spread)
    own = jnp.dot(
        queries[:, feature:], spread.astype(jnp.bfloat16), preferred_element_type=jnp.float32
    )

    def over_tokens(tile, combine):
        step = 1
        while step < history:
            left = pltpu.roll(tile, step, 1)
            right = pltpu.roll(tile, LANES - step, 1)
            tile = combine(tile, jnp.where(row_lane // step % 2 == 0, right, left))
            step = 2 * step
        return tile

    peak = jnp.maximum(over_tokens(packed, jnp.maximum), own)
    raised = jnp.exp(packed - peak)
    own = jnp.exp(own - peak)
    share = 1.0 / (over_tokens(raised, jnp.add) + own)
    share_ref[...] = jnp.where(row_live, own * share, 0.0).astype(jnp.bfloat16)
    packed = (raised * share).astype(jnp.bfloat16)
    for head in range(heads):
        spread_ref[head * rows : (head + 1) * rows] = jnp.where(
            row_lane // history == head, packed, jnp.zeros_like(packed)
        )
    weights = jnp.dot(spread_ref[...], fold[:LANES], preferred_element_type=jnp.float32)
    for head in range(heads):
        for tile in tiles:
            weight_ref[head, :, tile] = jnp.where(
                live[:, tile], weights[head * rows : (head + 1) * rows], 0.0
            ).astype(jnp.bfloat16)


def self_values_kernel(masks, *refs):
    out_refs = refs[-len(masks) :]
    weight_ref, share_ref, *cache_refs, cross_near_ref, cross_far_ref = refs[: -len(masks)]
    me = lax.axis_index("utt").astype(jnp.int32)
    mine = class_of(me)
    heads, rows, _ = weight_ref.shape
    feature = heads * HD
    beams = cross_near_ref.shape[0]
    blocks = [slice(at * beams, (at + 1) * beams) for at in (masks.index(m) for m in sorted(masks))]
    half_beams = beams // 2
    for out_ref, block in zip(out_refs, blocks):
        out_ref[:, feature:] = share_ref[block]

    place = lax.broadcasted_iota(jnp.int32, (rows, beams), 1)
    pick_utt = utt_of_rank(lax.broadcasted_iota(jnp.int32, (rows, beams), 0) % half_beams, me)
    row_beam = me ^ jnp.concatenate(
        [jnp.full((half_beams, beams), mask, jnp.int32) for mask in rows_of(masks, beams)], axis=0
    )
    near_pick = ((place == row_beam) & (pick_utt == me)).astype(jnp.bfloat16)
    far_pick = ((place == row_beam) & (pick_utt == (me ^ CORE))).astype(jnp.bfloat16)
    pick = jnp.concatenate([near_pick, far_pick], axis=1)
    for head in range(heads):
        at = slice(head * HD, (head + 1) * HD)
        out = jnp.dot(
            weight_ref[head], cached(*cache_refs, mine, at), preferred_element_type=jnp.float32
        )
        cross = jnp.concatenate([cross_near_ref[:, at], cross_far_ref[:, at]], axis=0)
        out = out + jnp.dot(pick, cross, preferred_element_type=jnp.float32)
        out = out.astype(jnp.bfloat16)
        for out_ref, block in zip(out_refs, blocks):
            out_ref[:, at] = out[block]


def finish_kernel(history, mine_ref, came_ref, value_ref, out_ref):
    rows, feature = out_ref.shape
    order = class_order(rows, lax.axis_index("utt"))

    def ordered(at):
        tile = jnp.concatenate(
            [mine_ref[:, at].astype(jnp.float32), came_ref[:, at].astype(jnp.float32)], axis=0
        ).astype(jnp.bfloat16)
        return lax.dot_general(
            order, tile, (((0,), (0,)), ((), ())), preferred_element_type=jnp.float32
        )

    shares = ordered(slice(feature, feature + LANES))
    for head in range(feature // HD):
        at = slice(head * HD, (head + 1) * HD)
        out = ordered(at) + shares[:, head * history : head * history + 1] * value_ref[:, at].astype(jnp.float32)
        out_ref[:, at] = out.astype(jnp.bfloat16)


def whole(shape):
    return pl.BlockSpec(shape, lambda *_: (0,) * len(shape))


def body_by_parent(devices, cache_kv, new_rows, cross_queries, enc_kv, lengths, parents):
    beams = parents.shape[1]
    rows, feature = cross_queries.shape
    frames = enc_kv.shape[1]
    history = cache_kv.shape[1]
    heads = feature // HD
    width = feature + LANES
    keys = beams * history
    me = lax.axis_index("utt").astype(jnp.int32)
    params = pltpu.CompilerParams(vmem_limit_bytes=16 * 1024 * 1024)

    def swap(array, bits):
        return lax.ppermute(array, "utt", [(i, i ^ bits) for i in range(devices)])

    def after(array, *others):
        return lax.optimization_barrier((array,) + others)[0]

    def in_hbm(array):
        return pltpu.with_memory_space_constraint(array, pltpu.HBM)

    hops = [(1 << k) | CORE for k in range(devices.bit_length() - 2, 1, -1)]

    near = cache_kv.reshape(beams // (2 * CLASS), 2, CLASS * history, 2 * feature)
    half_rows = jax.ShapeDtypeStruct((rows // 2, width), jnp.bfloat16)
    half_cache = jax.ShapeDtypeStruct(near.shape[:1] + near.shape[2:], jnp.bfloat16)
    own, other, other_cache = pl.pallas_call(
        pack_kernel,
        out_shape=(half_rows, half_rows, half_cache),
        in_specs=[pl.BlockSpec(memory_space=pltpu.HBM)] * 3,
        out_specs=(whole(half_rows.shape), whole(half_rows.shape), whole(half_cache.shape)),
        scratch_shapes=[
            pltpu.VMEM((rows, feature), jnp.bfloat16),
            pltpu.VMEM((rows, feature), jnp.bfloat16),
            pltpu.VMEM(parents.shape, jnp.int32),
            pltpu.SemaphoreType.DMA((4,)),
        ],
        compiler_params=params,
    )(
        in_hbm(new_rows),
        in_hbm(parents),
        in_hbm(near),
    )
    pair_rows = swap(other, PAIR)
    far = swap(near, CORE)
    pair_near = swap(other_cache, PAIR).reshape(keys // 2, 2 * feature)

    lists = jnp.pad(
        swap(after(parents, other), CORE).astype(jnp.bfloat16),
        ((0, 0), (feature + PARENT_LANE + beams, LANES - PARENT_LANE - 2 * beams)),
    )
    frame_count = jnp.broadcast_to(lengths.reshape(1, 1), (1, LANES))
    held = after(jnp.concatenate([own + lists, pair_rows], axis=0), frame_count)
    gathered, masks, held_masks = [held], [0], [0]

    frames_kv = in_hbm(enc_kv.reshape(frames, 2 * feature))
    cross_weights = pl.pallas_call(
        cross_weights_kernel,
        out_shape=jax.ShapeDtypeStruct((heads, rows, frames), jnp.bfloat16),
        in_specs=[whole((1, LANES))] + [pl.BlockSpec(memory_space=pltpu.HBM)] * 2,
        out_specs=whole((heads, rows, frames)),
        scratch_shapes=[
            pltpu.VMEM((rows, feature), jnp.bfloat16),
            pltpu.VMEM((frames, feature), jnp.bfloat16),
            pltpu.SemaphoreType.DMA((2,)),
        ],
        compiler_params=params,
    )(frame_count, in_hbm(after(cross_queries, held)), frames_kv)
    for bits in hops:
        came = swap(held, bits)
        gathered.append(came)
        masks = masks + [mask ^ bits for mask in held_masks]
        held_masks = masks
        if bits != hops[-1]:
            held = after(jnp.concatenate([held, came], axis=0), cross_weights)

    cross_near = pl.pallas_call(
        cross_values_kernel,
        out_shape=jax.ShapeDtypeStruct((rows, feature), jnp.bfloat16),
        grid=(1,),
        in_specs=[whole((heads, rows, frames)), pl.BlockSpec(memory_space=pltpu.HBM)],
        out_specs=whole((rows, feature)),
        scratch_shapes=[
            pltpu.VMEM((frames, feature), jnp.bfloat16),
            pltpu.SemaphoreType.DMA(()),
        ],
        compiler_params=params,
    )(after(cross_weights, held), frames_kv)
    cross_far = swap(cross_near, CORE)

    pair_keys, pair_values = pair_near[:, :feature], pair_near[:, feature:]
    pair_far_keys = swap(after(pair_keys, held), CORE)
    pair_far_values = swap(after(pair_values, gathered[-1], cross_near), CORE)

    all_rows = rows * len(masks)
    weight_shape = jax.ShapeDtypeStruct((heads, all_rows, 2 * keys), jnp.bfloat16)
    share_shape = jax.ShapeDtypeStruct((all_rows, LANES), jnp.bfloat16)
    part = jax.ShapeDtypeStruct((rows, width), jnp.bfloat16)
    near_shape = near.shape[:3] + (feature,)
    in_keys = pl.BlockSpec(near_shape, lambda i: (0, 0, 0, 0))
    in_values = pl.BlockSpec(near_shape, lambda i: (0, 0, 0, 1))
    pair_spec = whole(pair_keys.shape)
    weights, shares = pl.pallas_call(
        functools.partial(self_weights_kernel, tuple(masks), len(gathered)),
        out_shape=(weight_shape, share_shape),
        grid=(1,),
        in_specs=[whole(block.shape) for block in gathered]
        + [in_keys, in_keys, pair_spec, pair_spec],
        out_specs=(whole(weight_shape.shape), whole(share_shape.shape)),
        scratch_shapes=[
            pltpu.VMEM((heads * all_rows, 3 * LANES), jnp.bfloat16),
            pltpu.VMEM((heads * all_rows, LANES), jnp.bfloat16),
        ],
        compiler_params=params,
    )(*gathered, near, far, pair_keys, pair_far_keys)
    parts = pl.pallas_call(
        functools.partial(self_values_kernel, tuple(masks)),
        out_shape=(part,) * len(masks),
        grid=(1,),
        in_specs=[whole(weights.shape), whole(shares.shape)]
        + [in_values, in_values, pair_spec, pair_spec]
        + [whole((rows, feature))] * 2,
        out_specs=(whole(part.shape),) * len(masks),
        compiler_params=params,
    )(weights, shares, near, far, pair_values, pair_far_values, cross_near, cross_far)

    mixed = parts[0]
    for mask, part in zip(sorted(masks)[1:], parts[1:]):
        mixed = mixed + swap(part, mask)
    keep = mixed[: rows // 2]
    came = swap(mixed[rows // 2 :], PAIR)

    return pl.pallas_call(
        functools.partial(finish_kernel, history),
        out_shape=jax.ShapeDtypeStruct((rows, feature), jnp.bfloat16),
        grid=(1,),
        in_specs=[
            whole(half_rows.shape),
            whole(half_rows.shape),
            pl.BlockSpec((rows, feature), lambda i: (0, 2)),
        ],
        out_specs=whole((rows, feature)),
        compiler_params=params,
    )(keep, came, new_rows)


def solution(mesh):
    placed = (
        P(("groups", "utt"), None, None),
        P(("groups", "utt"), None),
        P(("groups", "utt"), None),
        P(("groups", "utt"), None, None),
        P(("groups", "utt")),
        P(("groups", "utt"), None),
    )
    devices = mesh.shape["utt"]

    def body(cache_kv, new_rows, cross_queries, enc_kv, lengths, parents):
        beams = parents.shape[1]
        heads = cross_queries.shape[1] // HD
        history = cache_kv.shape[1]
        fits = (
            parents.shape[0] == 1
            and devices == beams
            and devices >= 8
            and devices & (devices - 1) == 0
            and beams % 16 == 0
            and history & (history - 1) == 0
            and heads * history <= LANES
            and 3 * heads <= PARENT_LANE
            and PARENT_LANE + 2 * beams <= LANES
        )
        plan = functools.partial(body_by_parent, devices) if fits else body_by_utterance
        return plan(cache_kv, new_rows, cross_queries, enc_kv, lengths, parents)

    return jax.shard_map(
        body, mesh=mesh, in_specs=placed, out_specs=P(("groups", "utt"), None), check_vma=False
    )
```

```python
import functools

import jax
import jax.numpy as jnp
from jax import lax
from jax.experimental import pallas as pl
from jax.experimental.pallas import tpu as pltpu
from jax.sharding import PartitionSpec as P

HD = 128
LANES = 128
PARENT_LANE = 64
MASKED = -1e30


def reorder(cache_rows, parents):
    utterances, beam_width = parents.shape
    grouped = cache_rows.reshape(utterances, beam_width, cache_rows.shape[1], cache_rows.shape[2])
    picked = jax.vmap(lambda block, picks: block[picks])(grouped, parents)
    return picked.reshape(cache_rows.shape)


def attend_self(query, old_keys, old_values, new_key, new_value):
    row_count = query.shape[0]
    history = old_keys.shape[1]
    head_count = query.shape[1] // HD
    scale = HD ** (-0.5)
    query_heads = query.reshape(row_count, head_count, HD)
    key_heads = old_keys.reshape(row_count, history, head_count, HD)
    value_heads = old_values.reshape(row_count, history, head_count, HD)
    old_scores = (
        jnp.einsum("rhd,rthd->rht", query_heads, key_heads, preferred_element_type=jnp.float32)
        * scale
    )
    own_score = (
        jnp.einsum(
            "rhd,rhd->rh",
            query_heads,
            new_key.reshape(row_count, head_count, HD),
            preferred_element_type=jnp.float32,
        )
        * scale
    )
    peak = jnp.maximum(jnp.max(old_scores, axis=2), own_score)
    old_exp = jnp.exp(old_scores - peak[:, :, None])
    own_exp = jnp.exp(own_score - peak)
    total = jnp.sum(old_exp, axis=2) + own_exp
    old_weight = (old_exp / total[:, :, None]).astype(jnp.bfloat16)
    own_weight = (own_exp / total).astype(jnp.bfloat16)
    context = jnp.einsum(
        "rht,rthd->rhd", old_weight, value_heads, preferred_element_type=jnp.float32
    )
    context = context + own_weight.astype(jnp.float32)[:, :, None] * new_value.reshape(
        row_count, head_count, HD
    ).astype(jnp.float32)
    return context.reshape(row_count, head_count * HD).astype(jnp.bfloat16)


def attend_frames(queries, frames_kv, frame_counts):
    utterances = frame_counts.shape[0]
    beam_width = queries.shape[0] // utterances
    feature = queries.shape[1]
    head_count = feature // HD
    frame_total = frames_kv.shape[1]
    scale = HD ** (-0.5)
    query_heads = queries.reshape(utterances, beam_width, head_count, HD)
    key_heads = frames_kv[:, :, :feature].reshape(utterances, frame_total, head_count, HD)
    value_heads = frames_kv[:, :, feature:].reshape(utterances, frame_total, head_count, HD)
    scores = (
        jnp.einsum("ubhd,ufhd->uhbf", query_heads, key_heads, preferred_element_type=jnp.float32)
        * scale
    )
    live = (
        lax.broadcasted_iota(jnp.int32, (utterances, 1, 1, frame_total), 3)
        < frame_counts[:, None, None, None]
    )
    scores = jnp.where(live, scores, -1e30)
    peak = jnp.max(scores, axis=3, keepdims=True)
    raised = jnp.where(live, jnp.exp(scores - peak), 0.0)
    weights = (raised / jnp.sum(raised, axis=3, keepdims=True)).astype(jnp.bfloat16)
    context = jnp.einsum(
        "uhbf,ufhd->ubhd", weights, value_heads, preferred_element_type=jnp.float32
    )
    return context.reshape(utterances * beam_width, feature)


def body_by_utterance(cache_kv, new_rows, cross_queries, enc_kv, lengths, parents):
    feature = cross_queries.shape[1]
    cross_context = attend_frames(cross_queries, enc_kv, lengths)
    arrived, new_here = (
        lax.all_to_all(cache_kv, "utt", split_axis=0, concat_axis=0, tiled=True),
        lax.all_to_all(new_rows, "utt", split_axis=0, concat_axis=0, tiled=True),
    )
    reordered = reorder(arrived, parents)
    self_context = attend_self(
        new_here[:, :feature],
        reordered[:, :, :feature],
        reordered[:, :, feature:],
        new_here[:, feature : 2 * feature],
        new_here[:, 2 * feature :],
    )
    mixed_here = (self_context.astype(jnp.float32) + cross_context).astype(jnp.bfloat16)
    mixed = lax.all_to_all(mixed_here, "utt", split_axis=0, concat_axis=0, tiled=True)
    return mixed


CORE = 1
CLASS = 2
PAIR = CLASS | CORE
OVER_LAST = (((1,), (1,)), ((), ()))


def class_of(index):
    return (index // CLASS) % 2


def rank_in_class(utt):
    return utt // (2 * CLASS) * CLASS + utt % CLASS


def utt_of_rank(rank, device):
    return rank // CLASS * (2 * CLASS) + class_of(device) * CLASS + rank % CLASS


def class_order(beams, device):
    row = lax.broadcasted_iota(jnp.int32, (beams, beams), 0)
    col = lax.broadcasted_iota(jnp.int32, (beams, beams), 1)
    half = beams // 2
    place = rank_in_class(col) + jnp.where(class_of(col) == class_of(device), 0, half)
    return (row == place).astype(jnp.bfloat16)


def pack_kernel(
    new_ref,
    parents_hbm_ref,
    cache_ref,
    keep_ref,
    send_ref,
    keys_ref,
    values_ref,
    query_ref,
    key_ref,
    parents_ref,
    sems,
):
    rows, feature = query_ref.shape
    other = 1 - class_of(lax.axis_index("utt").astype(jnp.int32))
    slicing = [
        pltpu.make_async_copy(cache_ref.at[:, other, :, :feature], keys_ref, sems.at[3]),
        pltpu.make_async_copy(cache_ref.at[:, other, :, feature:], values_ref, sems.at[4]),
    ]
    copies = [
        pltpu.make_async_copy(new_ref.at[:, :feature], query_ref, sems.at[0]),
        pltpu.make_async_copy(new_ref.at[:, feature : 2 * feature], key_ref, sems.at[1]),
        pltpu.make_async_copy(parents_hbm_ref, parents_ref, sems.at[2]),
    ]
    for copy in copies + slicing:
        copy.start()
    half = rows // 2
    beams = parents_ref.shape[1]
    order = class_order(rows, lax.axis_index("utt"))
    for copy in copies:
        copy.wait()
    query = query_ref[...]
    product = query.astype(jnp.float32) * key_ref[...].astype(jnp.float32)
    lane = lax.broadcasted_iota(jnp.int32, (rows, LANES), 1)
    heads = feature // HD
    at_parent_lane = lax.broadcasted_iota(jnp.int32, (beams, LANES), 0) + PARENT_LANE
    at_parent_lane = at_parent_lane == lax.broadcasted_iota(jnp.int32, (beams, LANES), 1)
    extra = jnp.dot(
        jnp.broadcast_to(parents_ref[...], (rows, beams)).astype(jnp.bfloat16),
        at_parent_lane.astype(jnp.bfloat16),
        preferred_element_type=jnp.float32,
    )
    for head in range(heads):
        own = jnp.sum(product[:, head * HD : (head + 1) * HD], axis=1, keepdims=True) * HD ** (-0.5)
        for part in range(3):
            term = own.astype(jnp.bfloat16).astype(jnp.float32)
            extra = jnp.where(lane == part * heads + head, term, extra)
            own = own - term
    extra = extra.astype(jnp.bfloat16)
    for at in range(0, feature + LANES, LANES):
        tile = query[:, at : at + LANES] if at < feature else extra
        tile = jnp.dot(order, tile, preferred_element_type=jnp.float32)
        keep_ref[:, at : at + LANES] = tile[:half].astype(jnp.bfloat16)
        send_ref[:, at : at + LANES] = tile[half:].astype(jnp.bfloat16)
    for copy in slicing:
        copy.wait()


def cross_weights_kernel(
    lengths_ref, query_hbm_ref, frames_ref, out_ref, query_ref, keys_ref, sems
):
    rows, feature = query_ref.shape
    copies = [
        pltpu.make_async_copy(frames_ref.at[:, :feature], keys_ref, sems.at[0]),
        pltpu.make_async_copy(query_hbm_ref, query_ref, sems.at[1]),
    ]
    for copy in copies:
        copy.start()
    for copy in copies:
        copy.wait()
    frames = keys_ref.shape[0]
    heads = feature // HD
    live = lax.broadcasted_iota(jnp.int32, (rows, frames), 1) < lengths_ref[:, :1]
    scores = []
    for head in range(heads):
        at = slice(head * HD, (head + 1) * HD)
        scores.append(
            lax.dot_general(
                query_ref[:, at], keys_ref[:, at], OVER_LAST, preferred_element_type=jnp.float32
            )
        )
    for head in range(heads):
        masked = jnp.where(live, scores[head] * HD ** (-0.5), MASKED)
        raised = jnp.where(live, jnp.exp(masked - jnp.max(masked, axis=1, keepdims=True)), 0.0)
        weights = raised / jnp.sum(raised, axis=1, keepdims=True)
        out_ref[head] = weights.astype(jnp.bfloat16)


def cross_values_kernel(weights_ref, frames_ref, out_ref, values_ref, sem):
    feature = values_ref.shape[1]
    copy = pltpu.make_async_copy(frames_ref.at[:, feature:], values_ref, sem)
    copy.start()
    copy.wait()
    for head in range(weights_ref.shape[0]):
        at = slice(head * HD, (head + 1) * HD)
        out_ref[:, at] = jnp.dot(
            weights_ref[head], values_ref[:, at], preferred_element_type=jnp.float32
        ).astype(jnp.bfloat16)


def cached(near_ref, far_ref, pair_near_ref, pair_far_ref, mine, at):
    pieces = [ref[part, mine, :, at] for ref in (near_ref, far_ref) for part in range(near_ref.shape[0])]
    return jnp.concatenate(pieces + [pair_near_ref[:, at], pair_far_ref[:, at]], axis=0)


def rows_of(masks, beams):
    return [mask ^ pair for mask in masks for pair in (0, PAIR)]


def self_weights_kernel(masks, counts, *refs):
    query_refs, refs = refs[:counts], refs[counts:]
    *cache_refs, weight_ref, share_ref, terms_ref, spread_ref = refs
    me = lax.axis_index("utt").astype(jnp.int32)
    mine = class_of(me)
    pair_keys, feature = cache_refs[-1].shape
    heads, rows, keys = weight_ref.shape
    beams = query_refs[0].shape[0]
    half_beams = beams // 2
    history = pair_keys // half_beams
    queries = jnp.concatenate([ref[...] for ref in query_refs], axis=0)
    extra = queries[:, feature:].astype(jnp.float32)

    utt = utt_of_rank(lax.broadcasted_iota(jnp.int32, (half_beams, LANES), 0), me)
    lane = lax.broadcasted_iota(jnp.int32, (half_beams, LANES), 1)
    table = jnp.zeros((half_beams, LANES), jnp.float32)
    for at, mask in enumerate(masks):
        lists = extra[at * beams : at * beams + half_beams]
        owner = me ^ mask
        table = jnp.where(utt == owner, lists, table)
        table = jnp.where(utt == (owner ^ CORE), pltpu.roll(lists, LANES - beams, 1), table)
    chosen = jnp.concatenate(
        [
            jnp.sum(
                jnp.where(lane == PARENT_LANE + (me ^ mask), table, 0.0), axis=1, keepdims=True
            )
            for mask in rows_of(masks, beams)
        ],
        axis=0,
    ).astype(jnp.int32)

    row_rank = lax.broadcasted_iota(jnp.int32, (rows, keys), 0) % half_beams
    key = lax.broadcasted_iota(jnp.int32, (rows, keys), 1)
    key_rank = key % pair_keys // history
    run = key // pair_keys
    owner = me ^ jnp.where(
        run == 0, 0, jnp.where(run == 1, CORE, jnp.where(run == 2, PAIR, PAIR ^ CORE))
    )
    live = (key_rank == row_rank) & (chosen == owner)
    group = CORE | PAIR
    row_live = (chosen // (group + 1)) == (me // (group + 1))

    tiles = [slice(at, at + LANES) for at in range(0, keys, LANES)]
    for head in range(heads):
        at = slice(head * HD, (head + 1) * HD)
        scores = lax.dot_general(
            queries[:, at], cached(*cache_refs, mine, at), OVER_LAST, preferred_element_type=jnp.float32
        )
        scores = jnp.where(live, scores, 0.0)
        rest = sum(scores[:, tile] for tile in tiles)
        for term_at in range(3):
            term = rest.astype(jnp.bfloat16)
            rest = rest - term.astype(jnp.float32)
            terms_ref[head * rows : (head + 1) * rows, term_at * LANES : (term_at + 1) * LANES] = term
    row_lane = lax.broadcasted_iota(jnp.int32, (rows, LANES), 1)
    fold = lax.broadcasted_iota(jnp.int32, (3 * LANES, LANES), 0) % history
    fold = fold == lax.broadcasted_iota(jnp.int32, (3 * LANES, LANES), 1) % history
    fold = fold.astype(jnp.bfloat16)
    folded = jnp.dot(terms_ref[...], fold, preferred_element_type=jnp.float32)
    packed = jnp.zeros((rows, LANES), jnp.float32)
    for head in range(heads):
        packed = jnp.where(
            row_lane // history == head, folded[head * rows : (head + 1) * rows], packed
        )
    packed = packed * HD ** (-0.5)
    part = lax.broadcasted_iota(jnp.int32, (LANES, LANES), 0)
    spread = lax.broadcasted_iota(jnp.int32, (LANES, LANES), 1) // history
    spread = (part < 3 * heads) & (part % heads == spread)
    own = jnp.dot(
        queries[:, feature:], spread.astype(jnp.bfloat16), preferred_element_type=jnp.float32
    )

    def over_tokens(tile, combine):
        step = 1
        while step < history:
            left = pltpu.roll(tile, step, 1)
            right = pltpu.roll(tile, LANES - step, 1)
            tile = combine(tile, jnp.where(row_lane // step % 2 == 0, right, left))
            step = 2 * step
        return tile

    peak = jnp.maximum(over_tokens(packed, jnp.maximum), own)
    raised = jnp.exp(packed - peak)
    own = jnp.exp(own - peak)
    share = 1.0 / (over_tokens(raised, jnp.add) + own)
    share_ref[...] = jnp.where(row_live, own * share, 0.0).astype(jnp.bfloat16)
    packed = (raised * share).astype(jnp.bfloat16)
    for head in range(heads):
        spread_ref[head * rows : (head + 1) * rows] = jnp.where(
            row_lane // history == head, packed, jnp.zeros_like(packed)
        )
    weights = jnp.dot(spread_ref[...], fold[:LANES], preferred_element_type=jnp.float32)
    for head in range(heads):
        for tile in tiles:
            weight_ref[head, :, tile] = jnp.where(
                live[:, tile], weights[head * rows : (head + 1) * rows], 0.0
            ).astype(jnp.bfloat16)


def self_values_kernel(masks, *refs):
    out_refs = refs[-len(masks) :]
    weight_ref, share_ref, *cache_refs, cross_near_ref, cross_far_ref = refs[: -len(masks)]
    me = lax.axis_index("utt").astype(jnp.int32)
    mine = class_of(me)
    heads, rows, _ = weight_ref.shape
    feature = heads * HD
    beams = cross_near_ref.shape[0]
    blocks = [slice(at * beams, (at + 1) * beams) for at in (masks.index(m) for m in sorted(masks))]
    half_beams = beams // 2
    for out_ref, block in zip(out_refs, blocks):
        out_ref[:, feature:] = share_ref[block]

    place = lax.broadcasted_iota(jnp.int32, (rows, beams), 1)
    pick_utt = utt_of_rank(lax.broadcasted_iota(jnp.int32, (rows, beams), 0) % half_beams, me)
    row_beam = me ^ jnp.concatenate(
        [jnp.full((half_beams, beams), mask, jnp.int32) for mask in rows_of(masks, beams)], axis=0
    )
    near_pick = ((place == row_beam) & (pick_utt == me)).astype(jnp.bfloat16)
    far_pick = ((place == row_beam) & (pick_utt == (me ^ CORE))).astype(jnp.bfloat16)
    pick = jnp.concatenate([near_pick, far_pick], axis=1)
    for head in range(heads):
        at = slice(head * HD, (head + 1) * HD)
        out = jnp.dot(
            weight_ref[head], cached(*cache_refs, mine, at), preferred_element_type=jnp.float32
        )
        cross = jnp.concatenate([cross_near_ref[:, at], cross_far_ref[:, at]], axis=0)
        out = out + jnp.dot(pick, cross, preferred_element_type=jnp.float32)
        out = out.astype(jnp.bfloat16)
        for out_ref, block in zip(out_refs, blocks):
            out_ref[:, at] = out[block]


def finish_kernel(history, mine_ref, came_ref, value_ref, out_ref):
    rows, feature = out_ref.shape
    order = class_order(rows, lax.axis_index("utt"))

    def ordered(at):
        tile = jnp.concatenate(
            [mine_ref[:, at].astype(jnp.float32), came_ref[:, at].astype(jnp.float32)], axis=0
        ).astype(jnp.bfloat16)
        return lax.dot_general(
            order, tile, (((0,), (0,)), ((), ())), preferred_element_type=jnp.float32
        )

    shares = ordered(slice(feature, feature + LANES))
    for head in range(feature // HD):
        at = slice(head * HD, (head + 1) * HD)
        out = ordered(at) + shares[:, head * history : head * history + 1] * value_ref[:, at].astype(jnp.float32)
        out_ref[:, at] = out.astype(jnp.bfloat16)


def whole(shape):
    return pl.BlockSpec(shape, lambda *_: (0,) * len(shape))


def body_by_parent(devices, cache_kv, new_rows, cross_queries, enc_kv, lengths, parents):
    beams = parents.shape[1]
    rows, feature = cross_queries.shape
    frames = enc_kv.shape[1]
    history = cache_kv.shape[1]
    heads = feature // HD
    width = feature + LANES
    keys = beams * history
    me = lax.axis_index("utt").astype(jnp.int32)
    params = pltpu.CompilerParams(vmem_limit_bytes=16 * 1024 * 1024)

    def swap(array, bits):
        return lax.ppermute(array, "utt", [(i, i ^ bits) for i in range(devices)])

    def after(array, *others):
        return lax.optimization_barrier((array,) + others)[0]

    def in_hbm(array):
        return pltpu.with_memory_space_constraint(array, pltpu.HBM)

    hops = [(1 << k) | CORE for k in range(devices.bit_length() - 2, 1, -1)]

    near = cache_kv.reshape(beams // (2 * CLASS), 2, CLASS * history, 2 * feature)
    half_rows = jax.ShapeDtypeStruct((rows // 2, width), jnp.bfloat16)
    half_cache = jax.ShapeDtypeStruct(near.shape[:1] + near.shape[2:3] + (feature,), jnp.bfloat16)
    own, other, other_keys, other_values = pl.pallas_call(
        pack_kernel,
        out_shape=(half_rows, half_rows, half_cache, half_cache),
        in_specs=[pl.BlockSpec(memory_space=pltpu.HBM)] * 3,
        out_specs=(whole(half_rows.shape),) * 2 + (whole(half_cache.shape),) * 2,
        scratch_shapes=[
            pltpu.VMEM((rows, feature), jnp.bfloat16),
            pltpu.VMEM((rows, feature), jnp.bfloat16),
            pltpu.VMEM(parents.shape, jnp.int32),
            pltpu.SemaphoreType.DMA((5,)),
        ],
        compiler_params=params,
    )(
        in_hbm(new_rows),
        in_hbm(parents),
        in_hbm(near),
    )
    pair_rows = swap(other, PAIR)
    pair_keys = swap(other_keys, PAIR).reshape(keys // 2, feature)
    pair_values = swap(other_values, PAIR).reshape(keys // 2, feature)

    lists = jnp.pad(
        swap(after(parents, other), CORE).astype(jnp.bfloat16),
        ((0, 0), (feature + PARENT_LANE + beams, LANES - PARENT_LANE - 2 * beams)),
    )
    frame_count = jnp.broadcast_to(lengths.reshape(1, 1), (1, LANES))
    held = after(jnp.concatenate([own + lists, pair_rows], axis=0), frame_count)

    frames_kv = in_hbm(enc_kv.reshape(frames, 2 * feature))
    cross_weights = pl.pallas_call(
        cross_weights_kernel,
        out_shape=jax.ShapeDtypeStruct((heads, rows, frames), jnp.bfloat16),
        in_specs=[whole((1, LANES))] + [pl.BlockSpec(memory_space=pltpu.HBM)] * 2,
        out_specs=whole((heads, rows, frames)),
        scratch_shapes=[
            pltpu.VMEM((rows, feature), jnp.bfloat16),
            pltpu.VMEM((frames, feature), jnp.bfloat16),
            pltpu.SemaphoreType.DMA((2,)),
        ],
        compiler_params=params,
    )(frame_count, in_hbm(after(cross_queries, held)), frames_kv)
    far = swap(after(near, other), CORE)
    blocks = {0: held}
    for bits in hops:
        for mask, block in list(blocks.items()):
            blocks[mask ^ bits] = swap(after(block, cross_weights) if mask else block, bits)
    masks, gathered = list(blocks), list(blocks.values())

    cross_near = pl.pallas_call(
        cross_values_kernel,
        out_shape=jax.ShapeDtypeStruct((rows, feature), jnp.bfloat16),
        grid=(1,),
        in_specs=[whole((heads, rows, frames)), pl.BlockSpec(memory_space=pltpu.HBM)],
        out_specs=whole((rows, feature)),
        scratch_shapes=[
            pltpu.VMEM((frames, feature), jnp.bfloat16),
            pltpu.SemaphoreType.DMA(()),
        ],
        compiler_params=params,
    )(after(cross_weights, *gathered[:-1]), frames_kv)
    cross_far = swap(cross_near, CORE)

    pair_far_keys = swap(after(pair_keys, blocks[hops[0]]), CORE)
    pair_far_values = swap(after(pair_values, gathered[-1], cross_near), CORE)

    all_rows = rows * len(masks)
    weight_shape = jax.ShapeDtypeStruct((heads, all_rows, 2 * keys), jnp.bfloat16)
    share_shape = jax.ShapeDtypeStruct((all_rows, LANES), jnp.bfloat16)
    part = jax.ShapeDtypeStruct((rows, width), jnp.bfloat16)
    near_shape = near.shape[:3] + (feature,)
    in_keys = pl.BlockSpec(near_shape, lambda i: (0, 0, 0, 0))
    in_values = pl.BlockSpec(near_shape, lambda i: (0, 0, 0, 1))
    pair_spec = whole(pair_keys.shape)
    weights, shares = pl.pallas_call(
        functools.partial(self_weights_kernel, tuple(masks), len(gathered)),
        out_shape=(weight_shape, share_shape),
        grid=(1,),
        in_specs=[whole(block.shape) for block in gathered]
        + [in_keys, in_keys, pair_spec, pair_spec],
        out_specs=(whole(weight_shape.shape), whole(share_shape.shape)),
        scratch_shapes=[
            pltpu.VMEM((heads * all_rows, 3 * LANES), jnp.bfloat16),
            pltpu.VMEM((heads * all_rows, LANES), jnp.bfloat16),
        ],
        compiler_params=params,
    )(*gathered, near, far, pair_keys, pair_far_keys)
    parts = pl.pallas_call(
        functools.partial(self_values_kernel, tuple(masks)),
        out_shape=(part,) * len(masks),
        grid=(1,),
        in_specs=[whole(weights.shape), whole(shares.shape)]
        + [in_values, in_values, pair_spec, pair_spec]
        + [whole((rows, feature))] * 2,
        out_specs=(whole(part.shape),) * len(masks),
        compiler_params=params,
    )(weights, shares, near, far, pair_values, pair_far_values, cross_near, cross_far)

    parts = dict(zip(sorted(masks), parts))
    for bits in hops[::-1]:
        for mask in sorted(parts, reverse=True):
            if mask ^ bits in parts and mask ^ bits < mask:
                parts[mask ^ bits] = parts[mask ^ bits] + swap(parts.pop(mask), bits)
    (mixed,) = parts.values()
    keep = mixed[: rows // 2]
    came = swap(mixed[rows // 2 :], PAIR)

    return pl.pallas_call(
        functools.partial(finish_kernel, history),
        out_shape=jax.ShapeDtypeStruct((rows, feature), jnp.bfloat16),
        grid=(1,),
        in_specs=[
            whole(half_rows.shape),
            whole(half_rows.shape),
            pl.BlockSpec((rows, feature), lambda i: (0, 2)),
        ],
        out_specs=whole((rows, feature)),
        compiler_params=params,
    )(keep, came, new_rows)


def solution(mesh):
    placed = (
        P(("groups", "utt"), None, None),
        P(("groups", "utt"), None),
        P(("groups", "utt"), None),
        P(("groups", "utt"), None, None),
        P(("groups", "utt")),
        P(("groups", "utt"), None),
    )
    devices = mesh.shape["utt"]

    def body(cache_kv, new_rows, cross_queries, enc_kv, lengths, parents):
        beams = parents.shape[1]
        heads = cross_queries.shape[1] // HD
        history = cache_kv.shape[1]
        fits = (
            parents.shape[0] == 1
            and devices == beams
            and devices >= 8
            and devices & (devices - 1) == 0
            and beams % 16 == 0
            and history & (history - 1) == 0
            and heads * history <= LANES
            and 3 * heads <= PARENT_LANE
            and PARENT_LANE + 2 * beams <= LANES
        )
        plan = functools.partial(body_by_parent, devices) if fits else body_by_utterance
        return plan(cache_kv, new_rows, cross_queries, enc_kv, lengths, parents)

    return jax.shard_map(
        body, mesh=mesh, in_specs=placed, out_specs=P(("groups", "utt"), None), check_vma=False
    )
```

```python
import functools

import jax
import jax.numpy as jnp
from jax import lax
from jax.experimental import pallas as pl
from jax.experimental.pallas import tpu as pltpu
from jax.sharding import PartitionSpec as P

HD = 128
LANES = 128
PARENT_LANE = 64
MASKED = -1e30


def reorder(cache_rows, parents):
    utterances, beam_width = parents.shape
    grouped = cache_rows.reshape(utterances, beam_width, cache_rows.shape[1], cache_rows.shape[2])
    picked = jax.vmap(lambda block, picks: block[picks])(grouped, parents)
    return picked.reshape(cache_rows.shape)


def attend_self(query, old_keys, old_values, new_key, new_value):
    row_count = query.shape[0]
    history = old_keys.shape[1]
    head_count = query.shape[1] // HD
    scale = HD ** (-0.5)
    query_heads = query.reshape(row_count, head_count, HD)
    key_heads = old_keys.reshape(row_count, history, head_count, HD)
    value_heads = old_values.reshape(row_count, history, head_count, HD)
    old_scores = (
        jnp.einsum("rhd,rthd->rht", query_heads, key_heads, preferred_element_type=jnp.float32)
        * scale
    )
    own_score = (
        jnp.einsum(
            "rhd,rhd->rh",
            query_heads,
            new_key.reshape(row_count, head_count, HD),
            preferred_element_type=jnp.float32,
        )
        * scale
    )
    peak = jnp.maximum(jnp.max(old_scores, axis=2), own_score)
    old_exp = jnp.exp(old_scores - peak[:, :, None])
    own_exp = jnp.exp(own_score - peak)
    total = jnp.sum(old_exp, axis=2) + own_exp
    old_weight = (old_exp / total[:, :, None]).astype(jnp.bfloat16)
    own_weight = (own_exp / total).astype(jnp.bfloat16)
    context = jnp.einsum(
        "rht,rthd->rhd", old_weight, value_heads, preferred_element_type=jnp.float32
    )
    context = context + own_weight.astype(jnp.float32)[:, :, None] * new_value.reshape(
        row_count, head_count, HD
    ).astype(jnp.float32)
    return context.reshape(row_count, head_count * HD).astype(jnp.bfloat16)


def attend_frames(queries, frames_kv, frame_counts):
    utterances = frame_counts.shape[0]
    beam_width = queries.shape[0] // utterances
    feature = queries.shape[1]
    head_count = feature // HD
    frame_total = frames_kv.shape[1]
    scale = HD ** (-0.5)
    query_heads = queries.reshape(utterances, beam_width, head_count, HD)
    key_heads = frames_kv[:, :, :feature].reshape(utterances, frame_total, head_count, HD)
    value_heads = frames_kv[:, :, feature:].reshape(utterances, frame_total, head_count, HD)
    scores = (
        jnp.einsum("ubhd,ufhd->uhbf", query_heads, key_heads, preferred_element_type=jnp.float32)
        * scale
    )
    live = (
        lax.broadcasted_iota(jnp.int32, (utterances, 1, 1, frame_total), 3)
        < frame_counts[:, None, None, None]
    )
    scores = jnp.where(live, scores, -1e30)
    peak = jnp.max(scores, axis=3, keepdims=True)
    raised = jnp.where(live, jnp.exp(scores - peak), 0.0)
    weights = (raised / jnp.sum(raised, axis=3, keepdims=True)).astype(jnp.bfloat16)
    context = jnp.einsum(
        "uhbf,ufhd->ubhd", weights, value_heads, preferred_element_type=jnp.float32
    )
    return context.reshape(utterances * beam_width, feature)


def body_by_utterance(cache_kv, new_rows, cross_queries, enc_kv, lengths, parents):
    feature = cross_queries.shape[1]
    cross_context = attend_frames(cross_queries, enc_kv, lengths)
    arrived, new_here = (
        lax.all_to_all(cache_kv, "utt", split_axis=0, concat_axis=0, tiled=True),
        lax.all_to_all(new_rows, "utt", split_axis=0, concat_axis=0, tiled=True),
    )
    reordered = reorder(arrived, parents)
    self_context = attend_self(
        new_here[:, :feature],
        reordered[:, :, :feature],
        reordered[:, :, feature:],
        new_here[:, feature : 2 * feature],
        new_here[:, 2 * feature :],
    )
    mixed_here = (self_context.astype(jnp.float32) + cross_context).astype(jnp.bfloat16)
    mixed = lax.all_to_all(mixed_here, "utt", split_axis=0, concat_axis=0, tiled=True)
    return mixed


CORE = 1
CLASS = 2
PAIR = CLASS | CORE
OVER_LAST = (((1,), (1,)), ((), ()))


def class_of(index):
    return (index // CLASS) % 2


def rank_in_class(utt):
    return utt // (2 * CLASS) * CLASS + utt % CLASS


def utt_of_rank(rank, device):
    return rank // CLASS * (2 * CLASS) + class_of(device) * CLASS + rank % CLASS


def class_order(beams, device):
    row = lax.broadcasted_iota(jnp.int32, (beams, beams), 0)
    col = lax.broadcasted_iota(jnp.int32, (beams, beams), 1)
    half = beams // 2
    place = rank_in_class(col) + jnp.where(class_of(col) == class_of(device), 0, half)
    return (row == place).astype(jnp.bfloat16)


def pack_kernel(
    new_ref,
    parents_hbm_ref,
    cache_ref,
    keep_ref,
    send_ref,
    keys_ref,
    values_ref,
    query_ref,
    key_ref,
    parents_ref,
    sems,
):
    rows, feature = query_ref.shape
    other = 1 - class_of(lax.axis_index("utt").astype(jnp.int32))
    slicing = [
        pltpu.make_async_copy(cache_ref.at[:, other, :, :feature], keys_ref, sems.at[3]),
        pltpu.make_async_copy(cache_ref.at[:, other, :, feature:], values_ref, sems.at[4]),
    ]
    copies = [
        pltpu.make_async_copy(new_ref.at[:, :feature], query_ref, sems.at[0]),
        pltpu.make_async_copy(new_ref.at[:, feature : 2 * feature], key_ref, sems.at[1]),
        pltpu.make_async_copy(parents_hbm_ref, parents_ref, sems.at[2]),
    ]
    for copy in copies + slicing:
        copy.start()
    half = rows // 2
    beams = parents_ref.shape[1]
    order = class_order(rows, lax.axis_index("utt"))
    for copy in copies:
        copy.wait()
    query = query_ref[...]
    product = query.astype(jnp.float32) * key_ref[...].astype(jnp.float32)
    lane = lax.broadcasted_iota(jnp.int32, (rows, LANES), 1)
    heads = feature // HD
    at_parent_lane = lax.broadcasted_iota(jnp.int32, (beams, LANES), 0) + PARENT_LANE
    at_parent_lane = at_parent_lane == lax.broadcasted_iota(jnp.int32, (beams, LANES), 1)
    extra = jnp.dot(
        jnp.broadcast_to(parents_ref[...], (rows, beams)).astype(jnp.bfloat16),
        at_parent_lane.astype(jnp.bfloat16),
        preferred_element_type=jnp.float32,
    )
    for head in range(heads):
        own = jnp.sum(product[:, head * HD : (head + 1) * HD], axis=1, keepdims=True) * HD ** (-0.5)
        for part in range(3):
            term = own.astype(jnp.bfloat16).astype(jnp.float32)
            extra = jnp.where(lane == part * heads + head, term, extra)
            own = own - term
    extra = extra.astype(jnp.bfloat16)
    for at in range(0, feature + LANES, LANES):
        tile = query[:, at : at + LANES] if at < feature else extra
        tile = jnp.dot(order, tile, preferred_element_type=jnp.float32)
        keep_ref[:, at : at + LANES] = tile[:half].astype(jnp.bfloat16)
        send_ref[:, at : at + LANES] = tile[half:].astype(jnp.bfloat16)
    for copy in slicing:
        copy.wait()


def cross_weights_kernel(lengths_ref, query_ref, keys_ref, out_ref):
    rows, feature = query_ref.shape
    frames = keys_ref.shape[0]
    heads = feature // HD
    live = lax.broadcasted_iota(jnp.int32, (rows, frames), 1) < lengths_ref[:, :1]
    scores = []
    for head in range(heads):
        at = slice(head * HD, (head + 1) * HD)
        scores.append(
            lax.dot_general(
                query_ref[:, at], keys_ref[:, at], OVER_LAST, preferred_element_type=jnp.float32
            )
        )
    for head in range(heads):
        masked = jnp.where(live, scores[head] * HD ** (-0.5), MASKED)
        raised = jnp.where(live, jnp.exp(masked - jnp.max(masked, axis=1, keepdims=True)), 0.0)
        weights = raised / jnp.sum(raised, axis=1, keepdims=True)
        out_ref[head] = weights.astype(jnp.bfloat16)


def cross_values_kernel(weights_ref, values_ref, out_ref):
    for head in range(weights_ref.shape[0]):
        at = slice(head * HD, (head + 1) * HD)
        out_ref[:, at] = jnp.dot(
            weights_ref[head], values_ref[:, at], preferred_element_type=jnp.float32
        ).astype(jnp.bfloat16)


def cached(near_ref, far_ref, pair_near_ref, pair_far_ref, mine, at):
    pieces = [ref[part, mine, :, at] for ref in (near_ref, far_ref) for part in range(near_ref.shape[0])]
    return jnp.concatenate(pieces + [pair_near_ref[:, at], pair_far_ref[:, at]], axis=0)


def rows_of(masks, beams):
    return [mask ^ pair for mask in masks for pair in (0, PAIR)]


def self_weights_kernel(masks, counts, *refs):
    query_refs, refs = refs[:counts], refs[counts:]
    *cache_refs, weight_ref, share_ref, terms_ref, spread_ref = refs
    me = lax.axis_index("utt").astype(jnp.int32)
    mine = class_of(me)
    pair_keys, feature = cache_refs[-1].shape
    heads, rows, keys = weight_ref.shape
    beams = query_refs[0].shape[0]
    half_beams = beams // 2
    history = pair_keys // half_beams
    queries = jnp.concatenate([ref[...] for ref in query_refs], axis=0)
    extra = queries[:, feature:].astype(jnp.float32)

    utt = utt_of_rank(lax.broadcasted_iota(jnp.int32, (half_beams, LANES), 0), me)
    lane = lax.broadcasted_iota(jnp.int32, (half_beams, LANES), 1)
    table = jnp.zeros((half_beams, LANES), jnp.float32)
    for at, mask in enumerate(masks):
        lists = extra[at * beams : at * beams + half_beams]
        owner = me ^ mask
        table = jnp.where(utt == owner, lists, table)
        table = jnp.where(utt == (owner ^ CORE), pltpu.roll(lists, LANES - beams, 1), table)
    chosen = jnp.concatenate(
        [
            jnp.sum(
                jnp.where(lane == PARENT_LANE + (me ^ mask), table, 0.0), axis=1, keepdims=True
            )
            for mask in rows_of(masks, beams)
        ],
        axis=0,
    ).astype(jnp.int32)

    row_rank = lax.broadcasted_iota(jnp.int32, (rows, keys), 0) % half_beams
    key = lax.broadcasted_iota(jnp.int32, (rows, keys), 1)
    key_rank = key % pair_keys // history
    run = key // pair_keys
    owner = me ^ jnp.where(
        run == 0, 0, jnp.where(run == 1, CORE, jnp.where(run == 2, PAIR, PAIR ^ CORE))
    )
    live = (key_rank == row_rank) & (chosen == owner)
    group = CORE | PAIR
    row_live = (chosen // (group + 1)) == (me // (group + 1))

    tiles = [slice(at, at + LANES) for at in range(0, keys, LANES)]
    for head in range(heads):
        at = slice(head * HD, (head + 1) * HD)
        scores = lax.dot_general(
            queries[:, at], cached(*cache_refs, mine, at), OVER_LAST, preferred_element_type=jnp.float32
        )
        scores = jnp.where(live, scores, 0.0)
        rest = sum(scores[:, tile] for tile in tiles)
        for term_at in range(3):
            term = rest.astype(jnp.bfloat16)
            rest = rest - term.astype(jnp.float32)
            terms_ref[head * rows : (head + 1) * rows, term_at * LANES : (term_at + 1) * LANES] = term
    row_lane = lax.broadcasted_iota(jnp.int32, (rows, LANES), 1)
    fold = lax.broadcasted_iota(jnp.int32, (3 * LANES, LANES), 0) % history
    fold = fold == lax.broadcasted_iota(jnp.int32, (3 * LANES, LANES), 1) % history
    fold = fold.astype(jnp.bfloat16)
    folded = jnp.dot(terms_ref[...], fold, preferred_element_type=jnp.float32)
    packed = jnp.zeros((rows, LANES), jnp.float32)
    for head in range(heads):
        packed = jnp.where(
            row_lane // history == head, folded[head * rows : (head + 1) * rows], packed
        )
    packed = packed * HD ** (-0.5)
    part = lax.broadcasted_iota(jnp.int32, (LANES, LANES), 0)
    spread = lax.broadcasted_iota(jnp.int32, (LANES, LANES), 1) // history
    spread = (part < 3 * heads) & (part % heads == spread)
    own = jnp.dot(
        queries[:, feature:], spread.astype(jnp.bfloat16), preferred_element_type=jnp.float32
    )

    def over_tokens(tile, combine):
        step = 1
        while step < history:
            left = pltpu.roll(tile, step, 1)
            right = pltpu.roll(tile, LANES - step, 1)
            tile = combine(tile, jnp.where(row_lane // step % 2 == 0, right, left))
            step = 2 * step
        return tile

    peak = jnp.maximum(over_tokens(packed, jnp.maximum), own)
    raised = jnp.exp(packed - peak)
    own = jnp.exp(own - peak)
    share = 1.0 / (over_tokens(raised, jnp.add) + own)
    share_ref[...] = jnp.where(row_live, own * share, 0.0).astype(jnp.bfloat16)
    packed = (raised * share).astype(jnp.bfloat16)
    for head in range(heads):
        spread_ref[head * rows : (head + 1) * rows] = jnp.where(
            row_lane // history == head, packed, jnp.zeros_like(packed)
        )
    weights = jnp.dot(spread_ref[...], fold[:LANES], preferred_element_type=jnp.float32)
    for head in range(heads):
        for tile in tiles:
            weight_ref[head, :, tile] = jnp.where(
                live[:, tile], weights[head * rows : (head + 1) * rows], 0.0
            ).astype(jnp.bfloat16)


def self_values_kernel(masks, *refs):
    out_refs = refs[-len(masks) :]
    weight_ref, share_ref, *cache_refs, cross_near_ref, cross_far_ref = refs[: -len(masks)]
    me = lax.axis_index("utt").astype(jnp.int32)
    mine = class_of(me)
    heads, rows, _ = weight_ref.shape
    feature = heads * HD
    beams = cross_near_ref.shape[0]
    blocks = [slice(at * beams, (at + 1) * beams) for at in (masks.index(m) for m in sorted(masks))]
    half_beams = beams // 2
    for out_ref, block in zip(out_refs, blocks):
        out_ref[:, feature:] = share_ref[block]

    place = lax.broadcasted_iota(jnp.int32, (rows, beams), 1)
    pick_utt = utt_of_rank(lax.broadcasted_iota(jnp.int32, (rows, beams), 0) % half_beams, me)
    row_beam = me ^ jnp.concatenate(
        [jnp.full((half_beams, beams), mask, jnp.int32) for mask in rows_of(masks, beams)], axis=0
    )
    near_pick = ((place == row_beam) & (pick_utt == me)).astype(jnp.bfloat16)
    far_pick = ((place == row_beam) & (pick_utt == (me ^ CORE))).astype(jnp.bfloat16)
    pick = jnp.concatenate([near_pick, far_pick], axis=1)
    for head in range(heads):
        at = slice(head * HD, (head + 1) * HD)
        out = jnp.dot(
            weight_ref[head], cached(*cache_refs, mine, at), preferred_element_type=jnp.float32
        )
        cross = jnp.concatenate([cross_near_ref[:, at], cross_far_ref[:, at]], axis=0)
        out = out + jnp.dot(pick, cross, preferred_element_type=jnp.float32)
        out = out.astype(jnp.bfloat16)
        for out_ref, block in zip(out_refs, blocks):
            out_ref[:, at] = out[block]


def finish_kernel(history, mine_ref, came_ref, value_ref, out_ref):
    rows, feature = out_ref.shape
    order = class_order(rows, lax.axis_index("utt"))

    def ordered(at):
        tile = jnp.concatenate(
            [mine_ref[:, at].astype(jnp.float32), came_ref[:, at].astype(jnp.float32)], axis=0
        ).astype(jnp.bfloat16)
        return lax.dot_general(
            order, tile, (((0,), (0,)), ((), ())), preferred_element_type=jnp.float32
        )

    shares = ordered(slice(feature, feature + LANES))
    for head in range(feature // HD):
        at = slice(head * HD, (head + 1) * HD)
        out = ordered(at) + shares[:, head * history : head * history + 1] * value_ref[:, at].astype(jnp.float32)
        out_ref[:, at] = out.astype(jnp.bfloat16)


def whole(shape):
    return pl.BlockSpec(shape, lambda *_: (0,) * len(shape))


def body_by_parent(devices, cache_kv, new_rows, cross_queries, enc_kv, lengths, parents):
    beams = parents.shape[1]
    rows, feature = cross_queries.shape
    frames = enc_kv.shape[1]
    history = cache_kv.shape[1]
    heads = feature // HD
    width = feature + LANES
    keys = beams * history
    me = lax.axis_index("utt").astype(jnp.int32)
    params = pltpu.CompilerParams(vmem_limit_bytes=16 * 1024 * 1024)

    def swap(array, bits):
        return lax.ppermute(array, "utt", [(i, i ^ bits) for i in range(devices)])

    def after(array, *others):
        return lax.optimization_barrier((array,) + others)[0]

    def in_hbm(array):
        return pltpu.with_memory_space_constraint(array, pltpu.HBM)

    hops = [(1 << k) | CORE for k in range(devices.bit_length() - 2, 1, -1)]

    near = cache_kv.reshape(beams // (2 * CLASS), 2, CLASS * history, 2 * feature)
    half_rows = jax.ShapeDtypeStruct((rows // 2, width), jnp.bfloat16)
    half_cache = jax.ShapeDtypeStruct(near.shape[:1] + near.shape[2:3] + (feature,), jnp.bfloat16)
    own, other, other_keys, other_values = pl.pallas_call(
        pack_kernel,
        out_shape=(half_rows, half_rows, half_cache, half_cache),
        in_specs=[pl.BlockSpec(memory_space=pltpu.HBM)] * 3,
        out_specs=(whole(half_rows.shape),) * 2 + (whole(half_cache.shape),) * 2,
        scratch_shapes=[
            pltpu.VMEM((rows, feature), jnp.bfloat16),
            pltpu.VMEM((rows, feature), jnp.bfloat16),
            pltpu.VMEM(parents.shape, jnp.int32),
            pltpu.SemaphoreType.DMA((5,)),
        ],
        compiler_params=params,
        cost_estimate=pl.CostEstimate(
            flops=4_000_000_000, bytes_accessed=4 * near.size, transcendentals=0
        ),
    )(
        in_hbm(new_rows),
        in_hbm(parents),
        in_hbm(near),
    )
    pair_rows = swap(other, PAIR)
    pair_keys = swap(other_keys, PAIR).reshape(keys // 2, feature)
    pair_values = swap(other_values, PAIR).reshape(keys // 2, feature)

    lists = jnp.pad(
        swap(after(parents, other), CORE).astype(jnp.bfloat16),
        ((0, 0), (feature + PARENT_LANE + beams, LANES - PARENT_LANE - 2 * beams)),
    )
    frame_count = jnp.broadcast_to(lengths.reshape(1, 1), (1, LANES))
    held = jnp.concatenate([own + lists, pair_rows], axis=0)

    frames_kv = enc_kv.reshape(frames, 2 * feature)
    cross_weights = pl.pallas_call(
        cross_weights_kernel,
        out_shape=jax.ShapeDtypeStruct((heads, rows, frames), jnp.bfloat16),
        grid=(1,),
        in_specs=[
            whole((1, LANES)),
            whole((rows, feature)),
            pl.BlockSpec((frames, feature), lambda i: (0, 0)),
        ],
        out_specs=whole((heads, rows, frames)),
        compiler_params=params,
    )(frame_count, after(cross_queries, held), frames_kv)
    far = swap(after(near, other), CORE)
    blocks = {0: held}
    for bits in hops:
        for mask, block in list(blocks.items()):
            blocks[mask ^ bits] = swap(after(block, cross_weights) if mask else block, bits)
    masks, gathered = list(blocks), list(blocks.values())

    cross_near = pl.pallas_call(
        cross_values_kernel,
        out_shape=jax.ShapeDtypeStruct((rows, feature), jnp.bfloat16),
        grid=(1,),
        in_specs=[
            whole((heads, rows, frames)),
            pl.BlockSpec((frames, feature), lambda i: (0, 1)),
        ],
        out_specs=whole((rows, feature)),
        compiler_params=params,
    )(after(cross_weights, *gathered[:-1]), frames_kv)
    cross_far = swap(cross_near, CORE)

    pair_far_keys = swap(after(pair_keys, blocks[hops[0]]), CORE)
    pair_far_values = swap(after(pair_values, gathered[-1], cross_near), CORE)

    all_rows = rows * len(masks)
    weight_shape = jax.ShapeDtypeStruct((heads, all_rows, 2 * keys), jnp.bfloat16)
    share_shape = jax.ShapeDtypeStruct((all_rows, LANES), jnp.bfloat16)
    part = jax.ShapeDtypeStruct((rows, width), jnp.bfloat16)
    near_shape = near.shape[:3] + (feature,)
    in_keys = pl.BlockSpec(near_shape, lambda i: (0, 0, 0, 0))
    in_values = pl.BlockSpec(near_shape, lambda i: (0, 0, 0, 1))
    pair_spec = whole(pair_keys.shape)
    weights, shares = pl.pallas_call(
        functools.partial(self_weights_kernel, tuple(masks), len(gathered)),
        out_shape=(weight_shape, share_shape),
        grid=(1,),
        in_specs=[whole(block.shape) for block in gathered]
        + [in_keys, in_keys, pair_spec, pair_spec],
        out_specs=(whole(weight_shape.shape), whole(share_shape.shape)),
        scratch_shapes=[
            pltpu.VMEM((heads * all_rows, 3 * LANES), jnp.bfloat16),
            pltpu.VMEM((heads * all_rows, LANES), jnp.bfloat16),
        ],
        compiler_params=params,
    )(*gathered, near, far, pair_keys, pair_far_keys)
    parts = pl.pallas_call(
        functools.partial(self_values_kernel, tuple(masks)),
        out_shape=(part,) * len(masks),
        grid=(1,),
        in_specs=[whole(weights.shape), whole(shares.shape)]
        + [in_values, in_values, pair_spec, pair_spec]
        + [whole((rows, feature))] * 2,
        out_specs=(whole(part.shape),) * len(masks),
        compiler_params=params,
    )(weights, shares, near, far, pair_values, pair_far_values, cross_near, cross_far)

    parts = dict(zip(sorted(masks), parts))
    for bits in hops[::-1]:
        for mask in sorted(parts, reverse=True):
            if mask ^ bits in parts and mask ^ bits < mask:
                parts[mask ^ bits] = parts[mask ^ bits] + swap(parts.pop(mask), bits)
    (mixed,) = parts.values()
    keep = mixed[: rows // 2]
    came = swap(mixed[rows // 2 :], PAIR)

    return pl.pallas_call(
        functools.partial(finish_kernel, history),
        out_shape=jax.ShapeDtypeStruct((rows, feature), jnp.bfloat16),
        grid=(1,),
        in_specs=[
            whole(half_rows.shape),
            whole(half_rows.shape),
            pl.BlockSpec((rows, feature), lambda i: (0, 2)),
        ],
        out_specs=whole((rows, feature)),
        compiler_params=params,
    )(keep, came, new_rows)


def solution(mesh):
    placed = (
        P(("groups", "utt"), None, None),
        P(("groups", "utt"), None),
        P(("groups", "utt"), None),
        P(("groups", "utt"), None, None),
        P(("groups", "utt")),
        P(("groups", "utt"), None),
    )
    devices = mesh.shape["utt"]

    def body(cache_kv, new_rows, cross_queries, enc_kv, lengths, parents):
        beams = parents.shape[1]
        heads = cross_queries.shape[1] // HD
        history = cache_kv.shape[1]
        fits = (
            parents.shape[0] == 1
            and devices == beams
            and devices >= 8
            and devices & (devices - 1) == 0
            and beams % 16 == 0
            and history & (history - 1) == 0
            and heads * history <= LANES
            and 3 * heads <= PARENT_LANE
            and PARENT_LANE + 2 * beams <= LANES
        )
        plan = functools.partial(body_by_parent, devices) if fits else body_by_utterance
        return plan(cache_kv, new_rows, cross_queries, enc_kv, lengths, parents)

    return jax.shard_map(
        body, mesh=mesh, in_specs=placed, out_specs=P(("groups", "utt"), None), check_vma=False
    )
```

```python
import functools

import jax
import jax.numpy as jnp
from jax import lax
from jax.experimental import pallas as pl
from jax.experimental.pallas import tpu as pltpu
from jax.sharding import PartitionSpec as P

HD = 128
LANES = 128
PARENT_LANE = 64
MASKED = -1e30


def reorder(cache_rows, parents):
    utterances, beam_width = parents.shape
    grouped = cache_rows.reshape(utterances, beam_width, cache_rows.shape[1], cache_rows.shape[2])
    picked = jax.vmap(lambda block, picks: block[picks])(grouped, parents)
    return picked.reshape(cache_rows.shape)


def attend_self(query, old_keys, old_values, new_key, new_value):
    row_count = query.shape[0]
    history = old_keys.shape[1]
    head_count = query.shape[1] // HD
    scale = HD ** (-0.5)
    query_heads = query.reshape(row_count, head_count, HD)
    key_heads = old_keys.reshape(row_count, history, head_count, HD)
    value_heads = old_values.reshape(row_count, history, head_count, HD)
    old_scores = (
        jnp.einsum("rhd,rthd->rht", query_heads, key_heads, preferred_element_type=jnp.float32)
        * scale
    )
    own_score = (
        jnp.einsum(
            "rhd,rhd->rh",
            query_heads,
            new_key.reshape(row_count, head_count, HD),
            preferred_element_type=jnp.float32,
        )
        * scale
    )
    peak = jnp.maximum(jnp.max(old_scores, axis=2), own_score)
    old_exp = jnp.exp(old_scores - peak[:, :, None])
    own_exp = jnp.exp(own_score - peak)
    total = jnp.sum(old_exp, axis=2) + own_exp
    old_weight = (old_exp / total[:, :, None]).astype(jnp.bfloat16)
    own_weight = (own_exp / total).astype(jnp.bfloat16)
    context = jnp.einsum(
        "rht,rthd->rhd", old_weight, value_heads, preferred_element_type=jnp.float32
    )
    context = context + own_weight.astype(jnp.float32)[:, :, None] * new_value.reshape(
        row_count, head_count, HD
    ).astype(jnp.float32)
    return context.reshape(row_count, head_count * HD).astype(jnp.bfloat16)


def attend_frames(queries, frames_kv, frame_counts):
    utterances = frame_counts.shape[0]
    beam_width = queries.shape[0] // utterances
    feature = queries.shape[1]
    head_count = feature // HD
    frame_total = frames_kv.shape[1]
    scale = HD ** (-0.5)
    query_heads = queries.reshape(utterances, beam_width, head_count, HD)
    key_heads = frames_kv[:, :, :feature].reshape(utterances, frame_total, head_count, HD)
    value_heads = frames_kv[:, :, feature:].reshape(utterances, frame_total, head_count, HD)
    scores = (
        jnp.einsum("ubhd,ufhd->uhbf", query_heads, key_heads, preferred_element_type=jnp.float32)
        * scale
    )
    live = (
        lax.broadcasted_iota(jnp.int32, (utterances, 1, 1, frame_total), 3)
        < frame_counts[:, None, None, None]
    )
    scores = jnp.where(live, scores, -1e30)
    peak = jnp.max(scores, axis=3, keepdims=True)
    raised = jnp.where(live, jnp.exp(scores - peak), 0.0)
    weights = (raised / jnp.sum(raised, axis=3, keepdims=True)).astype(jnp.bfloat16)
    context = jnp.einsum(
        "uhbf,ufhd->ubhd", weights, value_heads, preferred_element_type=jnp.float32
    )
    return context.reshape(utterances * beam_width, feature)


def body_by_utterance(cache_kv, new_rows, cross_queries, enc_kv, lengths, parents):
    feature = cross_queries.shape[1]
    cross_context = attend_frames(cross_queries, enc_kv, lengths)
    arrived, new_here = (
        lax.all_to_all(cache_kv, "utt", split_axis=0, concat_axis=0, tiled=True),
        lax.all_to_all(new_rows, "utt", split_axis=0, concat_axis=0, tiled=True),
    )
    reordered = reorder(arrived, parents)
    self_context = attend_self(
        new_here[:, :feature],
        reordered[:, :, :feature],
        reordered[:, :, feature:],
        new_here[:, feature : 2 * feature],
        new_here[:, 2 * feature :],
    )
    mixed_here = (self_context.astype(jnp.float32) + cross_context).astype(jnp.bfloat16)
    mixed = lax.all_to_all(mixed_here, "utt", split_axis=0, concat_axis=0, tiled=True)
    return mixed


CORE = 1
CLASS = 2
PAIR = CLASS | CORE
OVER_LAST = (((1,), (1,)), ((), ()))


def class_of(index):
    return (index // CLASS) % 2


def rank_in_class(utt):
    return utt // (2 * CLASS) * CLASS + utt % CLASS


def utt_of_rank(rank, device):
    return rank // CLASS * (2 * CLASS) + class_of(device) * CLASS + rank % CLASS


def rank_of_row(row, half):
    return half - 1 - row % half


def class_order(beams, device):
    row = lax.broadcasted_iota(jnp.int32, (beams, beams), 0)
    col = lax.broadcasted_iota(jnp.int32, (beams, beams), 1)
    half = beams // 2
    place = rank_of_row(rank_in_class(col), half)
    place = place + jnp.where(class_of(col) == class_of(device), 0, half)
    return (row == place).astype(jnp.bfloat16)


def pack_kernel(
    new_ref,
    parents_hbm_ref,
    cache_ref,
    keep_ref,
    send_ref,
    keys_ref,
    values_ref,
    query_ref,
    key_ref,
    parents_ref,
    sems,
):
    rows, feature = query_ref.shape
    other = 1 - class_of(lax.axis_index("utt").astype(jnp.int32))
    slicing = [
        pltpu.make_async_copy(cache_ref.at[:, other, :, :feature], keys_ref, sems.at[3]),
        pltpu.make_async_copy(cache_ref.at[:, other, :, feature:], values_ref, sems.at[4]),
    ]
    copies = [
        pltpu.make_async_copy(new_ref.at[:, :feature], query_ref, sems.at[0]),
        pltpu.make_async_copy(new_ref.at[:, feature : 2 * feature], key_ref, sems.at[1]),
        pltpu.make_async_copy(parents_hbm_ref, parents_ref, sems.at[2]),
    ]
    for copy in copies + slicing:
        copy.start()
    half = rows // 2
    beams = parents_ref.shape[1]
    order = class_order(rows, lax.axis_index("utt"))
    for copy in copies:
        copy.wait()
    query = query_ref[...]
    product = query.astype(jnp.float32) * key_ref[...].astype(jnp.float32)
    lane = lax.broadcasted_iota(jnp.int32, (rows, LANES), 1)
    heads = feature // HD
    at_parent_lane = lax.broadcasted_iota(jnp.int32, (beams, LANES), 0) + PARENT_LANE
    at_parent_lane = at_parent_lane == lax.broadcasted_iota(jnp.int32, (beams, LANES), 1)
    extra = jnp.dot(
        jnp.broadcast_to(parents_ref[...], (rows, beams)).astype(jnp.bfloat16),
        at_parent_lane.astype(jnp.bfloat16),
        preferred_element_type=jnp.float32,
    )
    for head in range(heads):
        own = jnp.sum(product[:, head * HD : (head + 1) * HD], axis=1, keepdims=True) * HD ** (-0.5)
        for part in range(3):
            term = own.astype(jnp.bfloat16).astype(jnp.float32)
            extra = jnp.where(lane == part * heads + head, term, extra)
            own = own - term
    extra = extra.astype(jnp.bfloat16)
    for at in range(0, feature + LANES, LANES):
        tile = query[:, at : at + LANES] if at < feature else extra
        tile = jnp.dot(order, tile, preferred_element_type=jnp.float32)
        keep_ref[:, at : at + LANES] = tile[:half].astype(jnp.bfloat16)
        send_ref[:, at : at + LANES] = tile[half:].astype(jnp.bfloat16)
    for copy in slicing:
        copy.wait()


def cross_kernel(lengths_ref, query_ref, frames_ref, out_ref):
    rows, feature = query_ref.shape
    frames = frames_ref.shape[0]
    heads = feature // HD
    live = lax.broadcasted_iota(jnp.int32, (rows, frames), 1) < lengths_ref[:, :1]
    scores = []
    for head in range(heads):
        at = slice(head * HD, (head + 1) * HD)
        scores.append(
            lax.dot_general(
                query_ref[:, at], frames_ref[:, at], OVER_LAST, preferred_element_type=jnp.float32
            )
        )
    weights = []
    for head in range(heads):
        masked = jnp.where(live, scores[head] * HD ** (-0.5), MASKED)
        raised = jnp.where(live, jnp.exp(masked - jnp.max(masked, axis=1, keepdims=True)), 0.0)
        weights.append((raised / jnp.sum(raised, axis=1, keepdims=True)).astype(jnp.bfloat16))
    for head in range(heads):
        at = slice(head * HD, (head + 1) * HD)
        value_at = slice(feature + head * HD, feature + (head + 1) * HD)
        out_ref[:, at] = jnp.dot(
            weights[head], frames_ref[:, value_at], preferred_element_type=jnp.float32
        ).astype(jnp.bfloat16)


def cached(near_ref, far_ref, pair_near_ref, pair_far_ref, mine, at):
    pieces = [ref[part, mine, :, at] for ref in (near_ref, far_ref) for part in range(near_ref.shape[0])]
    return jnp.concatenate(pieces + [pair_near_ref[:, at], pair_far_ref[:, at]], axis=0)


def rows_of(masks, beams):
    return [mask ^ pair for mask in masks for pair in (0, PAIR)]


def self_weights_kernel(masks, counts, *refs):
    query_refs, refs = refs[:counts], refs[counts:]
    *cache_refs, weight_ref, share_ref, spread_ref = refs
    me = lax.axis_index("utt").astype(jnp.int32)
    mine = class_of(me)
    pair_keys, feature = cache_refs[-1].shape
    heads, rows, keys = weight_ref.shape
    beams = query_refs[0].shape[0]
    half_beams = beams // 2
    history = pair_keys // half_beams
    queries = jnp.concatenate([ref[...] for ref in query_refs], axis=0)
    extra = queries[:, feature:].astype(jnp.float32)

    utt = lax.broadcasted_iota(jnp.int32, (half_beams, LANES), 0)
    utt = utt_of_rank(rank_of_row(utt, half_beams), me)
    lane = lax.broadcasted_iota(jnp.int32, (half_beams, LANES), 1)
    table = jnp.zeros((half_beams, LANES), jnp.float32)
    for at, mask in enumerate(masks):
        lists = extra[at * beams : at * beams + half_beams]
        owner = me ^ mask
        table = jnp.where(utt == owner, lists, table)
        table = jnp.where(utt == (owner ^ CORE), pltpu.roll(lists, LANES - beams, 1), table)
    chosen = jnp.concatenate(
        [
            jnp.sum(
                jnp.where(lane == PARENT_LANE + (me ^ mask), table, 0.0), axis=1, keepdims=True
            )
            for mask in rows_of(masks, beams)
        ],
        axis=0,
    ).astype(jnp.int32)

    row_rank = rank_of_row(lax.broadcasted_iota(jnp.int32, (rows, keys), 0), half_beams)
    key = lax.broadcasted_iota(jnp.int32, (rows, keys), 1)
    key_rank = key % pair_keys // history
    run = key // pair_keys
    owner = me ^ jnp.where(
        run == 0, 0, jnp.where(run == 1, CORE, jnp.where(run == 2, PAIR, PAIR ^ CORE))
    )
    live = (key_rank == row_rank) & (chosen == owner)
    group = CORE | PAIR
    row_live = (chosen // (group + 1)) == (me // (group + 1))

    tiles = [slice(at, at + LANES) for at in range(0, keys, LANES)]
    row_lane = lax.broadcasted_iota(jnp.int32, (rows, LANES), 1)
    packed = jnp.zeros((rows, LANES), jnp.float32)
    for head in range(heads):
        at = slice(head * HD, (head + 1) * HD)
        scores = lax.dot_general(
            queries[:, at], cached(*cache_refs, mine, at), OVER_LAST, preferred_element_type=jnp.float32
        )
        scores = jnp.where(live, scores, 0.0)
        scores = sum(scores[:, tile] for tile in tiles)
        scores = scores + pltpu.roll(scores, pair_keys, 1)
        shift = (head + 1) * history % pair_keys
        scores = jnp.concatenate(
            [
                pltpu.roll(scores[row : row + half_beams], shift, 1, stride=history, stride_axis=0)
                for row in range(0, rows, half_beams)
            ],
            axis=0,
        )
        packed = jnp.where(row_lane // history == head, scores, packed)
    fold = lax.broadcasted_iota(jnp.int32, (LANES, LANES), 0) % history
    fold = fold == lax.broadcasted_iota(jnp.int32, (LANES, LANES), 1) % history
    fold = fold.astype(jnp.bfloat16)
    packed = packed * HD ** (-0.5)
    part = lax.broadcasted_iota(jnp.int32, (LANES, LANES), 0)
    spread = lax.broadcasted_iota(jnp.int32, (LANES, LANES), 1) // history
    spread = (part < 3 * heads) & (part % heads == spread)
    own = jnp.dot(
        queries[:, feature:], spread.astype(jnp.bfloat16), preferred_element_type=jnp.float32
    )

    def over_tokens(tile, combine):
        step = 1
        while step < history:
            left = pltpu.roll(tile, step, 1)
            right = pltpu.roll(tile, LANES - step, 1)
            tile = combine(tile, jnp.where(row_lane // step % 2 == 0, right, left))
            step = 2 * step
        return tile

    peak = jnp.maximum(over_tokens(packed, jnp.maximum), own)
    raised = jnp.exp(packed - peak)
    own = jnp.exp(own - peak)
    share = 1.0 / (over_tokens(raised, jnp.add) + own)
    share_ref[...] = jnp.where(row_live, own * share, 0.0).astype(jnp.bfloat16)
    packed = (raised * share).astype(jnp.bfloat16)
    for head in range(heads):
        spread_ref[head * rows : (head + 1) * rows] = jnp.where(
            row_lane // history == head, packed, jnp.zeros_like(packed)
        )
    weights = jnp.dot(spread_ref[...], fold, preferred_element_type=jnp.float32)
    for head in range(heads):
        for tile in tiles:
            weight_ref[head, :, tile] = jnp.where(
                live[:, tile], weights[head * rows : (head + 1) * rows], 0.0
            ).astype(jnp.bfloat16)


def self_values_kernel(masks, *refs):
    out_refs = refs[-len(masks) :]
    weight_ref, share_ref, *cache_refs, cross_near_ref, cross_far_ref = refs[: -len(masks)]
    me = lax.axis_index("utt").astype(jnp.int32)
    mine = class_of(me)
    heads, rows, _ = weight_ref.shape
    feature = heads * HD
    beams = cross_near_ref.shape[0]
    blocks = [slice(at * beams, (at + 1) * beams) for at in (masks.index(m) for m in sorted(masks))]
    half_beams = beams // 2
    for out_ref, block in zip(out_refs, blocks):
        out_ref[:, feature:] = share_ref[block]

    place = lax.broadcasted_iota(jnp.int32, (rows, beams), 1)
    pick_utt = lax.broadcasted_iota(jnp.int32, (rows, beams), 0)
    pick_utt = utt_of_rank(rank_of_row(pick_utt, half_beams), me)
    row_beam = me ^ jnp.concatenate(
        [jnp.full((half_beams, beams), mask, jnp.int32) for mask in rows_of(masks, beams)], axis=0
    )
    near_pick = ((place == row_beam) & (pick_utt == me)).astype(jnp.bfloat16)
    far_pick = ((place == row_beam) & (pick_utt == (me ^ CORE))).astype(jnp.bfloat16)
    pick = jnp.concatenate([near_pick, far_pick], axis=1)
    for head in range(heads):
        at = slice(head * HD, (head + 1) * HD)
        out = jnp.dot(
            weight_ref[head], cached(*cache_refs, mine, at), preferred_element_type=jnp.float32
        )
        cross = jnp.concatenate([cross_near_ref[:, at], cross_far_ref[:, at]], axis=0)
        out = out + jnp.dot(pick, cross, preferred_element_type=jnp.float32)
        out = out.astype(jnp.bfloat16)
        for out_ref, block in zip(out_refs, blocks):
            out_ref[:, at] = out[block]


def finish_kernel(history, mine_ref, came_ref, value_ref, out_ref):
    rows, feature = out_ref.shape
    order = class_order(rows, lax.axis_index("utt"))

    def ordered(at):
        tile = jnp.concatenate(
            [mine_ref[:, at].astype(jnp.float32), came_ref[:, at].astype(jnp.float32)], axis=0
        ).astype(jnp.bfloat16)
        return lax.dot_general(
            order, tile, (((0,), (0,)), ((), ())), preferred_element_type=jnp.float32
        )

    shares = ordered(slice(feature, feature + LANES))
    for head in range(feature // HD):
        at = slice(head * HD, (head + 1) * HD)
        out = ordered(at) + shares[:, head * history : head * history + 1] * value_ref[:, at].astype(jnp.float32)
        out_ref[:, at] = out.astype(jnp.bfloat16)


def whole(shape):
    return pl.BlockSpec(shape, lambda *_: (0,) * len(shape))


def body_by_parent(devices, cache_kv, new_rows, cross_queries, enc_kv, lengths, parents):
    beams = parents.shape[1]
    rows, feature = cross_queries.shape
    frames = enc_kv.shape[1]
    history = cache_kv.shape[1]
    heads = feature // HD
    width = feature + LANES
    keys = beams * history
    me = lax.axis_index("utt").astype(jnp.int32)
    params = pltpu.CompilerParams(vmem_limit_bytes=16 * 1024 * 1024)

    def swap(array, bits):
        return lax.ppermute(array, "utt", [(i, i ^ bits) for i in range(devices)])

    def after(array, *others):
        return lax.optimization_barrier((array,) + others)[0]

    def in_hbm(array):
        return pltpu.with_memory_space_constraint(array, pltpu.HBM)

    hops = [(1 << k) | CORE for k in range(devices.bit_length() - 2, 1, -1)]

    near = cache_kv.reshape(beams // (2 * CLASS), 2, CLASS * history, 2 * feature)
    half_rows = jax.ShapeDtypeStruct((rows // 2, width), jnp.bfloat16)
    half_cache = jax.ShapeDtypeStruct(near.shape[:1] + near.shape[2:3] + (feature,), jnp.bfloat16)
    own, other, other_keys, other_values = pl.pallas_call(
        pack_kernel,
        out_shape=(half_rows, half_rows, half_cache, half_cache),
        in_specs=[pl.BlockSpec(memory_space=pltpu.HBM)] * 3,
        out_specs=(whole(half_rows.shape),) * 2 + (whole(half_cache.shape),) * 2,
        scratch_shapes=[
            pltpu.VMEM((rows, feature), jnp.bfloat16),
            pltpu.VMEM((rows, feature), jnp.bfloat16),
            pltpu.VMEM(parents.shape, jnp.int32),
            pltpu.SemaphoreType.DMA((5,)),
        ],
        compiler_params=params,
        cost_estimate=pl.CostEstimate(
            flops=4_000_000_000, bytes_accessed=4 * near.size, transcendentals=0
        ),
    )(
        in_hbm(new_rows),
        in_hbm(parents),
        in_hbm(near),
    )
    pair_rows = swap(other, PAIR)
    pair_keys = swap(other_keys, PAIR).reshape(keys // 2, feature)
    pair_values = swap(other_values, PAIR).reshape(keys // 2, feature)

    lists = jnp.pad(
        swap(after(parents, other), CORE).astype(jnp.bfloat16),
        ((0, 0), (feature + PARENT_LANE + beams, LANES - PARENT_LANE - 2 * beams)),
    )
    frame_count = jnp.broadcast_to(lengths.reshape(1, 1), (1, LANES))
    held = jnp.concatenate([own + lists, pair_rows], axis=0)

    cross_near = pl.pallas_call(
        cross_kernel,
        out_shape=jax.ShapeDtypeStruct((rows, feature), jnp.bfloat16),
        grid=(1,),
        in_specs=[whole((1, LANES)), whole((rows, feature)), whole((frames, 2 * feature))],
        out_specs=whole((rows, feature)),
        compiler_params=params,
    )(frame_count, after(cross_queries, held), enc_kv.reshape(frames, 2 * feature))
    far = swap(after(near, other), CORE)
    blocks = {0: held}
    for bits in hops:
        for mask, block in list(blocks.items()):
            blocks[mask ^ bits] = swap(after(block, cross_near) if mask else block, bits)
    masks, gathered = list(blocks), list(blocks.values())

    cross_far = swap(cross_near, CORE)

    pair_far_keys = swap(after(pair_keys, *gathered[:-1]), CORE)
    pair_far_values = swap(after(pair_values, gathered[-1], cross_near), CORE)

    all_rows = rows * len(masks)
    weight_shape = jax.ShapeDtypeStruct((heads, all_rows, 2 * keys), jnp.bfloat16)
    share_shape = jax.ShapeDtypeStruct((all_rows, LANES), jnp.bfloat16)
    part = jax.ShapeDtypeStruct((rows, width), jnp.bfloat16)
    near_shape = near.shape[:3] + (feature,)
    in_keys = pl.BlockSpec(near_shape, lambda i: (0, 0, 0, 0))
    in_values = pl.BlockSpec(near_shape, lambda i: (0, 0, 0, 1))
    pair_spec = whole(pair_keys.shape)
    weights, shares = pl.pallas_call(
        functools.partial(self_weights_kernel, tuple(masks), len(gathered)),
        out_shape=(weight_shape, share_shape),
        grid=(1,),
        in_specs=[whole(block.shape) for block in gathered]
        + [in_keys, in_keys, pair_spec, pair_spec],
        out_specs=(whole(weight_shape.shape), whole(share_shape.shape)),
        scratch_shapes=[pltpu.VMEM((heads * all_rows, LANES), jnp.bfloat16)],
        compiler_params=params,
    )(*gathered, near, far, pair_keys, pair_far_keys)
    parts = pl.pallas_call(
        functools.partial(self_values_kernel, tuple(masks)),
        out_shape=(part,) * len(masks),
        grid=(1,),
        in_specs=[whole(weights.shape), whole(shares.shape)]
        + [in_values, in_values, pair_spec, pair_spec]
        + [whole((rows, feature))] * 2,
        out_specs=(whole(part.shape),) * len(masks),
        compiler_params=params,
    )(weights, shares, near, far, pair_values, pair_far_values, cross_near, cross_far)

    parts = dict(zip(sorted(masks), parts))
    for bits in hops[::-1]:
        for mask in sorted(parts, reverse=True):
            if mask ^ bits in parts and mask ^ bits < mask:
                parts[mask ^ bits] = parts[mask ^ bits] + swap(parts.pop(mask), bits)
    (mixed,) = parts.values()
    keep = mixed[: rows // 2]
    came = swap(mixed[rows // 2 :], PAIR)

    return pl.pallas_call(
        functools.partial(finish_kernel, history),
        out_shape=jax.ShapeDtypeStruct((rows, feature), jnp.bfloat16),
        grid=(1,),
        in_specs=[
            whole(half_rows.shape),
            whole(half_rows.shape),
            pl.BlockSpec((rows, feature), lambda i: (0, 2)),
        ],
        out_specs=whole((rows, feature)),
        compiler_params=params,
    )(keep, came, new_rows)


def solution(mesh):
    placed = (
        P(("groups", "utt"), None, None),
        P(("groups", "utt"), None),
        P(("groups", "utt"), None),
        P(("groups", "utt"), None, None),
        P(("groups", "utt")),
        P(("groups", "utt"), None),
    )
    devices = mesh.shape["utt"]

    def body(cache_kv, new_rows, cross_queries, enc_kv, lengths, parents):
        beams = parents.shape[1]
        heads = cross_queries.shape[1] // HD
        history = cache_kv.shape[1]
        fits = (
            parents.shape[0] == 1
            and devices == beams
            and devices >= 8
            and devices & (devices - 1) == 0
            and beams % 16 == 0
            and history & (history - 1) == 0
            and heads * history <= LANES
            and beams * history == LANES
            and 3 * heads <= PARENT_LANE
            and PARENT_LANE + 2 * beams <= LANES
        )
        plan = functools.partial(body_by_parent, devices) if fits else body_by_utterance
        return plan(cache_kv, new_rows, cross_queries, enc_kv, lengths, parents)

    return jax.shard_map(
        body, mesh=mesh, in_specs=placed, out_specs=P(("groups", "utt"), None), check_vma=False
    )
```

```python
import functools

import jax
import jax.numpy as jnp
from jax import lax
from jax.experimental import pallas as pl
from jax.experimental.pallas import tpu as pltpu
from jax.sharding import PartitionSpec as P

HD = 128
LANES = 128
PARENT_LANE = 64
MASKED = -1e30


def reorder(cache_rows, parents):
    utterances, beam_width = parents.shape
    grouped = cache_rows.reshape(utterances, beam_width, cache_rows.shape[1], cache_rows.shape[2])
    picked = jax.vmap(lambda block, picks: block[picks])(grouped, parents)
    return picked.reshape(cache_rows.shape)


def attend_self(query, old_keys, old_values, new_key, new_value):
    row_count = query.shape[0]
    history = old_keys.shape[1]
    head_count = query.shape[1] // HD
    scale = HD ** (-0.5)
    query_heads = query.reshape(row_count, head_count, HD)
    key_heads = old_keys.reshape(row_count, history, head_count, HD)
    value_heads = old_values.reshape(row_count, history, head_count, HD)
    old_scores = (
        jnp.einsum("rhd,rthd->rht", query_heads, key_heads, preferred_element_type=jnp.float32)
        * scale
    )
    own_score = (
        jnp.einsum(
            "rhd,rhd->rh",
            query_heads,
            new_key.reshape(row_count, head_count, HD),
            preferred_element_type=jnp.float32,
        )
        * scale
    )
    peak = jnp.maximum(jnp.max(old_scores, axis=2), own_score)
    old_exp = jnp.exp(old_scores - peak[:, :, None])
    own_exp = jnp.exp(own_score - peak)
    total = jnp.sum(old_exp, axis=2) + own_exp
    old_weight = (old_exp / total[:, :, None]).astype(jnp.bfloat16)
    own_weight = (own_exp / total).astype(jnp.bfloat16)
    context = jnp.einsum(
        "rht,rthd->rhd", old_weight, value_heads, preferred_element_type=jnp.float32
    )
    context = context + own_weight.astype(jnp.float32)[:, :, None] * new_value.reshape(
        row_count, head_count, HD
    ).astype(jnp.float32)
    return context.reshape(row_count, head_count * HD).astype(jnp.bfloat16)


def attend_frames(queries, frames_kv, frame_counts):
    utterances = frame_counts.shape[0]
    beam_width = queries.shape[0] // utterances
    feature = queries.shape[1]
    head_count = feature // HD
    frame_total = frames_kv.shape[1]
    scale = HD ** (-0.5)
    query_heads = queries.reshape(utterances, beam_width, head_count, HD)
    key_heads = frames_kv[:, :, :feature].reshape(utterances, frame_total, head_count, HD)
    value_heads = frames_kv[:, :, feature:].reshape(utterances, frame_total, head_count, HD)
    scores = (
        jnp.einsum("ubhd,ufhd->uhbf", query_heads, key_heads, preferred_element_type=jnp.float32)
        * scale
    )
    live = (
        lax.broadcasted_iota(jnp.int32, (utterances, 1, 1, frame_total), 3)
        < frame_counts[:, None, None, None]
    )
    scores = jnp.where(live, scores, -1e30)
    peak = jnp.max(scores, axis=3, keepdims=True)
    raised = jnp.where(live, jnp.exp(scores - peak), 0.0)
    weights = (raised / jnp.sum(raised, axis=3, keepdims=True)).astype(jnp.bfloat16)
    context = jnp.einsum(
        "uhbf,ufhd->ubhd", weights, value_heads, preferred_element_type=jnp.float32
    )
    return context.reshape(utterances * beam_width, feature)


def body_by_utterance(cache_kv, new_rows, cross_queries, enc_kv, lengths, parents):
    feature = cross_queries.shape[1]
    cross_context = attend_frames(cross_queries, enc_kv, lengths)
    arrived, new_here = (
        lax.all_to_all(cache_kv, "utt", split_axis=0, concat_axis=0, tiled=True),
        lax.all_to_all(new_rows, "utt", split_axis=0, concat_axis=0, tiled=True),
    )
    reordered = reorder(arrived, parents)
    self_context = attend_self(
        new_here[:, :feature],
        reordered[:, :, :feature],
        reordered[:, :, feature:],
        new_here[:, feature : 2 * feature],
        new_here[:, 2 * feature :],
    )
    mixed_here = (self_context.astype(jnp.float32) + cross_context).astype(jnp.bfloat16)
    mixed = lax.all_to_all(mixed_here, "utt", split_axis=0, concat_axis=0, tiled=True)
    return mixed


CORE = 1
CLASS = 2
PAIR = CLASS | CORE
OVER_LAST = (((1,), (1,)), ((), ()))


def class_of(index):
    return (index // CLASS) % 2


def rank_in_class(utt):
    return utt // (2 * CLASS) * CLASS + utt % CLASS


def utt_of_rank(rank, device):
    return rank // CLASS * (2 * CLASS) + class_of(device) * CLASS + rank % CLASS


def rank_of_row(row, half):
    return half - 1 - row % half


def class_order(beams, device):
    row = lax.broadcasted_iota(jnp.int32, (beams, beams), 0)
    col = lax.broadcasted_iota(jnp.int32, (beams, beams), 1)
    half = beams // 2
    place = rank_of_row(rank_in_class(col), half)
    place = place + jnp.where(class_of(col) == class_of(device), 0, half)
    return (row == place).astype(jnp.bfloat16)


def pack_kernel(
    new_ref,
    parents_hbm_ref,
    cache_ref,
    keep_ref,
    send_ref,
    keys_ref,
    values_ref,
    query_ref,
    key_ref,
    parents_ref,
    sems,
):
    rows, feature = query_ref.shape
    other = 1 - class_of(lax.axis_index("utt").astype(jnp.int32))
    slicing = [
        pltpu.make_async_copy(cache_ref.at[:, other, :, :feature], keys_ref, sems.at[3]),
        pltpu.make_async_copy(cache_ref.at[:, other, :, feature:], values_ref, sems.at[4]),
    ]
    copies = [
        pltpu.make_async_copy(new_ref.at[:, :feature], query_ref, sems.at[0]),
        pltpu.make_async_copy(new_ref.at[:, feature : 2 * feature], key_ref, sems.at[1]),
        pltpu.make_async_copy(parents_hbm_ref, parents_ref, sems.at[2]),
    ]
    for copy in copies + slicing:
        copy.start()
    half = rows // 2
    beams = parents_ref.shape[1]
    order = class_order(rows, lax.axis_index("utt"))
    for copy in copies:
        copy.wait()
    query = query_ref[...]
    product = query.astype(jnp.float32) * key_ref[...].astype(jnp.float32)
    lane = lax.broadcasted_iota(jnp.int32, (rows, LANES), 1)
    heads = feature // HD
    at_parent_lane = lax.broadcasted_iota(jnp.int32, (beams, LANES), 0) + PARENT_LANE
    at_parent_lane = at_parent_lane == lax.broadcasted_iota(jnp.int32, (beams, LANES), 1)
    extra = jnp.dot(
        jnp.broadcast_to(parents_ref[...], (rows, beams)).astype(jnp.bfloat16),
        at_parent_lane.astype(jnp.bfloat16),
        preferred_element_type=jnp.float32,
    )
    for head in range(heads):
        own = jnp.sum(product[:, head * HD : (head + 1) * HD], axis=1, keepdims=True) * HD ** (-0.5)
        for part in range(3):
            term = own.astype(jnp.bfloat16).astype(jnp.float32)
            extra = jnp.where(lane == part * heads + head, term, extra)
            own = own - term
    extra = extra.astype(jnp.bfloat16)
    for at in range(0, feature + LANES, LANES):
        tile = query[:, at : at + LANES] if at < feature else extra
        tile = jnp.dot(order, tile, preferred_element_type=jnp.float32)
        keep_ref[:, at : at + LANES] = tile[:half].astype(jnp.bfloat16)
        send_ref[:, at : at + LANES] = tile[half:].astype(jnp.bfloat16)
    for copy in slicing:
        copy.wait()


def cross_kernel(lengths_ref, query_ref, frames_ref, out_ref):
    rows, feature = query_ref.shape
    frames = frames_ref.shape[0]
    heads = feature // HD
    live = lax.broadcasted_iota(jnp.int32, (rows, frames), 1) < lengths_ref[:, :1]
    scores = []
    for head in range(heads):
        at = slice(head * HD, (head + 1) * HD)
        scores.append(
            lax.dot_general(
                query_ref[:, at], frames_ref[:, at], OVER_LAST, preferred_element_type=jnp.float32
            )
        )
    weights = []
    for head in range(heads):
        masked = jnp.where(live, scores[head] * HD ** (-0.5), MASKED)
        raised = jnp.where(live, jnp.exp(masked - jnp.max(masked, axis=1, keepdims=True)), 0.0)
        weights.append((raised / jnp.sum(raised, axis=1, keepdims=True)).astype(jnp.bfloat16))
    for head in range(heads):
        at = slice(head * HD, (head + 1) * HD)
        value_at = slice(feature + head * HD, feature + (head + 1) * HD)
        out_ref[:, at] = jnp.dot(
            weights[head], frames_ref[:, value_at], preferred_element_type=jnp.float32
        ).astype(jnp.bfloat16)


def cached(near_ref, far_ref, pair_near_ref, pair_far_ref, mine, at):
    pieces = [ref[part, mine, :, at] for ref in (near_ref, far_ref) for part in range(near_ref.shape[0])]
    return jnp.concatenate(pieces + [pair_near_ref[:, at], pair_far_ref[:, at]], axis=0)


def rows_of(masks, beams):
    return [mask ^ pair for mask in masks for pair in (0, PAIR)]


def self_weights_kernel(masks, counts, *refs):
    query_refs, refs = refs[:counts], refs[counts:]
    *cache_refs, weight_ref, share_ref, spread_ref = refs
    me = lax.axis_index("utt").astype(jnp.int32)
    mine = class_of(me)
    pair_keys, feature = cache_refs[-1].shape
    heads, rows, keys = weight_ref.shape
    beams = query_refs[0].shape[0]
    half_beams = beams // 2
    history = pair_keys // half_beams
    queries = jnp.concatenate([ref[...] for ref in query_refs], axis=0)
    extra = queries[:, feature:].astype(jnp.float32)

    utt = lax.broadcasted_iota(jnp.int32, (half_beams, LANES), 0)
    utt = utt_of_rank(rank_of_row(utt, half_beams), me)
    lane = lax.broadcasted_iota(jnp.int32, (half_beams, LANES), 1)
    table = jnp.zeros((half_beams, LANES), jnp.float32)
    for at, mask in enumerate(masks):
        lists = extra[at * beams : at * beams + half_beams]
        owner = me ^ mask
        table = jnp.where(utt == owner, lists, table)
        table = jnp.where(utt == (owner ^ CORE), pltpu.roll(lists, LANES - beams, 1), table)
    chosen = jnp.concatenate(
        [
            jnp.sum(
                jnp.where(lane == PARENT_LANE + (me ^ mask), table, 0.0), axis=1, keepdims=True
            )
            for mask in rows_of(masks, beams)
        ],
        axis=0,
    ).astype(jnp.int32)

    row_rank = rank_of_row(lax.broadcasted_iota(jnp.int32, (rows, keys), 0), half_beams)
    key = lax.broadcasted_iota(jnp.int32, (rows, keys), 1)
    key_rank = key % pair_keys // history
    run = key // pair_keys
    owner = me ^ jnp.where(
        run == 0, 0, jnp.where(run == 1, CORE, jnp.where(run == 2, PAIR, PAIR ^ CORE))
    )
    live = (key_rank == row_rank) & (chosen == owner)
    group = CORE | PAIR
    row_live = (chosen // (group + 1)) == (me // (group + 1))

    tiles = [slice(at, at + LANES) for at in range(0, keys, LANES)]
    row_lane = lax.broadcasted_iota(jnp.int32, (rows, LANES), 1)
    packed = jnp.zeros((rows, LANES), jnp.float32)
    for head in range(heads):
        at = slice(head * HD, (head + 1) * HD)
        scores = lax.dot_general(
            queries[:, at], cached(*cache_refs, mine, at), OVER_LAST, preferred_element_type=jnp.float32
        )
        scores = jnp.where(live, scores, 0.0)
        scores = sum(scores[:, tile] for tile in tiles)
        scores = scores + pltpu.roll(scores, pair_keys, 1)
        shift = (head + 1) * history % pair_keys
        scores = jnp.concatenate(
            [
                pltpu.roll(scores[row : row + half_beams], shift, 1, stride=history, stride_axis=0)
                for row in range(0, rows, half_beams)
            ],
            axis=0,
        )
        packed = jnp.where(row_lane // history == head, scores, packed)
    fold = lax.broadcasted_iota(jnp.int32, (LANES, LANES), 0) % history
    fold = fold == lax.broadcasted_iota(jnp.int32, (LANES, LANES), 1) % history
    fold = fold.astype(jnp.bfloat16)
    packed = packed * HD ** (-0.5)
    part = lax.broadcasted_iota(jnp.int32, (LANES, LANES), 0)
    spread = lax.broadcasted_iota(jnp.int32, (LANES, LANES), 1) // history
    spread = (part < 3 * heads) & (part % heads == spread)
    own = jnp.dot(
        queries[:, feature:], spread.astype(jnp.bfloat16), preferred_element_type=jnp.float32
    )

    def over_tokens(tile, combine):
        step = 1
        while step < history:
            left = pltpu.roll(tile, step, 1)
            right = pltpu.roll(tile, LANES - step, 1)
            tile = combine(tile, jnp.where(row_lane // step % 2 == 0, right, left))
            step = 2 * step
        return tile

    peak = jnp.maximum(over_tokens(packed, jnp.maximum), own)
    raised = jnp.exp(packed - peak)
    own = jnp.exp(own - peak)
    share = 1.0 / (over_tokens(raised, jnp.add) + own)
    share_ref[...] = jnp.where(row_live, own * share, 0.0).astype(jnp.bfloat16)
    packed = (raised * share).astype(jnp.bfloat16)
    for head in range(heads):
        spread_ref[head * rows : (head + 1) * rows] = jnp.where(
            row_lane // history == head, packed, jnp.zeros_like(packed)
        )
    weights = jnp.dot(spread_ref[...], fold, preferred_element_type=jnp.float32)
    for head in range(heads):
        for tile in tiles:
            weight_ref[head, :, tile] = jnp.where(
                live[:, tile], weights[head * rows : (head + 1) * rows], 0.0
            ).astype(jnp.bfloat16)


def self_values_kernel(masks, *refs):
    out_refs = refs[-len(masks) :]
    weight_ref, share_ref, *cache_refs, cross_near_ref, cross_far_ref = refs[: -len(masks)]
    me = lax.axis_index("utt").astype(jnp.int32)
    mine = class_of(me)
    heads, rows, _ = weight_ref.shape
    feature = heads * HD
    beams = cross_near_ref.shape[0]
    blocks = [slice(at * beams, (at + 1) * beams) for at in (masks.index(m) for m in sorted(masks))]
    half_beams = beams // 2
    for out_ref, block in zip(out_refs, blocks):
        out_ref[:, feature:] = share_ref[block]

    place = lax.broadcasted_iota(jnp.int32, (rows, beams), 1)
    pick_utt = lax.broadcasted_iota(jnp.int32, (rows, beams), 0)
    pick_utt = utt_of_rank(rank_of_row(pick_utt, half_beams), me)
    row_beam = me ^ jnp.concatenate(
        [jnp.full((half_beams, beams), mask, jnp.int32) for mask in rows_of(masks, beams)], axis=0
    )
    near_pick = ((place == row_beam) & (pick_utt == me)).astype(jnp.bfloat16)
    far_pick = ((place == row_beam) & (pick_utt == (me ^ CORE))).astype(jnp.bfloat16)
    pick = jnp.concatenate([near_pick, far_pick], axis=1)
    for head in range(heads):
        at = slice(head * HD, (head + 1) * HD)
        out = jnp.dot(
            weight_ref[head], cached(*cache_refs, mine, at), preferred_element_type=jnp.float32
        )
        cross = jnp.concatenate([cross_near_ref[:, at], cross_far_ref[:, at]], axis=0)
        out = out + jnp.dot(pick, cross, preferred_element_type=jnp.float32)
        out = out.astype(jnp.bfloat16)
        for out_ref, block in zip(out_refs, blocks):
            out_ref[:, at] = out[block]


def finish_kernel(history, mine_ref, came_ref, value_ref, out_ref):
    rows, feature = out_ref.shape
    order = class_order(rows, lax.axis_index("utt"))

    def ordered(at):
        tile = jnp.concatenate(
            [mine_ref[:, at].astype(jnp.float32), came_ref[:, at].astype(jnp.float32)], axis=0
        ).astype(jnp.bfloat16)
        return lax.dot_general(
            order, tile, (((0,), (0,)), ((), ())), preferred_element_type=jnp.float32
        )

    shares = ordered(slice(feature, feature + LANES))
    for head in range(feature // HD):
        at = slice(head * HD, (head + 1) * HD)
        out = ordered(at) + shares[:, head * history : head * history + 1] * value_ref[:, at].astype(jnp.float32)
        out_ref[:, at] = out.astype(jnp.bfloat16)


def whole(shape):
    return pl.BlockSpec(shape, lambda *_: (0,) * len(shape))


def body_by_parent(devices, cache_kv, new_rows, cross_queries, enc_kv, lengths, parents):
    beams = parents.shape[1]
    rows, feature = cross_queries.shape
    frames = enc_kv.shape[1]
    history = cache_kv.shape[1]
    heads = feature // HD
    width = feature + LANES
    keys = beams * history
    me = lax.axis_index("utt").astype(jnp.int32)
    params = pltpu.CompilerParams(vmem_limit_bytes=16 * 1024 * 1024)

    def swap(array, bits):
        return lax.ppermute(array, "utt", [(i, i ^ bits) for i in range(devices)])

    def after(array, *others):
        return lax.optimization_barrier((array,) + others)[0]

    def in_hbm(array):
        return pltpu.with_memory_space_constraint(array, pltpu.HBM)

    hops = [(1 << k) | CORE for k in range(devices.bit_length() - 2, 1, -1)]

    near = cache_kv.reshape(beams // (2 * CLASS), 2, CLASS * history, 2 * feature)
    half_rows = jax.ShapeDtypeStruct((rows // 2, width), jnp.bfloat16)
    half_cache = jax.ShapeDtypeStruct(near.shape[:1] + near.shape[2:3] + (feature,), jnp.bfloat16)
    own, other, other_keys, other_values = pl.pallas_call(
        pack_kernel,
        out_shape=(half_rows, half_rows, half_cache, half_cache),
        in_specs=[pl.BlockSpec(memory_space=pltpu.HBM)] * 3,
        out_specs=(whole(half_rows.shape),) * 2 + (whole(half_cache.shape),) * 2,
        scratch_shapes=[
            pltpu.VMEM((rows, feature), jnp.bfloat16),
            pltpu.VMEM((rows, feature), jnp.bfloat16),
            pltpu.VMEM(parents.shape, jnp.int32),
            pltpu.SemaphoreType.DMA((5,)),
        ],
        compiler_params=params,
        cost_estimate=pl.CostEstimate(
            flops=1_500_000_000, bytes_accessed=4 * near.size, transcendentals=0
        ),
    )(
        in_hbm(new_rows),
        in_hbm(parents),
        in_hbm(near),
    )
    pair_rows = swap(other, PAIR)
    pair_keys = swap(other_keys, PAIR).reshape(keys // 2, feature)
    pair_values = swap(other_values, PAIR).reshape(keys // 2, feature)

    lists = jnp.pad(
        swap(after(parents, other), CORE).astype(jnp.bfloat16),
        ((0, 0), (feature + PARENT_LANE + beams, LANES - PARENT_LANE - 2 * beams)),
    )
    frame_count = jnp.broadcast_to(lengths.reshape(1, 1), (1, LANES))
    held = jnp.concatenate([own + lists, pair_rows], axis=0)

    cross_near = pl.pallas_call(
        cross_kernel,
        out_shape=jax.ShapeDtypeStruct((rows, feature), jnp.bfloat16),
        grid=(1,),
        in_specs=[whole((1, LANES)), whole((rows, feature)), whole((frames, 2 * feature))],
        out_specs=whole((rows, feature)),
        compiler_params=params,
    )(frame_count, after(cross_queries, held), enc_kv.reshape(frames, 2 * feature))
    far = swap(after(near, other), CORE)
    blocks = {0: held}
    for bits in hops:
        for mask, block in list(blocks.items()):
            blocks[mask ^ bits] = swap(after(block, cross_near) if mask else block, bits)
    masks, gathered = list(blocks), list(blocks.values())

    cross_far = swap(after(cross_near, gathered[2]), CORE)

    pair_far_keys = swap(after(pair_keys, *gathered[:-1], cross_far), CORE)
    pair_far_values = swap(after(pair_values, gathered[-1], cross_near), CORE)

    all_rows = rows * len(masks)
    weight_shape = jax.ShapeDtypeStruct((heads, all_rows, 2 * keys), jnp.bfloat16)
    share_shape = jax.ShapeDtypeStruct((all_rows, LANES), jnp.bfloat16)
    part = jax.ShapeDtypeStruct((rows, width), jnp.bfloat16)
    near_shape = near.shape[:3] + (feature,)
    in_keys = pl.BlockSpec(near_shape, lambda i: (0, 0, 0, 0))
    in_values = pl.BlockSpec(near_shape, lambda i: (0, 0, 0, 1))
    pair_spec = whole(pair_keys.shape)
    weights, shares = pl.pallas_call(
        functools.partial(self_weights_kernel, tuple(masks), len(gathered)),
        out_shape=(weight_shape, share_shape),
        grid=(1,),
        in_specs=[whole(block.shape) for block in gathered]
        + [in_keys, in_keys, pair_spec, pair_spec],
        out_specs=(whole(weight_shape.shape), whole(share_shape.shape)),
        scratch_shapes=[pltpu.VMEM((heads * all_rows, LANES), jnp.bfloat16)],
        compiler_params=params,
    )(*gathered, near, far, pair_keys, pair_far_keys)
    parts = pl.pallas_call(
        functools.partial(self_values_kernel, tuple(masks)),
        out_shape=(part,) * len(masks),
        grid=(1,),
        in_specs=[whole(weights.shape), whole(shares.shape)]
        + [in_values, in_values, pair_spec, pair_spec]
        + [whole((rows, feature))] * 2,
        out_specs=(whole(part.shape),) * len(masks),
        compiler_params=params,
    )(weights, shares, near, far, pair_values, pair_far_values, cross_near, cross_far)

    parts = dict(zip(sorted(masks), parts))
    for bits in hops[::-1]:
        for mask in sorted(parts, reverse=True):
            if mask ^ bits in parts and mask ^ bits < mask:
                parts[mask ^ bits] = parts[mask ^ bits] + swap(parts.pop(mask), bits)
    (mixed,) = parts.values()
    keep = mixed[: rows // 2]
    came = swap(mixed[rows // 2 :], PAIR)

    return pl.pallas_call(
        functools.partial(finish_kernel, history),
        out_shape=jax.ShapeDtypeStruct((rows, feature), jnp.bfloat16),
        grid=(1,),
        in_specs=[
            whole(half_rows.shape),
            whole(half_rows.shape),
            pl.BlockSpec((rows, feature), lambda i: (0, 2)),
        ],
        out_specs=whole((rows, feature)),
        compiler_params=params,
    )(keep, came, new_rows)


def solution(mesh):
    placed = (
        P(("groups", "utt"), None, None),
        P(("groups", "utt"), None),
        P(("groups", "utt"), None),
        P(("groups", "utt"), None, None),
        P(("groups", "utt")),
        P(("groups", "utt"), None),
    )
    devices = mesh.shape["utt"]

    def body(cache_kv, new_rows, cross_queries, enc_kv, lengths, parents):
        beams = parents.shape[1]
        heads = cross_queries.shape[1] // HD
        history = cache_kv.shape[1]
        fits = (
            parents.shape[0] == 1
            and devices == beams
            and devices >= 8
            and devices & (devices - 1) == 0
            and beams % 16 == 0
            and history & (history - 1) == 0
            and heads * history <= LANES
            and beams * history == LANES
            and 3 * heads <= PARENT_LANE
            and PARENT_LANE + 2 * beams <= LANES
        )
        plan = functools.partial(body_by_parent, devices) if fits else body_by_utterance
        return plan(cache_kv, new_rows, cross_queries, enc_kv, lengths, parents)

    return jax.shard_map(
        body, mesh=mesh, in_specs=placed, out_specs=P(("groups", "utt"), None), check_vma=False
    )
```

```python
import functools

import jax
import jax.numpy as jnp
from jax import lax
from jax.experimental import pallas as pl
from jax.experimental.pallas import tpu as pltpu
from jax.sharding import PartitionSpec as P

HD = 128
LANES = 128
PARENT_LANE = 64
MASKED = -1e30


def reorder(cache_rows, parents):
    utterances, beam_width = parents.shape
    grouped = cache_rows.reshape(utterances, beam_width, cache_rows.shape[1], cache_rows.shape[2])
    picked = jax.vmap(lambda block, picks: block[picks])(grouped, parents)
    return picked.reshape(cache_rows.shape)


def attend_self(query, old_keys, old_values, new_key, new_value):
    row_count = query.shape[0]
    history = old_keys.shape[1]
    head_count = query.shape[1] // HD
    scale = HD ** (-0.5)
    query_heads = query.reshape(row_count, head_count, HD)
    key_heads = old_keys.reshape(row_count, history, head_count, HD)
    value_heads = old_values.reshape(row_count, history, head_count, HD)
    old_scores = (
        jnp.einsum("rhd,rthd->rht", query_heads, key_heads, preferred_element_type=jnp.float32)
        * scale
    )
    own_score = (
        jnp.einsum(
            "rhd,rhd->rh",
            query_heads,
            new_key.reshape(row_count, head_count, HD),
            preferred_element_type=jnp.float32,
        )
        * scale
    )
    peak = jnp.maximum(jnp.max(old_scores, axis=2), own_score)
    old_exp = jnp.exp(old_scores - peak[:, :, None])
    own_exp = jnp.exp(own_score - peak)
    total = jnp.sum(old_exp, axis=2) + own_exp
    old_weight = (old_exp / total[:, :, None]).astype(jnp.bfloat16)
    own_weight = (own_exp / total).astype(jnp.bfloat16)
    context = jnp.einsum(
        "rht,rthd->rhd", old_weight, value_heads, preferred_element_type=jnp.float32
    )
    context = context + own_weight.astype(jnp.float32)[:, :, None] * new_value.reshape(
        row_count, head_count, HD
    ).astype(jnp.float32)
    return context.reshape(row_count, head_count * HD).astype(jnp.bfloat16)


def attend_frames(queries, frames_kv, frame_counts):
    utterances = frame_counts.shape[0]
    beam_width = queries.shape[0] // utterances
    feature = queries.shape[1]
    head_count = feature // HD
    frame_total = frames_kv.shape[1]
    scale = HD ** (-0.5)
    query_heads = queries.reshape(utterances, beam_width, head_count, HD)
    key_heads = frames_kv[:, :, :feature].reshape(utterances, frame_total, head_count, HD)
    value_heads = frames_kv[:, :, feature:].reshape(utterances, frame_total, head_count, HD)
    scores = (
        jnp.einsum("ubhd,ufhd->uhbf", query_heads, key_heads, preferred_element_type=jnp.float32)
        * scale
    )
    live = (
        lax.broadcasted_iota(jnp.int32, (utterances, 1, 1, frame_total), 3)
        < frame_counts[:, None, None, None]
    )
    scores = jnp.where(live, scores, -1e30)
    peak = jnp.max(scores, axis=3, keepdims=True)
    raised = jnp.where(live, jnp.exp(scores - peak), 0.0)
    weights = (raised / jnp.sum(raised, axis=3, keepdims=True)).astype(jnp.bfloat16)
    context = jnp.einsum(
        "uhbf,ufhd->ubhd", weights, value_heads, preferred_element_type=jnp.float32
    )
    return context.reshape(utterances * beam_width, feature)


def body_by_utterance(cache_kv, new_rows, cross_queries, enc_kv, lengths, parents):
    feature = cross_queries.shape[1]
    cross_context = attend_frames(cross_queries, enc_kv, lengths)
    arrived, new_here = (
        lax.all_to_all(cache_kv, "utt", split_axis=0, concat_axis=0, tiled=True),
        lax.all_to_all(new_rows, "utt", split_axis=0, concat_axis=0, tiled=True),
    )
    reordered = reorder(arrived, parents)
    self_context = attend_self(
        new_here[:, :feature],
        reordered[:, :, :feature],
        reordered[:, :, feature:],
        new_here[:, feature : 2 * feature],
        new_here[:, 2 * feature :],
    )
    mixed_here = (self_context.astype(jnp.float32) + cross_context).astype(jnp.bfloat16)
    mixed = lax.all_to_all(mixed_here, "utt", split_axis=0, concat_axis=0, tiled=True)
    return mixed


CORE = 1
CLASS = 2
PAIR = CLASS | CORE
OVER_LAST = (((1,), (1,)), ((), ()))


def class_of(index):
    return (index // CLASS) % 2


def rank_in_class(utt):
    return utt // (2 * CLASS) * CLASS + utt % CLASS


def utt_of_rank(rank, device):
    return rank // CLASS * (2 * CLASS) + class_of(device) * CLASS + rank % CLASS


def rank_of_row(row, half):
    return half - 1 - row % half


def class_order(beams, device):
    row = lax.broadcasted_iota(jnp.int32, (beams, beams), 0)
    col = lax.broadcasted_iota(jnp.int32, (beams, beams), 1)
    half = beams // 2
    place = rank_of_row(rank_in_class(col), half)
    place = place + jnp.where(class_of(col) == class_of(device), 0, half)
    return (row == place).astype(jnp.bfloat16)


def pack_kernel(
    new_ref,
    parents_hbm_ref,
    cache_ref,
    keep_ref,
    send_ref,
    keys_ref,
    values_ref,
    query_ref,
    key_ref,
    parents_ref,
    sems,
):
    rows, feature = query_ref.shape
    other = 1 - class_of(lax.axis_index("utt").astype(jnp.int32))
    slicing = [
        pltpu.make_async_copy(cache_ref.at[:, other, :, :feature], keys_ref, sems.at[3]),
        pltpu.make_async_copy(cache_ref.at[:, other, :, feature:], values_ref, sems.at[4]),
    ]
    copies = [
        pltpu.make_async_copy(new_ref.at[:, :feature], query_ref, sems.at[0]),
        pltpu.make_async_copy(new_ref.at[:, feature : 2 * feature], key_ref, sems.at[1]),
        pltpu.make_async_copy(parents_hbm_ref, parents_ref, sems.at[2]),
    ]
    for copy in copies + slicing:
        copy.start()
    half = rows // 2
    beams = parents_ref.shape[1]
    order = class_order(rows, lax.axis_index("utt"))
    for copy in copies:
        copy.wait()
    query = query_ref[...]
    product = query.astype(jnp.float32) * key_ref[...].astype(jnp.float32)
    lane = lax.broadcasted_iota(jnp.int32, (rows, LANES), 1)
    heads = feature // HD
    at_parent_lane = lax.broadcasted_iota(jnp.int32, (beams, LANES), 0) + PARENT_LANE
    at_parent_lane = at_parent_lane == lax.broadcasted_iota(jnp.int32, (beams, LANES), 1)
    extra = jnp.dot(
        jnp.broadcast_to(parents_ref[...], (rows, beams)).astype(jnp.bfloat16),
        at_parent_lane.astype(jnp.bfloat16),
        preferred_element_type=jnp.float32,
    )
    for head in range(heads):
        own = jnp.sum(product[:, head * HD : (head + 1) * HD], axis=1, keepdims=True) * HD ** (-0.5)
        for part in range(3):
            term = own.astype(jnp.bfloat16).astype(jnp.float32)
            extra = jnp.where(lane == part * heads + head, term, extra)
            own = own - term
    extra = extra.astype(jnp.bfloat16)
    for at in range(0, feature + LANES, LANES):
        tile = query[:, at : at + LANES] if at < feature else extra
        tile = jnp.dot(order, tile, preferred_element_type=jnp.float32)
        keep_ref[:, at : at + LANES] = tile[:half].astype(jnp.bfloat16)
        send_ref[:, at : at + LANES] = tile[half:].astype(jnp.bfloat16)
    for copy in slicing:
        copy.wait()


def cross_kernel(lengths_ref, query_ref, frames_ref, out_ref):
    rows, feature = query_ref.shape
    frames = frames_ref.shape[0]
    heads = feature // HD
    live = lax.broadcasted_iota(jnp.int32, (rows, frames), 1) < lengths_ref[:, :1]
    scores = []
    for head in range(heads):
        at = slice(head * HD, (head + 1) * HD)
        scores.append(
            lax.dot_general(
                query_ref[:, at], frames_ref[:, at], OVER_LAST, preferred_element_type=jnp.float32
            )
        )
    weights = []
    for head in range(heads):
        masked = jnp.where(live, scores[head] * HD ** (-0.5), MASKED)
        raised = jnp.where(live, jnp.exp(masked - jnp.max(masked, axis=1, keepdims=True)), 0.0)
        weights.append((raised / jnp.sum(raised, axis=1, keepdims=True)).astype(jnp.bfloat16))
    for head in range(heads):
        at = slice(head * HD, (head + 1) * HD)
        value_at = slice(feature + head * HD, feature + (head + 1) * HD)
        out_ref[:, at] = jnp.dot(
            weights[head], frames_ref[:, value_at], preferred_element_type=jnp.float32
        ).astype(jnp.bfloat16)


def cached(near_ref, far_ref, pair_near_ref, pair_far_ref, mine, at):
    pieces = [ref[part, mine, :, at] for ref in (near_ref, far_ref) for part in range(near_ref.shape[0])]
    return jnp.concatenate(pieces + [pair_near_ref[:, at], pair_far_ref[:, at]], axis=0)


def rows_of(masks, beams):
    return [mask ^ pair for mask in masks for pair in (0, PAIR)]


def self_weights_kernel(masks, counts, *refs):
    query_refs, refs = refs[:counts], refs[counts:]
    *cache_refs, weight_ref, share_ref, spread_ref = refs
    me = lax.axis_index("utt").astype(jnp.int32)
    mine = class_of(me)
    pair_keys, feature = cache_refs[-1].shape
    heads, rows, keys = weight_ref.shape
    beams = query_refs[0].shape[0]
    half_beams = beams // 2
    history = pair_keys // half_beams
    queries = jnp.concatenate([ref[...] for ref in query_refs], axis=0)
    extra = queries[:, feature:].astype(jnp.float32)

    utt = lax.broadcasted_iota(jnp.int32, (half_beams, LANES), 0)
    utt = utt_of_rank(rank_of_row(utt, half_beams), me)
    lane = lax.broadcasted_iota(jnp.int32, (half_beams, LANES), 1)
    table = jnp.zeros((half_beams, LANES), jnp.float32)
    for at, mask in enumerate(masks):
        lists = extra[at * beams : at * beams + half_beams]
        owner = me ^ mask
        table = jnp.where(utt == owner, lists, table)
        table = jnp.where(utt == (owner ^ CORE), pltpu.roll(lists, LANES - beams, 1), table)
    chosen = jnp.concatenate(
        [
            jnp.sum(
                jnp.where(lane == PARENT_LANE + (me ^ mask), table, 0.0), axis=1, keepdims=True
            )
            for mask in rows_of(masks, beams)
        ],
        axis=0,
    ).astype(jnp.int32)

    row_rank = rank_of_row(lax.broadcasted_iota(jnp.int32, (rows, keys), 0), half_beams)
    key = lax.broadcasted_iota(jnp.int32, (rows, keys), 1)
    key_rank = key % pair_keys // history
    run = key // pair_keys
    owner = me ^ jnp.where(
        run == 0, 0, jnp.where(run == 1, CORE, jnp.where(run == 2, PAIR, PAIR ^ CORE))
    )
    live = (key_rank == row_rank) & (chosen == owner)
    group = CORE | PAIR
    row_live = (chosen // (group + 1)) == (me // (group + 1))

    tiles = [slice(at, at + LANES) for at in range(0, keys, LANES)]
    row_lane = lax.broadcasted_iota(jnp.int32, (rows, LANES), 1)
    packed = jnp.zeros((rows, LANES), jnp.float32)
    for head in range(heads):
        at = slice(head * HD, (head + 1) * HD)
        scores = lax.dot_general(
            queries[:, at], cached(*cache_refs, mine, at), OVER_LAST, preferred_element_type=jnp.float32
        )
        scores = jnp.where(live, scores, 0.0)
        scores = sum(scores[:, tile] for tile in tiles)
        scores = scores + pltpu.roll(scores, pair_keys, 1)
        shift = (head + 1) * history % pair_keys
        scores = jnp.concatenate(
            [
                pltpu.roll(scores[row : row + half_beams], shift, 1, stride=history, stride_axis=0)
                for row in range(0, rows, half_beams)
            ],
            axis=0,
        )
        packed = jnp.where(row_lane // history == head, scores, packed)
    fold = lax.broadcasted_iota(jnp.int32, (LANES, LANES), 0) % history
    fold = fold == lax.broadcasted_iota(jnp.int32, (LANES, LANES), 1) % history
    fold = fold.astype(jnp.bfloat16)
    packed = packed * HD ** (-0.5)
    part = lax.broadcasted_iota(jnp.int32, (LANES, LANES), 0)
    spread = lax.broadcasted_iota(jnp.int32, (LANES, LANES), 1) // history
    spread = (part < 3 * heads) & (part % heads == spread)
    own = jnp.dot(
        queries[:, feature:], spread.astype(jnp.bfloat16), preferred_element_type=jnp.float32
    )

    def over_tokens(tile, combine):
        step = 1
        while step < history:
            left = pltpu.roll(tile, step, 1)
            right = pltpu.roll(tile, LANES - step, 1)
            tile = combine(tile, jnp.where(row_lane // step % 2 == 0, right, left))
            step = 2 * step
        return tile

    peak = jnp.maximum(over_tokens(packed, jnp.maximum), own)
    raised = jnp.exp(packed - peak)
    own = jnp.exp(own - peak)
    share = 1.0 / (over_tokens(raised, jnp.add) + own)
    share_ref[...] = jnp.where(row_live, own * share, 0.0).astype(jnp.bfloat16)
    packed = (raised * share).astype(jnp.bfloat16)
    for head in range(heads):
        spread_ref[head * rows : (head + 1) * rows] = jnp.where(
            row_lane // history == head, packed, jnp.zeros_like(packed)
        )
    weights = jnp.dot(spread_ref[...], fold, preferred_element_type=jnp.float32)
    for head in range(heads):
        for tile in tiles:
            weight_ref[head, :, tile] = jnp.where(
                live[:, tile], weights[head * rows : (head + 1) * rows], 0.0
            ).astype(jnp.bfloat16)


def self_values_kernel(masks, *refs):
    out_refs = refs[-len(masks) :]
    weight_ref, share_ref, *cache_refs, cross_near_ref, cross_far_ref = refs[: -len(masks)]
    me = lax.axis_index("utt").astype(jnp.int32)
    mine = class_of(me)
    heads, rows, _ = weight_ref.shape
    feature = heads * HD
    beams = cross_near_ref.shape[0]
    blocks = [slice(at * beams, (at + 1) * beams) for at in (masks.index(m) for m in sorted(masks))]
    half_beams = beams // 2
    for out_ref, block in zip(out_refs, blocks):
        out_ref[:, feature:] = share_ref[block]

    place = lax.broadcasted_iota(jnp.int32, (rows, beams), 1)
    pick_utt = lax.broadcasted_iota(jnp.int32, (rows, beams), 0)
    pick_utt = utt_of_rank(rank_of_row(pick_utt, half_beams), me)
    row_beam = me ^ jnp.concatenate(
        [jnp.full((half_beams, beams), mask, jnp.int32) for mask in rows_of(masks, beams)], axis=0
    )
    near_pick = ((place == row_beam) & (pick_utt == me)).astype(jnp.bfloat16)
    far_pick = ((place == row_beam) & (pick_utt == (me ^ CORE))).astype(jnp.bfloat16)
    pick = jnp.concatenate([near_pick, far_pick], axis=1)
    for head in range(heads):
        at = slice(head * HD, (head + 1) * HD)
        out = jnp.dot(
            weight_ref[head], cached(*cache_refs, mine, at), preferred_element_type=jnp.float32
        )
        cross = jnp.concatenate([cross_near_ref[:, at], cross_far_ref[:, at]], axis=0)
        out = out + jnp.dot(pick, cross, preferred_element_type=jnp.float32)
        out = out.astype(jnp.bfloat16)
        for out_ref, block in zip(out_refs, blocks):
            out_ref[:, at] = out[block]


def finish_kernel(history, mine_ref, came_ref, value_ref, out_ref):
    rows, feature = out_ref.shape
    order = class_order(rows, lax.axis_index("utt"))

    def ordered(at):
        tile = jnp.concatenate(
            [mine_ref[:, at].astype(jnp.float32), came_ref[:, at].astype(jnp.float32)], axis=0
        ).astype(jnp.bfloat16)
        return lax.dot_general(
            order, tile, (((0,), (0,)), ((), ())), preferred_element_type=jnp.float32
        )

    shares = ordered(slice(feature, feature + LANES))
    for head in range(feature // HD):
        at = slice(head * HD, (head + 1) * HD)
        out = ordered(at) + shares[:, head * history : head * history + 1] * value_ref[:, at].astype(jnp.float32)
        out_ref[:, at] = out.astype(jnp.bfloat16)


def whole(shape):
    return pl.BlockSpec(shape, lambda *_: (0,) * len(shape))


def body_by_parent(devices, cache_kv, new_rows, cross_queries, enc_kv, lengths, parents):
    beams = parents.shape[1]
    rows, feature = cross_queries.shape
    frames = enc_kv.shape[1]
    history = cache_kv.shape[1]
    heads = feature // HD
    width = feature + LANES
    keys = beams * history
    me = lax.axis_index("utt").astype(jnp.int32)
    params = pltpu.CompilerParams(vmem_limit_bytes=16 * 1024 * 1024)

    def swap(array, bits):
        return lax.ppermute(array, "utt", [(i, i ^ bits) for i in range(devices)])

    def after(array, *others):
        return lax.optimization_barrier((array,) + others)[0]

    def in_hbm(array):
        return pltpu.with_memory_space_constraint(array, pltpu.HBM)

    hops = [(1 << k) | CORE for k in range(devices.bit_length() - 2, 1, -1)]

    near = cache_kv.reshape(beams // (2 * CLASS), 2, CLASS * history, 2 * feature)
    half_rows = jax.ShapeDtypeStruct((rows // 2, width), jnp.bfloat16)
    half_cache = jax.ShapeDtypeStruct(near.shape[:1] + near.shape[2:3] + (feature,), jnp.bfloat16)
    own, other, other_keys, other_values = pl.pallas_call(
        pack_kernel,
        out_shape=(half_rows, half_rows, half_cache, half_cache),
        in_specs=[pl.BlockSpec(memory_space=pltpu.HBM)] * 3,
        out_specs=(whole(half_rows.shape),) * 2 + (whole(half_cache.shape),) * 2,
        scratch_shapes=[
            pltpu.VMEM((rows, feature), jnp.bfloat16),
            pltpu.VMEM((rows, feature), jnp.bfloat16),
            pltpu.VMEM(parents.shape, jnp.int32),
            pltpu.SemaphoreType.DMA((5,)),
        ],
        compiler_params=params,
        cost_estimate=pl.CostEstimate(
            flops=1_500_000_000, bytes_accessed=4 * near.size, transcendentals=0
        ),
    )(
        in_hbm(new_rows),
        in_hbm(parents),
        in_hbm(near),
    )
    pair_rows = swap(other, PAIR)
    pair_keys = swap(other_keys, PAIR).reshape(keys // 2, feature)
    pair_values = swap(other_values, PAIR).reshape(keys // 2, feature)

    lists = jnp.pad(
        swap(after(parents, other), CORE).astype(jnp.bfloat16),
        ((0, 0), (feature + PARENT_LANE + beams, LANES - PARENT_LANE - 2 * beams)),
    )
    frame_count = jnp.broadcast_to(lengths.reshape(1, 1), (1, LANES))
    held = jnp.concatenate([own + lists, pair_rows], axis=0)

    cross_near = pl.pallas_call(
        cross_kernel,
        out_shape=jax.ShapeDtypeStruct((rows, feature), jnp.bfloat16),
        grid=(1,),
        in_specs=[whole((1, LANES)), whole((rows, feature)), whole((frames, 2 * feature))],
        out_specs=whole((rows, feature)),
        compiler_params=params,
    )(frame_count, after(cross_queries, held), enc_kv.reshape(frames, 2 * feature))
    far = swap(after(near, other), CORE)
    blocks = {0: held}
    for bits in hops:
        for mask, block in list(blocks.items()):
            blocks[mask ^ bits] = swap(after(block, cross_near) if mask else block, bits)
    masks, gathered = list(blocks), list(blocks.values())

    cross_far = swap(after(cross_near, gathered[2]), CORE)

    pair_far_keys = swap(after(pair_keys, *gathered[:-1], cross_far), CORE)
    pair_far_values = swap(after(pair_values, gathered[-1], cross_near), CORE)

    all_rows = rows * len(masks)
    weight_shape = jax.ShapeDtypeStruct((heads, all_rows, 2 * keys), jnp.bfloat16)
    share_shape = jax.ShapeDtypeStruct((all_rows, LANES), jnp.bfloat16)
    part = jax.ShapeDtypeStruct((rows, width), jnp.bfloat16)
    near_shape = near.shape[:3] + (feature,)
    in_keys = pl.BlockSpec(near_shape, lambda i: (0, 0, 0, 0))
    in_values = pl.BlockSpec(near_shape, lambda i: (0, 0, 0, 1))
    pair_spec = whole(pair_keys.shape)
    weights, shares = pl.pallas_call(
        functools.partial(self_weights_kernel, tuple(masks), len(gathered)),
        out_shape=(weight_shape, share_shape),
        grid=(1,),
        in_specs=[whole(block.shape) for block in gathered]
        + [in_keys, in_keys, pair_spec, pair_spec],
        out_specs=(whole(weight_shape.shape), whole(share_shape.shape)),
        scratch_shapes=[pltpu.VMEM((heads * all_rows, LANES), jnp.bfloat16)],
        compiler_params=params,
    )(*gathered, near, far, pair_keys, pair_far_keys)
    parts = pl.pallas_call(
        functools.partial(self_values_kernel, tuple(masks)),
        out_shape=(part,) * len(masks),
        grid=(1,),
        in_specs=[whole(weights.shape), whole(shares.shape)]
        + [in_values, in_values, pair_spec, pair_spec]
        + [whole((rows, feature))] * 2,
        out_specs=(whole(part.shape),) * len(masks),
        compiler_params=params,
    )(weights, shares, near, far, pair_values, pair_far_values, cross_near, cross_far)

    parts = dict(zip(sorted(masks), parts))
    far_hop, near_hop = hops
    half = rows // 2
    relayed = parts[far_hop] + swap(parts[far_hop ^ near_hop], near_hop)
    mixed = parts[0] + swap(parts[near_hop], near_hop)
    keep = mixed[:half] + swap(relayed[:half], far_hop)
    came = swap(mixed[half:], PAIR) + swap(relayed[half:], far_hop ^ PAIR)

    return pl.pallas_call(
        functools.partial(finish_kernel, history),
        out_shape=jax.ShapeDtypeStruct((rows, feature), jnp.bfloat16),
        grid=(1,),
        in_specs=[
            whole(half_rows.shape),
            whole(half_rows.shape),
            pl.BlockSpec((rows, feature), lambda i: (0, 2)),
        ],
        out_specs=whole((rows, feature)),
        compiler_params=params,
    )(keep, came, new_rows)


def solution(mesh):
    placed = (
        P(("groups", "utt"), None, None),
        P(("groups", "utt"), None),
        P(("groups", "utt"), None),
        P(("groups", "utt"), None, None),
        P(("groups", "utt")),
        P(("groups", "utt"), None),
    )
    devices = mesh.shape["utt"]

    def body(cache_kv, new_rows, cross_queries, enc_kv, lengths, parents):
        beams = parents.shape[1]
        heads = cross_queries.shape[1] // HD
        history = cache_kv.shape[1]
        fits = (
            parents.shape[0] == 1
            and devices == beams
            and devices >= 8
            and devices & (devices - 1) == 0
            and beams % 16 == 0
            and history & (history - 1) == 0
            and heads * history <= LANES
            and beams * history == LANES
            and 3 * heads <= PARENT_LANE
            and PARENT_LANE + 2 * beams <= LANES
        )
        plan = functools.partial(body_by_parent, devices) if fits else body_by_utterance
        return plan(cache_kv, new_rows, cross_queries, enc_kv, lengths, parents)

    return jax.shard_map(
        body, mesh=mesh, in_specs=placed, out_specs=P(("groups", "utt"), None), check_vma=False
    )
```

```python
import functools

import jax
import jax.numpy as jnp
from jax import lax
from jax.experimental import pallas as pl
from jax.experimental.pallas import tpu as pltpu
from jax.sharding import PartitionSpec as P

HD = 128
LANES = 128
PARENT_LANE = 64
MASKED = -1e30


def reorder(cache_rows, parents):
    utterances, beam_width = parents.shape
    grouped = cache_rows.reshape(utterances, beam_width, cache_rows.shape[1], cache_rows.shape[2])
    picked = jax.vmap(lambda block, picks: block[picks])(grouped, parents)
    return picked.reshape(cache_rows.shape)


def attend_self(query, old_keys, old_values, new_key, new_value):
    row_count = query.shape[0]
    history = old_keys.shape[1]
    head_count = query.shape[1] // HD
    scale = HD ** (-0.5)
    query_heads = query.reshape(row_count, head_count, HD)
    key_heads = old_keys.reshape(row_count, history, head_count, HD)
    value_heads = old_values.reshape(row_count, history, head_count, HD)
    old_scores = (
        jnp.einsum("rhd,rthd->rht", query_heads, key_heads, preferred_element_type=jnp.float32)
        * scale
    )
    own_score = (
        jnp.einsum(
            "rhd,rhd->rh",
            query_heads,
            new_key.reshape(row_count, head_count, HD),
            preferred_element_type=jnp.float32,
        )
        * scale
    )
    peak = jnp.maximum(jnp.max(old_scores, axis=2), own_score)
    old_exp = jnp.exp(old_scores - peak[:, :, None])
    own_exp = jnp.exp(own_score - peak)
    total = jnp.sum(old_exp, axis=2) + own_exp
    old_weight = (old_exp / total[:, :, None]).astype(jnp.bfloat16)
    own_weight = (own_exp / total).astype(jnp.bfloat16)
    context = jnp.einsum(
        "rht,rthd->rhd", old_weight, value_heads, preferred_element_type=jnp.float32
    )
    context = context + own_weight.astype(jnp.float32)[:, :, None] * new_value.reshape(
        row_count, head_count, HD
    ).astype(jnp.float32)
    return context.reshape(row_count, head_count * HD).astype(jnp.bfloat16)


def attend_frames(queries, frames_kv, frame_counts):
    utterances = frame_counts.shape[0]
    beam_width = queries.shape[0] // utterances
    feature = queries.shape[1]
    head_count = feature // HD
    frame_total = frames_kv.shape[1]
    scale = HD ** (-0.5)
    query_heads = queries.reshape(utterances, beam_width, head_count, HD)
    key_heads = frames_kv[:, :, :feature].reshape(utterances, frame_total, head_count, HD)
    value_heads = frames_kv[:, :, feature:].reshape(utterances, frame_total, head_count, HD)
    scores = (
        jnp.einsum("ubhd,ufhd->uhbf", query_heads, key_heads, preferred_element_type=jnp.float32)
        * scale
    )
    live = (
        lax.broadcasted_iota(jnp.int32, (utterances, 1, 1, frame_total), 3)
        < frame_counts[:, None, None, None]
    )
    scores = jnp.where(live, scores, -1e30)
    peak = jnp.max(scores, axis=3, keepdims=True)
    raised = jnp.where(live, jnp.exp(scores - peak), 0.0)
    weights = (raised / jnp.sum(raised, axis=3, keepdims=True)).astype(jnp.bfloat16)
    context = jnp.einsum(
        "uhbf,ufhd->ubhd", weights, value_heads, preferred_element_type=jnp.float32
    )
    return context.reshape(utterances * beam_width, feature)


def body_by_utterance(cache_kv, new_rows, cross_queries, enc_kv, lengths, parents):
    feature = cross_queries.shape[1]
    cross_context = attend_frames(cross_queries, enc_kv, lengths)
    arrived, new_here = (
        lax.all_to_all(cache_kv, "utt", split_axis=0, concat_axis=0, tiled=True),
        lax.all_to_all(new_rows, "utt", split_axis=0, concat_axis=0, tiled=True),
    )
    reordered = reorder(arrived, parents)
    self_context = attend_self(
        new_here[:, :feature],
        reordered[:, :, :feature],
        reordered[:, :, feature:],
        new_here[:, feature : 2 * feature],
        new_here[:, 2 * feature :],
    )
    mixed_here = (self_context.astype(jnp.float32) + cross_context).astype(jnp.bfloat16)
    mixed = lax.all_to_all(mixed_here, "utt", split_axis=0, concat_axis=0, tiled=True)
    return mixed


CORE = 1
CLASS = 2
PAIR = CLASS | CORE
OVER_LAST = (((1,), (1,)), ((), ()))


def class_of(index):
    return (index // CLASS) % 2


def rank_in_class(utt):
    return utt // (2 * CLASS) * CLASS + utt % CLASS


def utt_of_rank(rank, device):
    return rank // CLASS * (2 * CLASS) + class_of(device) * CLASS + rank % CLASS


def rank_of_row(row, half):
    return half - 1 - row % half


def class_order(beams, device):
    row = lax.broadcasted_iota(jnp.int32, (beams, beams), 0)
    col = lax.broadcasted_iota(jnp.int32, (beams, beams), 1)
    half = beams // 2
    place = rank_of_row(rank_in_class(col), half)
    place = place + jnp.where(class_of(col) == class_of(device), 0, half)
    return (row == place).astype(jnp.bfloat16)


def pack_kernel(
    new_ref,
    parents_hbm_ref,
    cache_ref,
    keep_ref,
    send_ref,
    keys_ref,
    values_ref,
    query_ref,
    key_ref,
    parents_ref,
    sems,
):
    rows, feature = query_ref.shape
    other = 1 - class_of(lax.axis_index("utt").astype(jnp.int32))
    slicing = [
        pltpu.make_async_copy(cache_ref.at[:, other, :, :feature], keys_ref, sems.at[3]),
        pltpu.make_async_copy(cache_ref.at[:, other, :, feature:], values_ref, sems.at[4]),
    ]
    copies = [
        pltpu.make_async_copy(new_ref.at[:, :feature], query_ref, sems.at[0]),
        pltpu.make_async_copy(new_ref.at[:, feature : 2 * feature], key_ref, sems.at[1]),
        pltpu.make_async_copy(parents_hbm_ref, parents_ref, sems.at[2]),
    ]
    for copy in copies + slicing:
        copy.start()
    half = rows // 2
    beams = parents_ref.shape[1]
    order = class_order(rows, lax.axis_index("utt"))
    for copy in copies:
        copy.wait()
    query = query_ref[...]
    product = query.astype(jnp.float32) * key_ref[...].astype(jnp.float32)
    lane = lax.broadcasted_iota(jnp.int32, (rows, LANES), 1)
    heads = feature // HD
    at_parent_lane = lax.broadcasted_iota(jnp.int32, (beams, LANES), 0) + PARENT_LANE
    at_parent_lane = at_parent_lane == lax.broadcasted_iota(jnp.int32, (beams, LANES), 1)
    extra = jnp.dot(
        jnp.broadcast_to(parents_ref[...], (rows, beams)).astype(jnp.bfloat16),
        at_parent_lane.astype(jnp.bfloat16),
        preferred_element_type=jnp.float32,
    )
    for head in range(heads):
        own = jnp.sum(product[:, head * HD : (head + 1) * HD], axis=1, keepdims=True) * HD ** (-0.5)
        for part in range(3):
            term = own.astype(jnp.bfloat16).astype(jnp.float32)
            extra = jnp.where(lane == part * heads + head, term, extra)
            own = own - term
    extra = extra.astype(jnp.bfloat16)
    for at in range(0, feature + LANES, LANES):
        tile = query[:, at : at + LANES] if at < feature else extra
        tile = jnp.dot(order, tile, preferred_element_type=jnp.float32)
        keep_ref[:, at : at + LANES] = tile[:half].astype(jnp.bfloat16)
        send_ref[:, at : at + LANES] = tile[half:].astype(jnp.bfloat16)
    for copy in slicing:
        copy.wait()


def cross_kernel(lengths_ref, query_ref, frames_ref, out_ref):
    rows, feature = query_ref.shape
    frames = frames_ref.shape[0]
    heads = feature // HD
    live = lax.broadcasted_iota(jnp.int32, (rows, frames), 1) < lengths_ref[:, :1]
    scores = []
    for head in range(heads):
        at = slice(head * HD, (head + 1) * HD)
        scores.append(
            lax.dot_general(
                query_ref[:, at], frames_ref[:, at], OVER_LAST, preferred_element_type=jnp.float32
            )
        )
    weights = []
    for head in range(heads):
        masked = jnp.where(live, scores[head] * HD ** (-0.5), MASKED)
        raised = jnp.where(live, jnp.exp(masked - jnp.max(masked, axis=1, keepdims=True)), 0.0)
        weights.append((raised / jnp.sum(raised, axis=1, keepdims=True)).astype(jnp.bfloat16))
    for head in range(heads):
        at = slice(head * HD, (head + 1) * HD)
        value_at = slice(feature + head * HD, feature + (head + 1) * HD)
        out_ref[:, at] = jnp.dot(
            weights[head], frames_ref[:, value_at], preferred_element_type=jnp.float32
        ).astype(jnp.bfloat16)


def cached(near_ref, far_ref, pair_near_ref, pair_far_ref, mine, at):
    pieces = [ref[part, mine, :, at] for ref in (near_ref, far_ref) for part in range(near_ref.shape[0])]
    return jnp.concatenate(pieces + [pair_near_ref[:, at], pair_far_ref[:, at]], axis=0)


def rows_of(masks, beams):
    return [mask ^ pair for mask in masks for pair in (0, PAIR)]


def self_weights_kernel(masks, counts, *refs):
    query_refs, refs = refs[:counts], refs[counts:]
    *cache_refs, weight_ref, share_ref, spread_ref = refs
    me = lax.axis_index("utt").astype(jnp.int32)
    mine = class_of(me)
    pair_keys, feature = cache_refs[-1].shape
    heads, rows, keys = weight_ref.shape
    beams = query_refs[0].shape[0]
    half_beams = beams // 2
    history = pair_keys // half_beams
    queries = jnp.concatenate([ref[...] for ref in query_refs], axis=0)
    extra = queries[:, feature:].astype(jnp.float32)

    utt = lax.broadcasted_iota(jnp.int32, (half_beams, LANES), 0)
    utt = utt_of_rank(rank_of_row(utt, half_beams), me)
    lane = lax.broadcasted_iota(jnp.int32, (half_beams, LANES), 1)
    table = jnp.zeros((half_beams, LANES), jnp.float32)
    for at, mask in enumerate(masks):
        lists = extra[at * beams : at * beams + half_beams]
        owner = me ^ mask
        table = jnp.where(utt == owner, lists, table)
        table = jnp.where(utt == (owner ^ CORE), pltpu.roll(lists, LANES - beams, 1), table)
    chosen = jnp.concatenate(
        [
            jnp.sum(
                jnp.where(lane == PARENT_LANE + (me ^ mask), table, 0.0), axis=1, keepdims=True
            )
            for mask in rows_of(masks, beams)
        ],
        axis=0,
    ).astype(jnp.int32)

    row_rank = rank_of_row(lax.broadcasted_iota(jnp.int32, (rows, keys), 0), half_beams)
    key = lax.broadcasted_iota(jnp.int32, (rows, keys), 1)
    key_rank = key % pair_keys // history
    run = key // pair_keys
    owner = me ^ jnp.where(
        run == 0, 0, jnp.where(run == 1, CORE, jnp.where(run == 2, PAIR, PAIR ^ CORE))
    )
    live = (key_rank == row_rank) & (chosen == owner)
    group = CORE | PAIR
    row_live = (chosen // (group + 1)) == (me // (group + 1))

    tiles = [slice(at, at + LANES) for at in range(0, keys, LANES)]
    row_lane = lax.broadcasted_iota(jnp.int32, (rows, LANES), 1)
    packed = jnp.zeros((rows, LANES), jnp.float32)
    for head in range(heads):
        at = slice(head * HD, (head + 1) * HD)
        scores = lax.dot_general(
            queries[:, at], cached(*cache_refs, mine, at), OVER_LAST, preferred_element_type=jnp.float32
        )
        scores = jnp.where(live, scores, 0.0)
        scores = sum(scores[:, tile] for tile in tiles)
        scores = scores + pltpu.roll(scores, pair_keys, 1)
        shift = (head + 1) * history % pair_keys
        scores = jnp.concatenate(
            [
                pltpu.roll(scores[row : row + half_beams], shift, 1, stride=history, stride_axis=0)
                for row in range(0, rows, half_beams)
            ],
            axis=0,
        )
        packed = jnp.where(row_lane // history == head, scores, packed)
    fold = lax.broadcasted_iota(jnp.int32, (LANES, LANES), 0) % history
    fold = fold == lax.broadcasted_iota(jnp.int32, (LANES, LANES), 1) % history
    fold = fold.astype(jnp.bfloat16)
    packed = packed * HD ** (-0.5)
    part = lax.broadcasted_iota(jnp.int32, (LANES, LANES), 0)
    spread = lax.broadcasted_iota(jnp.int32, (LANES, LANES), 1) // history
    spread = (part < 3 * heads) & (part % heads == spread)
    own = jnp.dot(
        queries[:, feature:], spread.astype(jnp.bfloat16), preferred_element_type=jnp.float32
    )

    def over_tokens(tile, combine):
        step = 1
        while step < history:
            left = pltpu.roll(tile, step, 1)
            right = pltpu.roll(tile, LANES - step, 1)
            tile = combine(tile, jnp.where(row_lane // step % 2 == 0, right, left))
            step = 2 * step
        return tile

    peak = jnp.maximum(over_tokens(packed, jnp.maximum), own)
    raised = jnp.exp(packed - peak)
    own = jnp.exp(own - peak)
    share = 1.0 / (over_tokens(raised, jnp.add) + own)
    share_ref[...] = jnp.where(row_live, own * share, 0.0).astype(jnp.bfloat16)
    packed = (raised * share).astype(jnp.bfloat16)
    for head in range(heads):
        spread_ref[head * rows : (head + 1) * rows] = jnp.where(
            row_lane // history == head, packed, jnp.zeros_like(packed)
        )
    weights = jnp.dot(spread_ref[...], fold, preferred_element_type=jnp.float32)
    for head in range(heads):
        for tile in tiles:
            weight_ref[head, :, tile] = jnp.where(
                live[:, tile], weights[head * rows : (head + 1) * rows], 0.0
            ).astype(jnp.bfloat16)


def self_values_kernel(masks, *refs):
    out_refs = refs[-len(masks) :]
    weight_ref, share_ref, *cache_refs, cross_near_ref, cross_far_ref = refs[: -len(masks)]
    me = lax.axis_index("utt").astype(jnp.int32)
    mine = class_of(me)
    heads, rows, _ = weight_ref.shape
    feature = heads * HD
    beams = cross_near_ref.shape[0]
    blocks = [slice(at * beams, (at + 1) * beams) for at in (masks.index(m) for m in sorted(masks))]
    half_beams = beams // 2
    for out_ref, block in zip(out_refs, blocks):
        out_ref[:, feature:] = share_ref[block]

    place = lax.broadcasted_iota(jnp.int32, (rows, beams), 1)
    pick_utt = lax.broadcasted_iota(jnp.int32, (rows, beams), 0)
    pick_utt = utt_of_rank(rank_of_row(pick_utt, half_beams), me)
    row_beam = me ^ jnp.concatenate(
        [jnp.full((half_beams, beams), mask, jnp.int32) for mask in rows_of(masks, beams)], axis=0
    )
    near_pick = ((place == row_beam) & (pick_utt == me)).astype(jnp.bfloat16)
    far_pick = ((place == row_beam) & (pick_utt == (me ^ CORE))).astype(jnp.bfloat16)
    pick = jnp.concatenate([near_pick, far_pick], axis=1)
    for head in range(heads):
        at = slice(head * HD, (head + 1) * HD)
        out = jnp.dot(
            weight_ref[head], cached(*cache_refs, mine, at), preferred_element_type=jnp.float32
        )
        cross = jnp.concatenate([cross_near_ref[:, at], cross_far_ref[:, at]], axis=0)
        out = out + jnp.dot(pick, cross, preferred_element_type=jnp.float32)
        out = out.astype(jnp.bfloat16)
        for out_ref, block in zip(out_refs, blocks):
            out_ref[:, at] = out[block]


def finish_kernel(history, mine_ref, came_ref, value_ref, out_ref):
    rows, feature = out_ref.shape
    order = class_order(rows, lax.axis_index("utt"))

    def ordered(at):
        tile = jnp.concatenate(
            [mine_ref[:, at].astype(jnp.float32), came_ref[:, at].astype(jnp.float32)], axis=0
        ).astype(jnp.bfloat16)
        return lax.dot_general(
            order, tile, (((0,), (0,)), ((), ())), preferred_element_type=jnp.float32
        )

    shares = ordered(slice(feature, feature + LANES))
    for head in range(feature // HD):
        at = slice(head * HD, (head + 1) * HD)
        out = ordered(at) + shares[:, head * history : head * history + 1] * value_ref[:, at].astype(jnp.float32)
        out_ref[:, at] = out.astype(jnp.bfloat16)


def whole(shape):
    return pl.BlockSpec(shape, lambda *_: (0,) * len(shape))


def body_by_parent(devices, cache_kv, new_rows, cross_queries, enc_kv, lengths, parents):
    beams = parents.shape[1]
    rows, feature = cross_queries.shape
    frames = enc_kv.shape[1]
    history = cache_kv.shape[1]
    heads = feature // HD
    width = feature + LANES
    keys = beams * history
    me = lax.axis_index("utt").astype(jnp.int32)
    params = pltpu.CompilerParams(vmem_limit_bytes=16 * 1024 * 1024)

    def swap(array, bits):
        return lax.ppermute(array, "utt", [(i, i ^ bits) for i in range(devices)])

    def after(array, *others):
        return lax.optimization_barrier((array,) + others)[0]

    def in_hbm(array):
        return pltpu.with_memory_space_constraint(array, pltpu.HBM)

    hops = [(1 << k) | CORE for k in range(devices.bit_length() - 2, 1, -1)]

    near = cache_kv.reshape(beams // (2 * CLASS), 2, CLASS * history, 2 * feature)
    half_rows = jax.ShapeDtypeStruct((rows // 2, width), jnp.bfloat16)
    half_cache = jax.ShapeDtypeStruct(near.shape[:1] + near.shape[2:3] + (feature,), jnp.bfloat16)
    own, other, other_keys, other_values = pl.pallas_call(
        pack_kernel,
        out_shape=(half_rows, half_rows, half_cache, half_cache),
        in_specs=[pl.BlockSpec(memory_space=pltpu.HBM)] * 3,
        out_specs=(whole(half_rows.shape),) * 2 + (whole(half_cache.shape),) * 2,
        scratch_shapes=[
            pltpu.VMEM((rows, feature), jnp.bfloat16),
            pltpu.VMEM((rows, feature), jnp.bfloat16),
            pltpu.VMEM(parents.shape, jnp.int32),
            pltpu.SemaphoreType.DMA((5,)),
        ],
        compiler_params=params,
        cost_estimate=pl.CostEstimate(
            flops=1_500_000_000, bytes_accessed=4 * near.size, transcendentals=0
        ),
    )(
        in_hbm(new_rows),
        in_hbm(parents),
        in_hbm(near),
    )
    pair_rows = swap(other, PAIR)
    pair_keys = swap(other_keys, PAIR).reshape(keys // 2, feature)
    pair_values = swap(other_values, PAIR).reshape(keys // 2, feature)

    lists = jnp.pad(
        swap(after(parents, other), CORE).astype(jnp.bfloat16),
        ((0, 0), (feature + PARENT_LANE + beams, LANES - PARENT_LANE - 2 * beams)),
    )
    frame_count = jnp.broadcast_to(lengths.reshape(1, 1), (1, LANES))
    held = jnp.concatenate([own + lists, pair_rows], axis=0)

    cross_near = pl.pallas_call(
        cross_kernel,
        out_shape=jax.ShapeDtypeStruct((rows, feature), jnp.bfloat16),
        grid=(1,),
        in_specs=[whole((1, LANES)), whole((rows, feature)), whole((frames, 2 * feature))],
        out_specs=whole((rows, feature)),
        compiler_params=params,
    )(frame_count, after(cross_queries, held), enc_kv.reshape(frames, 2 * feature))
    far = swap(after(near, other), CORE)
    blocks = {0: held}
    for bits in hops:
        for mask, block in list(blocks.items()):
            blocks[mask ^ bits] = swap(after(block, cross_near) if mask else block, bits)
    masks, gathered = list(blocks), list(blocks.values())

    cross_far = swap(after(cross_near, gathered[2]), CORE)

    pair_far_keys = swap(after(pair_keys, *gathered[:-1], cross_far), CORE)
    pair_far_values = swap(after(pair_values, gathered[-1], cross_near), CORE)

    all_rows = rows * len(masks)
    weight_shape = jax.ShapeDtypeStruct((heads, all_rows, 2 * keys), jnp.bfloat16)
    share_shape = jax.ShapeDtypeStruct((all_rows, LANES), jnp.bfloat16)
    part = jax.ShapeDtypeStruct((rows, width), jnp.bfloat16)
    near_shape = near.shape[:3] + (feature,)
    in_keys = pl.BlockSpec(near_shape, lambda i: (0, 0, 0, 0))
    in_values = pl.BlockSpec(near_shape, lambda i: (0, 0, 0, 1))
    pair_spec = whole(pair_keys.shape)
    weights, shares = pl.pallas_call(
        functools.partial(self_weights_kernel, tuple(masks), len(gathered)),
        out_shape=(weight_shape, share_shape),
        grid=(1,),
        in_specs=[whole(block.shape) for block in gathered]
        + [in_keys, in_keys, pair_spec, pair_spec],
        out_specs=(whole(weight_shape.shape), whole(share_shape.shape)),
        scratch_shapes=[pltpu.VMEM((heads * all_rows, LANES), jnp.bfloat16)],
        compiler_params=params,
    )(*gathered, near, far, pair_keys, pair_far_keys)
    parts = pl.pallas_call(
        functools.partial(self_values_kernel, tuple(masks)),
        out_shape=(part,) * len(masks),
        grid=(1,),
        in_specs=[whole(weights.shape), whole(shares.shape)]
        + [in_values, in_values, pair_spec, pair_spec]
        + [whole((rows, feature))] * 2,
        out_specs=(whole(part.shape),) * len(masks),
        compiler_params=params,
    )(weights, shares, near, far, pair_values, pair_far_values, cross_near, cross_far)

    parts = dict(zip(sorted(masks), parts))
    far_hop, near_hop = hops
    half = rows // 2
    relayed = parts[far_hop] + swap(parts[far_hop ^ near_hop], near_hop)
    near_rows = swap(parts[near_hop][:half], near_hop)
    came = swap(parts[0][half:], PAIR)
    relayed = after(relayed, came, near_rows)
    keep = parts[0][:half] + near_rows
    came = came + swap(parts[near_hop][half:], near_hop ^ PAIR)
    keep = keep + swap(relayed[:half], far_hop)
    came = came + swap(relayed[half:], far_hop ^ PAIR)

    return pl.pallas_call(
        functools.partial(finish_kernel, history),
        out_shape=jax.ShapeDtypeStruct((rows, feature), jnp.bfloat16),
        grid=(1,),
        in_specs=[
            whole(half_rows.shape),
            whole(half_rows.shape),
            pl.BlockSpec((rows, feature), lambda i: (0, 2)),
        ],
        out_specs=whole((rows, feature)),
        compiler_params=params,
    )(keep, came, new_rows)


def solution(mesh):
    placed = (
        P(("groups", "utt"), None, None),
        P(("groups", "utt"), None),
        P(("groups", "utt"), None),
        P(("groups", "utt"), None, None),
        P(("groups", "utt")),
        P(("groups", "utt"), None),
    )
    devices = mesh.shape["utt"]

    def body(cache_kv, new_rows, cross_queries, enc_kv, lengths, parents):
        beams = parents.shape[1]
        heads = cross_queries.shape[1] // HD
        history = cache_kv.shape[1]
        fits = (
            parents.shape[0] == 1
            and devices == beams
            and devices >= 8
            and devices & (devices - 1) == 0
            and beams % 16 == 0
            and history & (history - 1) == 0
            and heads * history <= LANES
            and beams * history == LANES
            and 3 * heads <= PARENT_LANE
            and PARENT_LANE + 2 * beams <= LANES
        )
        plan = functools.partial(body_by_parent, devices) if fits else body_by_utterance
        return plan(cache_kv, new_rows, cross_queries, enc_kv, lengths, parents)

    return jax.shard_map(
        body, mesh=mesh, in_specs=placed, out_specs=P(("groups", "utt"), None), check_vma=False
    )
```
